32 devices in a mesh: grp: 8 (over z, y), row: 4 (over x, core).
Axes of the slice: x: 2, y: 2, z: 4, core: 2. Of those that a mesh axis runs over, the one named last changes fastest.
Arguments:
- hidden_in: bfloat16 [16384, 768], P(('grp', 'row')), may hold values from -6 to 6
- cotangent: bfloat16 [16384, 768], P(('grp', 'row')), may hold values from -6 to 6
- w_qkv: bfloat16 [768, 2304], P('row', 'grp'), may hold values from -0.21875 to 0.21875
- w_out: bfloat16 [768, 768], P('row', 'grp'), may hold values from -0.625 to 0.625
- w_fc: bfloat16 [768, 3072], P('row', 'grp'), may hold values from -0.21875 to 0.21875
- w_proj: bfloat16 [3072, 768], P('row', 'grp'), may hold values from -0.15625 to 0.15625
- vectors: bfloat16 [8, 768], P('row', 'grp')
- fc_bias: bfloat16 [3072], P(('grp', 'row')), may hold values from -1.5 to 1.5
- first_qkv: float32 [768, 2304], P('row', 'grp'), may hold values from -0.18 to 0.18
- first_out: float32 [768, 768], P('row', 'grp'), may hold values from -0.18 to 0.18
- first_fc: float32 [768, 3072], P('row', 'grp'), may hold values from -0.18 to 0.18
- first_proj: float32 [3072, 768], P('row', 'grp'), may hold values from -0.18 to 0.18
- first_vectors: float32 [8, 768], P('row', 'grp'), may hold values from -0.18 to 0.18
- first_fc_bias: float32 [3072], P(('grp', 'row')), may hold values from -0.18 to 0.18
- second_qkv: float32 [768, 2304], P('row', 'grp'), may hold values from 1e-05 to 0.001
- second_out: float32 [768, 768], P('row', 'grp'), may hold values from 1e-05 to 0.001
- second_fc: float32 [768, 3072], P('row', 'grp'), may hold values from 1e-05 to 0.001
- second_proj: float32 [3072, 768], P('row', 'grp'), may hold values from 1e-05 to 0.001
- second_vectors: float32 [8, 768], P('row', 'grp'), may hold values from 1e-05 to 0.001
- second_fc_bias: float32 [3072], P(('grp', 'row')), may hold values from 1e-05 to 0.001
- seg_ends: int32 [32, 8], P(('grp', 'row')), may hold values from 1 to 512, as said below
- pass_counts: int32 [8], P('grp'), may hold values from 1 to 2, as said below
- reset_flag: int32 [768], replicated, may hold values 0 or 1
Outputs:
- hidden: bfloat16 [16384, 768], P(('grp', 'row'))
- input_grad: float32 [16384, 768], P(('grp', 'row'))
- grad_qkv: float32 [768, 2304], P('row', 'grp')
- grad_out: float32 [768, 768], P('row', 'grp')
- grad_fc: float32 [768, 3072], P('row', 'grp')
- grad_proj: float32 [3072, 768], P('row', 'grp')
- grad_vectors: float32 [8, 768], P('row', 'grp')
- grad_fc_bias: float32 [3072], P(('grp', 'row'))
- new_qkv: bfloat16 [768, 2304], P('row', 'grp')
- new_out: bfloat16 [768, 768], P('row', 'grp')
- new_fc: bfloat16 [768, 3072], P('row', 'grp')
- new_proj: bfloat16 [3072, 768], P('row', 'grp')
- new_vectors: bfloat16 [8, 768], P('row', 'grp')
- new_fc_bias: bfloat16 [3072], P(('grp', 'row'))
- new_first_qkv: float32 [768, 2304], P('row', 'grp')
- new_first_out: float32 [768, 768], P('row', 'grp')
- new_first_fc: float32 [768, 3072], P('row', 'grp')
- new_first_proj: float32 [3072, 768], P('row', 'grp')
- new_first_vectors: float32 [8, 768], P('row', 'grp')
- new_first_fc_bias: float32 [3072], P(('grp', 'row'))
- new_second_qkv: float32 [768, 2304], P('row', 'grp')
- new_second_out: float32 [768, 768], P('row', 'grp')
- new_second_fc: float32 [768, 3072], P('row', 'grp')
- new_second_proj: float32 [3072, 768], P('row', 'grp')
- new_second_vectors: float32 [8, 768], P('row', 'grp')
- new_second_fc_bias: float32 [3072], P(('grp', 'row'))
The draws below stay inside these ranges and needn't reach their ends.
Inputs may be any that keep to these rules, and one draw needn't show every extreme that they name: `seg_ends`: each row's ends never fall; tokens at or after a row's last end are padding, and some row has no padding. `pass_counts`: some group runs 2 passes and some group runs one.
All inputs are finite; a program needn't handle non-finite values.
Results may differ from the reference program's by a relative error of at most 0.02.
Values may be sent and summed in bfloat16 or wider, within the bound.
No kernel may reach another device: no remote copies, remote signals or barrier semaphores. Data moves between devices by JAX's collectives and lax.ppermute only.
A program may use at most 320 MiB of HBM per device.

```python
import math
import jax
import jax.numpy as jnp
from jax import lax

D = 768
HEADS = 12
HEAD = 64
FF = 3072
ROW_LEN = 512
SEGS = 8
PASSES = 2
STEP = 10
GROUPS = 8
ROWS = 32
TOKENS = 16384
N_ROW = 4


def draw_vectors(key, part):
    keys = jax.random.split(key, 2)
    noise = jnp.clip(jax.random.normal(keys[0], (8, D), jnp.float32), -4.0, 4.0)
    spread = jax.random.uniform(keys[1], (8, D), jnp.float32, -1.0, 1.0)
    is_gain = (jnp.arange(8) % 5 == 0)[:, None]
    return jnp.where(is_gain, 1.0 + 0.25 * spread, 0.3 * noise).astype(jnp.bfloat16)


def draw_seg_ends(key, part):
    row_ids = jnp.arange(ROWS, dtype=jnp.int32)
    valid_len = ROW_LEN // 4 + 3 * ROW_LEN // 4 * row_ids // max(ROWS - 1, 1)
    cuts = jax.random.randint(key, (ROWS, SEGS - 1), 1, valid_len[:, None])
    cuts = jnp.sort(cuts, axis=1)
    return jnp.concatenate([cuts, valid_len[:, None]], 1).astype(jnp.int32)


def draw_pass_counts(key, part):
    keys = jax.random.split(key, 2)
    counts = jax.random.randint(keys[0], (GROUPS,), 1, PASSES + 1)
    order = jax.random.permutation(keys[1], GROUPS)
    counts = counts.at[order[0]].set(PASSES)
    return counts.at[order[1]].set(1).astype(jnp.int32)


def set_ends(entries, own_key, low, high):
    longest = entries.shape.index(max(entries.shape))
    spots = []
    for shift in (0, 1):
        where = [jax.random.randint(jax.random.fold_in(own_key, axis), (), 0, length) for axis, length in enumerate(entries.shape)]
        where[longest] = (where[longest] + shift) % entries.shape[longest]
        spots.append(tuple(where))
    return entries.at[spots[0]].set(low).at[spots[1]].set(high)


def level_of(rng, extent, cuts, least, high):
    level, own = 1.0, jax.random.fold_in(rng, 6)
    for dim, blocks in cuts:
        steps = jnp.exp(jax.random.uniform(jax.random.fold_in(own, dim), (blocks,), jnp.float32, least / len(cuts), high / len(cuts)))
        level = level * jnp.repeat(steps, extent[dim] // blocks).reshape([-1 if axis == dim else 1 for axis in range(len(extent))])
    return level


def bell_draw(stream_key, extent, scale, most, shards=(), kind=jnp.bfloat16):
    level = level_of(stream_key, extent, shards, -0.22, 0.18) if shards else 1.0
    array = jax.random.normal(stream_key, extent, jnp.float32) * scale * level
    return jnp.minimum(jnp.maximum(array, -most), most).astype(kind)


def setup_inputs(seed: int = 0) -> dict:
    key_of = jax.random.split(jax.random.key(seed), 24)
    hidden_in = bell_draw(key_of[0], (TOKENS, D), 1.0, 6.0, ((0, 32),))
    cotangent = bell_draw(key_of[1], (TOKENS, D), 1.0, 6.0, ((0, 32),))
    w_qkv = bell_draw(key_of[2], (D, 3 * D), D ** -0.5, 0.21875, ((0, 4), (1, 8)))
    w_out = bell_draw(key_of[3], (D, D), (D // 8) ** -0.5, 0.625, ((0, 4), (1, 8)))
    w_fc = bell_draw(key_of[4], (D, FF), D ** -0.5, 0.21875, ((0, 4), (1, 8)))
    w_proj = bell_draw(key_of[5], (FF, D), (FF // 2) ** -0.5, 0.15625, ((0, 4), (1, 8)))
    vectors = draw_vectors(jax.random.fold_in(key_of[23], 71), 0)
    fc_bias = bell_draw(key_of[7], (FF,), 0.3, 1.5, ((0, 32),))
    first_qkv = bell_draw(key_of[8], (D, 3 * D), 0.03, 0.18, ((0, 4), (1, 8)), jnp.float32)
    first_out = bell_draw(key_of[9], (D, D), 0.03, 0.18, ((0, 4), (1, 8)), jnp.float32)
    first_fc = bell_draw(key_of[10], (D, FF), 0.03, 0.18, ((0, 4), (1, 8)), jnp.float32)
    first_proj = bell_draw(key_of[11], (FF, D), 0.03, 0.18, ((0, 4), (1, 8)), jnp.float32)
    first_vectors = bell_draw(key_of[12], (8, D), 0.03, 0.18, ((0, 4), (1, 8)), jnp.float32)
    first_fc_bias = bell_draw(key_of[13], (FF,), 0.03, 0.18, ((0, 32),), jnp.float32)
    second_qkv = jnp.clip(jnp.exp(math.log(0.001) - 4.6051703 * jax.random.uniform(key_of[14], (D, 3 * D), jnp.float32) ** level_of(key_of[14], (D, 3 * D), ((0, 4), (1, 8)), -0.2, 0.2)), 9.999999747378752e-06, 0.001)
    second_out = jnp.clip(jnp.exp(math.log(0.001) - 4.6051703 * jax.random.uniform(key_of[15], (D, D), jnp.float32) ** level_of(key_of[15], (D, D), ((0, 4), (1, 8)), -0.2, 0.2)), 9.999999747378752e-06, 0.001)
    second_fc = jnp.clip(jnp.exp(math.log(0.001) - 4.6051703 * jax.random.uniform(key_of[16], (D, FF), jnp.float32) ** level_of(key_of[16], (D, FF), ((0, 4), (1, 8)), -0.2, 0.2)), 9.999999747378752e-06, 0.001)
    second_proj = jnp.clip(jnp.exp(math.log(0.001) - 4.6051703 * jax.random.uniform(key_of[17], (FF, D), jnp.float32) ** level_of(key_of[17], (FF, D), ((0, 4), (1, 8)), -0.2, 0.2)), 9.999999747378752e-06, 0.001)
    second_vectors = jnp.clip(jnp.exp(math.log(0.001) - 4.6051703 * jax.random.uniform(key_of[18], (8, D), jnp.float32) ** level_of(key_of[18], (8, D), ((0, 4), (1, 8)), -0.2, 0.2)), 9.999999747378752e-06, 0.001)
    second_fc_bias = jnp.clip(jnp.exp(math.log(0.001) - 4.6051703 * jax.random.uniform(key_of[19], (FF,), jnp.float32) ** level_of(key_of[19], (FF,), ((0, 32),), -0.2, 0.2)), 9.999999747378752e-06, 0.001)
    seg_ends = draw_seg_ends(jax.random.fold_in(key_of[23], 71), 0)
    pass_counts = draw_pass_counts(jax.random.fold_in(key_of[23], 71), 0)
    reset_flag = set_ends((jax.random.randint(key_of[22], (D,), 0, 4) < 1).astype(jnp.int32), jax.random.fold_in(key_of[22], 1), 0, 1)
    return dict(hidden_in=hidden_in, cotangent=cotangent, w_qkv=w_qkv, w_out=w_out, w_fc=w_fc, w_proj=w_proj, vectors=vectors, fc_bias=fc_bias, first_qkv=first_qkv, first_out=first_out, first_fc=first_fc, first_proj=first_proj, first_vectors=first_vectors, first_fc_bias=first_fc_bias, second_qkv=second_qkv, second_out=second_out, second_fc=second_fc, second_proj=second_proj, second_vectors=second_vectors, second_fc_bias=second_fc_bias, seg_ends=seg_ends, pass_counts=pass_counts, reset_flag=reset_flag)


HIGH = lax.Precision.HIGHEST
LEARN_RATE = 0.03
WEIGHT_DECAY = 0.1

@jax.custom_vjp
def low(v):
    return lax.optimization_barrier(v.astype(jnp.bfloat16)).astype(jnp.float32)

@jax.custom_vjp
def low_back(v):
    return v

def low_keep(v):
    return (low(v), None)

def low_pass(kept, grad):
    return (grad,)

def back_keep(v):
    return (v, None)

def back_low(kept, grad):
    return (low(grad),)
low.defvjp(low_keep, low_pass)
low_back.defvjp(back_keep, back_low)

def layer_norm(h, gain, bias):
    mean_h = lax.optimization_barrier(jnp.mean(h, -1, keepdims=True))
    centred = h - mean_h
    var_h = lax.optimization_barrier(jnp.mean(centred * centred, -1, keepdims=True))
    return centred * lax.rsqrt(var_h + 1e-05) * gain + bias

def matmul_rows(left, weight):
    return jnp.einsum('bld,de->ble', left, weight, precision=HIGH)

def block_pass(params, h, visible):
    w_qkv, w_out, w_fc, w_proj, vectors, fc_bias = params
    rows_here, length = (h.shape[0], h.shape[1])
    a_in = low(layer_norm(h, vectors[0], vectors[1]))
    qkv = low_back(matmul_rows(a_in, w_qkv))
    query = low(qkv[..., :D] + vectors[2]).reshape(rows_here, length, HEADS, HEAD)
    keys = low(qkv[..., D:2 * D]).reshape(rows_here, length, HEADS, HEAD)
    values = low(qkv[..., 2 * D:] + vectors[3]).reshape(rows_here, length, HEADS, HEAD)
    scores = low_back(jnp.einsum('bqhd,bkhd->bhqk', query, keys, precision=HIGH)) * HEAD ** (-0.5)
    scores = jnp.where(visible[:, None], scores, -1e+30)
    probs = low(jax.nn.softmax(scores, axis=-1))
    mixed = jnp.einsum('bhqk,bkhd->bqhd', probs, values, precision=HIGH).reshape(rows_here, length, D)
    mixed = low(low_back(mixed))
    h_mid = h + low_back(matmul_rows(mixed, w_out)) + vectors[4]
    c_in = low(layer_norm(h_mid, vectors[5], vectors[6]))
    f_pre = low_back(matmul_rows(c_in, w_fc)) + fc_bias
    g_in = low(jax.nn.gelu(f_pre, approximate=True))
    return h_mid + low_back(matmul_rows(g_in, w_proj)) + vectors[7]

def forward(params, x_rows, visible, active):
    state = x_rows
    for turn in range(PASSES):
        state = jnp.where((turn < active)[:, None, None], block_pass(params, state, visible), state)
    return state

def adam_update(weight, first, second, grad, keep_frac, t_step):
    first_new = 0.9 * first * keep_frac + 0.1 * grad
    second_new = 0.95 * second * keep_frac + 0.05 * grad * grad
    first_hat = first_new / (1.0 - 0.9 ** t_step)
    second_hat = second_new / (1.0 - 0.95 ** t_step)
    weight_new = weight.astype(jnp.float32) * (1.0 - LEARN_RATE * WEIGHT_DECAY) - LEARN_RATE * first_hat / (jnp.sqrt(second_hat) + 1e-08)
    return (weight_new.astype(jnp.bfloat16), first_new, second_new)

def reference(hidden_in, cotangent, w_qkv, w_out, w_fc, w_proj, vectors, fc_bias, first_qkv, first_out, first_fc, first_proj, first_vectors, first_fc_bias, second_qkv, second_out, second_fc, second_proj, second_vectors, second_fc_bias, seg_ends, pass_counts, reset_flag):
    weights = (w_qkv, w_out, w_fc, w_proj, vectors, fc_bias)
    params = tuple((w.astype(jnp.float32) for w in weights))
    rows_blk = math.gcd(ROWS, max(1, 4096 // ROW_LEN))
    blocks = ROWS // rows_blk
    x_all = hidden_in.astype(jnp.float32).reshape(blocks, rows_blk, ROW_LEN, D)
    cot_all = cotangent.astype(jnp.float32).reshape(blocks, rows_blk, ROW_LEN, D)
    ends_all = seg_ends.reshape(blocks, rows_blk, SEGS)
    active_all = jnp.repeat(pass_counts, N_ROW).reshape(blocks, rows_blk)
    position = jnp.arange(ROW_LEN, dtype=jnp.int32)

    def one_block(acc, inputs):
        x_blk, cot_blk, ends_blk, act_blk = inputs
        segment = lax.optimization_barrier(jnp.sum((position[None, :, None] >= ends_blk[:, None, :]).astype(jnp.int32), -1))
        valid = position[None, :] < ends_blk[:, -1:]
        visible = (segment[:, :, None] == segment[:, None, :]) & (position[None, None, :] <= position[None, :, None])
        out, back = jax.vjp(lambda prm, xin: forward(prm, xin, visible, act_blk), params, x_blk)
        d_params, d_x = back(cot_blk * valid[..., None].astype(jnp.float32))
        acc = tuple((a + b for a, b in zip(acc, d_params)))
        return (acc, (out.astype(jnp.bfloat16), d_x, jnp.sum(valid.astype(jnp.float32))))
    acc_zero = tuple((jnp.zeros(p.shape, jnp.float32) for p in params))
    sums, (outs, d_xs, counts) = lax.scan(one_block, acc_zero, (x_all, cot_all, ends_all, active_all))
    total = jnp.sum(counts)
    grads = tuple((s / total for s in sums))
    keep_feat = 1.0 - reset_flag.astype(jnp.float32)
    keeps = (keep_feat[:, None], keep_feat[:, None], keep_feat[:, None], keep_feat[None, :], keep_feat[None, :], jnp.tile(keep_feat, FF // D))
    t_step = float(STEP)
    firsts = (first_qkv, first_out, first_fc, first_proj, first_vectors, first_fc_bias)
    seconds = (second_qkv, second_out, second_fc, second_proj, second_vectors, second_fc_bias)
    updated = [adam_update(w, m, v, g, kp, t_step) for w, m, v, g, kp in zip(weights, firsts, seconds, grads, keeps)]
    hidden = outs.reshape(TOKENS, D)
    input_grad = d_xs.reshape(TOKENS, D)
    return (hidden, input_grad, grads[0], grads[1], grads[2], grads[3], grads[4], grads[5], updated[0][0], updated[1][0], updated[2][0], updated[3][0], updated[4][0], updated[5][0], updated[0][1], updated[1][1], updated[2][1], updated[3][1], updated[4][1], updated[5][1], updated[0][2], updated[1][2], updated[2][2], updated[3][2], updated[4][2], updated[5][2])
```

```python
import functools

import jax
import jax.numpy as jnp
from jax import lax
from jax.experimental import pallas as pl
from jax.experimental.pallas import tpu as pltpu
from jax.sharding import PartitionSpec as P

D = 768
HEADS = 12
HEAD = 64
FF = 3072
STEP = 10
LEARN_RATE = 0.03
WEIGHT_DECAY = 0.1
F32 = jnp.float32
BF16 = jnp.bfloat16
NN = (((1,), (0,)), ((), ()))
NT = (((1,), (1,)), ((), ()))
TN = (((0,), (0,)), ((), ()))
NB = 256
EXTRA = 16
GELU_A = 0.7978845608028654
GELU_B = 0.044715
BOTH = ("grp", "row")

VM = pl.BlockSpec(memory_space=pltpu.VMEM)
SM = pl.BlockSpec(memory_space=pltpu.SMEM)
HB = pl.BlockSpec(memory_space=pl.ANY)
PARAMS = pltpu.CompilerParams(vmem_limit_bytes=60 * 2**20)


def like(shape, dtype):
    return jax.ShapeDtypeStruct(shape, dtype)


def mm(a, b, dims):
    return lax.dot_general(a, b, dims, preferred_element_type=F32)


def kernel_call(body, outs, specs, scratch=(), out_specs=None):
    return pl.pallas_call(
        body,
        out_shape=outs,
        in_specs=specs,
        out_specs=out_specs or [VM] * len(outs),
        scratch_shapes=list(scratch),
        compiler_params=PARAMS,
    )


def norm_stats(x):
    centred = x - jnp.mean(x, -1, keepdims=True)
    inv = lax.rsqrt(jnp.mean(centred * centred, -1, keepdims=True) + 1e-5)
    return centred * inv, inv


def colsum(x):
    return jnp.sum(x, 0, keepdims=True)


def fill_mask(ends_ref, mask_ref):
    tokens = mask_ref.shape[0]
    n_ends = ends_ref.shape[1]

    def segments(pos):
        seg = jnp.zeros(pos.shape, jnp.int32)
        for e in range(n_ends):
            seg += (pos >= ends_ref[0, e]).astype(jnp.int32)
        return seg

    seg_keys = segments(lax.broadcasted_iota(jnp.int32, (1, tokens), 1))
    for i in range(0, tokens, 128):
        pos = lax.broadcasted_iota(jnp.int32, (128, 1), 0) + i
        key = lax.broadcasted_iota(jnp.int32, (128, tokens), 1)
        seen = (segments(pos) == seg_keys) & (key <= pos)
        mask_ref[i : i + 128, :] = jnp.where(seen, 0.0, -1e30)


def attention_forward(h, wqkv, wout, vec, mask, a, qkv, lse, mixed, h_mid, tile=256):
    tokens = h.shape[0]
    xhat, _ = norm_stats(h[...].astype(F32))
    a[...] = (xhat * vec[0:1, :] + vec[1:2, :]).astype(BF16)
    for part in range(3):
        for j in range(0, D, NB):
            o = part * D + j
            r = mm(a[...], wqkv[:, o : o + NB], NN)
            if part == 0:
                r = r + vec[2:3, j : j + NB]
            if part == 2:
                r = r + vec[3:4, j : j + NB]
            qkv[:, o : o + NB] = r.astype(BF16)
    lanes = lax.broadcasted_iota(jnp.int32, (tile, 128), 1)
    low = lanes < HEAD
    for i in range(tokens // tile):
        rows = slice(i * tile, (i + 1) * tile)
        seen = (i + 1) * tile
        lse[rows, :] = jnp.zeros((tile, 128), F32)
        for p in range(HEADS // 2):
            c = 128 * p
            q = qkv[rows, c : c + 128] * BF16(HEAD**-0.5)
            k = qkv[0:seen, D + c : D + c + 128]
            v = qkv[0:seen, 2 * D + c : 2 * D + c + 128]
            outs = []
            for half in range(2):
                own = low if half == 0 else ~low
                s = mm(jnp.where(own, q, BF16(0)), k, NT) + mask[rows, 0:seen]
                top = jnp.max(s, -1, keepdims=True)
                e = jnp.exp(s - top)
                den = jnp.sum(e, -1, keepdims=True)
                outs.append(mm(e.astype(BF16), v, NN) / den)
                lse[rows, :] = jnp.where(lanes == 2 * p + half, top + jnp.log(den), lse[rows, :])
            mixed[rows, c : c + 128] = jnp.where(low, outs[0], outs[1]).astype(BF16)
    for j in range(0, D, NB):
        r = mm(mixed[...], wout[:, j : j + NB], NN)
        h_mid[:, j : j + NB] = h[:, j : j + NB].astype(F32) + r + vec[4:5, j : j + NB]


def ffn_forward(h_mid, wfc, wpt, vec, fb, c, g, gp, h_out):
    xhat, _ = norm_stats(h_mid[...])
    c[...] = (xhat * vec[5:6, :] + vec[6:7, :]).astype(BF16)
    for j in range(0, FF, NB):
        f = mm(c[...], wfc[:, j : j + NB], NN) + fb[0:1, j : j + NB]
        sq = f * f
        t = jnp.tanh(GELU_A * (f + GELU_B * sq * f))
        half = 0.5 * (1.0 + t)
        g[:, j : j + NB] = (f * half).astype(BF16)
        slope = half + (0.5 * GELU_A) * f * (1.0 - t * t) * (1.0 + (3 * GELU_B) * sq)
        gp[:, j : j + NB] = slope.astype(BF16)
    for j in range(0, D, NB):
        r = mm(g[...], wpt[j : j + NB, :], NT)
        h_out[:, j : j + NB] = h_mid[:, j : j + NB] + r + vec[7:8, j : j + NB]


def norm_backward(dout, x, gain):
    xhat, inv = norm_stats(x)
    d_gain = colsum(dout * xhat)
    d_bias = colsum(dout)
    dx = dout * gain
    m1 = jnp.mean(dx, -1, keepdims=True)
    m2 = jnp.mean(dx * xhat, -1, keepdims=True)
    return inv * (dx - m1 - xhat * m2), d_gain, d_bias


def ffn_backward(dy, h_mid, gp, wfc, wpt, vec, dy_low, df_low, dfb, dh_mid, dh_low, dvec, dc):
    d_out = dy[...]
    dy_low[...] = d_out.astype(BF16)
    dvec[0:4, :] = jnp.zeros((4, D), F32)
    dvec[7:8, :] = colsum(d_out)
    for j in range(0, FF, NB):
        d = mm(dy_low[...], wpt[:, j : j + NB], NN)
        df = d * gp[:, j : j + NB].astype(F32)
        dfb[0:1, j : j + NB] = colsum(df)
        df_low[:, j : j + NB] = df.astype(BF16)
    for j in range(0, D, NB):
        dc[:, j : j + NB] = mm(df_low[...], wfc[j : j + NB, :], NT)
    dx, d_gain, d_bias = norm_backward(dc[...], h_mid[...], vec[5:6, :])
    total = dy[...] + dx
    dh_mid[...] = total
    dh_low[...] = total.astype(BF16)
    dvec[4:5, :] = colsum(total)
    dvec[5:6, :] = d_gain
    dvec[6:7, :] = d_bias


def attention_backward(
    dh_mid, dh_low, h, qkv, lse, mixed, mask, wqkv, wout, vec, dmix, dqkv, da, d_in, dvec
):
    tokens = h.shape[0]
    for j in range(0, D, NB):
        dmix[:, j : j + NB] = mm(dh_low[...], wout[j : j + NB, :], NT).astype(BF16)
    low = lax.broadcasted_iota(jnp.int32, (tokens, 128), 1) < HEAD
    low_rows = lax.broadcasted_iota(jnp.int32, (128, tokens), 0) < HEAD
    for p in range(HEADS // 2):
        c = 128 * p
        cs = slice(c, c + 128)
        q = qkv[:, cs] * BF16(HEAD**-0.5)
        k = qkv[:, D + c : D + c + 128]
        v = qkv[:, 2 * D + c : 2 * D + c + 128]
        dm = dmix[:, cs]
        prod = dm.astype(F32) * mixed[:, cs].astype(F32)
        dm_t = dm.astype(F32).T.astype(BF16)
        q_t = q.astype(F32).T.astype(BF16)
        dq = jnp.zeros((tokens, 128), F32)
        dk_t = jnp.zeros((128, tokens), F32)
        dv_t = jnp.zeros((128, tokens), F32)
        for half in range(2):
            own = low if half == 0 else ~low
            own_rows = low_rows if half == 0 else ~low_rows
            delta = jnp.sum(jnp.where(own, prod, 0.0), -1, keepdims=True)
            s = mm(jnp.where(own, q, BF16(0)), k, NT) + mask[...]
            probs = jnp.exp(s - lse[:, 2 * p + half : 2 * p + half + 1])
            dp = mm(jnp.where(own, dm, BF16(0)), v, NT)
            ds = (probs * (dp - delta)).astype(BF16)
            dv_t += mm(jnp.where(own_rows, dm_t, BF16(0)), probs.astype(BF16), NN)
            dk_t += mm(jnp.where(own_rows, q_t, BF16(0)), ds, NN)
            dq += mm(ds, jnp.where(own, k, BF16(0)), NN)
        dq = dq * HEAD**-0.5
        dv = dv_t.T
        dvec[2:3, cs] = colsum(dq)
        dvec[3:4, cs] = colsum(dv)
        dqkv[:, cs] = dq.astype(BF16)
        dqkv[:, D + c : D + c + 128] = dk_t.T.astype(BF16)
        dqkv[:, 2 * D + c : 2 * D + c + 128] = dv.astype(BF16)
    for j in range(0, D, NB):
        da[:, j : j + NB] = mm(dqkv[...], wqkv[j : j + NB, :], NT)
    dx, d_gain, d_bias = norm_backward(da[...], h[...].astype(F32), vec[0:1, :])
    d_in[...] = dh_mid[...] + dx
    dvec[4:8, :] = jnp.zeros((4, D), F32)
    dvec[0:1, :] = d_gain
    dvec[1:2, :] = d_bias


def attention_forward_call(ends, h, wqkv, wout, vec):
    t = h.shape[0]

    def body(ends, h, wqkv, wout, vec, a, qkv, lse, mixed, h_mid, mask):
        fill_mask(ends, mask)
        attention_forward(h, wqkv, wout, vec, mask, a, qkv, lse, mixed, h_mid)

    outs = [
        like((t, D), BF16),
        like((t, 3 * D), BF16),
        like((t, 128), F32),
        like((t, D), BF16),
        like((t, D), F32),
    ]
    return kernel_call(body, outs, [SM, VM, VM, VM, VM], [pltpu.VMEM((t, t), F32)])(
        ends, h, wqkv, wout, vec
    )


def ffn_forward_call(h_mid, wfc, wpt, vec, fb):
    t = h_mid.shape[0]
    outs = [like((t, D), BF16), like((t, FF), BF16), like((t, FF), BF16), like((t, D), F32)]
    return kernel_call(ffn_forward, outs, [VM] * 5)(h_mid, wfc, wpt, vec, fb)


def ffn_backward_call(dy, h_mid, gp, wfc, wpt, vec):
    t = dy.shape[0]
    outs = [
        like((t, D), BF16),
        like((t, FF), BF16),
        like((1, FF), F32),
        like((t, D), F32),
        like((t, D), BF16),
        like((8, D), F32),
    ]
    return kernel_call(ffn_backward, outs, [VM] * 6, [pltpu.VMEM((t, D), F32)])(
        dy, h_mid, gp, wfc, wpt, vec
    )


def attention_backward_call(ends, dh_mid, dh_low, h, qkv, lse, mixed, wqkv, wout, vec):
    t = h.shape[0]

    def body(
        ends, dh_mid, dh_low, h, qkv, lse, mixed, wqkv, wout, vec, dqkv, d_in, dvec, mask, dmix, da
    ):
        fill_mask(ends, mask)
        attention_backward(
            dh_mid, dh_low, h, qkv, lse, mixed, mask, wqkv, wout, vec, dmix, dqkv, da, d_in, dvec
        )

    outs = [like((t, 3 * D), BF16), like((t, D), F32), like((8, D), F32)]
    scratch = [pltpu.VMEM((t, t), F32), pltpu.VMEM((t, D), BF16), pltpu.VMEM((t, D), F32)]
    return kernel_call(body, outs, [SM] + [VM] * 9, scratch)(
        ends, dh_mid, dh_low, h, qkv, lse, mixed, wqkv, wout, vec
    )


class Cube:
    def __init__(self, groups, rows):
        self.groups, self.rows = groups, rows
        self.n = groups * rows
        self.bits = self.n.bit_length() - 1
        far = list(range(self.bits - 1, 2, -1))
        self.gather_plans = (far + [2, 1], far + [1, 2])
        self.scatter_plans = tuple(list(reversed(p)) for p in self.gather_plans)
        self.half = self.n // 2

    def swap(self, x, plans, step):
        pairs = [(i, i ^ (1 << plans[i & 1][step])) for i in range(self.n)]
        return lax.ppermute(x, BOTH, pairs)

    def swap_core(self, x):
        return lax.ppermute(x, BOTH, [(i, i ^ 1) for i in range(self.n)])

    def gather(self, block):
        held = block[None]
        for step in range(self.bits - 1):
            held = jnp.concatenate([held, self.swap(held, self.gather_plans, step)], 0)
        return held, self.swap_core(held)

    def scatter(self, slots):
        held = slots[: self.half] + self.swap_core(slots[self.half :])
        for step in range(self.bits - 1):
            mid = held.shape[0] // 2
            got = self.swap(held[mid:], self.scatter_plans, step)
            held = held[:mid] + got
        return held[0]

    def gather_source(self, me, side, slot):
        core = (me & 1) ^ side
        dest = me ^ side
        for k in range(self.bits - 1):
            if (slot >> k) & 1:
                flip0, flip1 = 1 << self.gather_plans[0][k], 1 << self.gather_plans[1][k]
                dest = dest ^ jnp.where(core == 1, flip1, flip0)
        return dest

    def scatter_slot(self, me, dest):
        rel = me ^ dest
        core = dest & 1
        slot = (rel & 1) * self.half
        for k in range(self.bits - 1):
            place = self.bits - 2 - k
            b0 = (rel >> self.scatter_plans[0][k]) & 1
            b1 = (rel >> self.scatter_plans[1][k]) & 1
            slot = slot + (jnp.where(core == 1, b1, b0) << place)
        return slot


def my_number(cube):
    return lax.axis_index("grp") * cube.rows + lax.axis_index("row")


def canonical(cube, held, other):
    me = my_number(cube)
    ids = [cube.gather_source(me, side, s) for side in (0, 1) for s in range(cube.half)]
    return jnp.zeros((cube.n,) + held.shape[1:], held.dtype).at[jnp.stack(ids)].set(
        jnp.concatenate([held, other], 0)
    )


def fits(rows, cols):
    return rows % 16 == 0 and cols % 128 == 0


def place_blocks(cube, held, other, sem, target):
    me = my_number(cube)
    copies = []
    for side, src in enumerate((held, other)):
        for s in range(cube.half):
            dev = cube.gather_source(me, side, s)
            copies.append(
                pltpu.make_async_copy(src.at[s], target(dev // cube.rows, dev % cube.rows), sem)
            )
    for cp in copies:
        cp.start()
    for cp in copies:
        cp.wait()


def assemble_fc(cube, held, other):
    br, bc = held.shape[1:]
    if not fits(br, bc):
        full = canonical(cube, held, other).reshape(cube.groups, cube.rows, br, bc)
        return full.transpose(1, 2, 0, 3).reshape(cube.rows * br, cube.groups * bc)

    def body(held, other, out, sem):
        def target(g, r):
            return out.at[pl.ds(pl.multiple_of(r * br, 16), br), pl.ds(pl.multiple_of(g * bc, 128), bc)]

        place_blocks(cube, held, other, sem, target)

    outs = [like((cube.rows * br, cube.groups * bc), BF16)]
    return kernel_call(body, outs, [HB, HB], [pltpu.SemaphoreType.DMA], [HB])(held, other)[0]


def assemble_proj(cube, held, other):
    br, bc = held.shape[1:]
    if not fits(br, bc):
        full = canonical(cube, held, other).reshape(cube.groups, cube.rows, br, bc)
        return full.transpose(0, 2, 1, 3).reshape(cube.groups * br, cube.rows * bc)

    def body(held, other, out, sem):
        def target(g, r):
            return out.at[pl.ds(pl.multiple_of(g * br, 16), br), pl.ds(pl.multiple_of(r * bc, 128), bc)]

        place_blocks(cube, held, other, sem, target)

    outs = [like((cube.groups * br, cube.rows * bc), BF16)]
    return kernel_call(body, outs, [HB, HB], [pltpu.SemaphoreType.DMA], [HB])(held, other)[0]


def assemble_attn(cube, held, other, sizes):
    bq, bo, rows_w, vrows, vcols, bias = sizes
    g_n, r_n = cube.groups, cube.rows
    br, bc = held.shape[1:]
    if not fits(br, bc):
        full = canonical(cube, held, other).reshape(g_n, r_n, br, bc)
        body_part = full[:, :, :rows_w]
        wqkv = body_part[..., :bq].transpose(1, 2, 0, 3).reshape(r_n * rows_w, g_n * bq)
        wout = body_part[..., bq : bq + bo].transpose(1, 2, 0, 3).reshape(r_n * rows_w, g_n * bo)
        ext = full[:, :, rows_w:].astype(F32)
        vec = ext[:, :, :vrows, :vcols].transpose(1, 2, 0, 3).reshape(r_n * vrows, g_n * vcols)
        fb = ext[:, :, vrows, :bias].reshape(1, g_n * r_n * bias)
        total = jnp.sum(ext[:, :, vrows + 1, 0]) * 16.0 + jnp.sum(ext[:, :, vrows + 1, 1])
        return wqkv, wout, vec, fb, jnp.full((8, 128), total, F32)

    def body(held, other, wqkv, wout, vec, fb, tot, blk, sem):
        def target(g, r):
            return blk.at[g, pl.ds(pl.multiple_of(r * br, 16), br)]

        place_blocks(cube, held, other, sem, target)
        count = jnp.zeros((1, 128), F32)
        for g in range(g_n):
            for r in range(r_n):
                rows = slice(r * rows_w, (r + 1) * rows_w)
                wqkv[rows, g * bq : (g + 1) * bq] = blk[g, r * br : r * br + rows_w, 0:bq]
                wout[rows, g * bo : (g + 1) * bo] = blk[g, r * br : r * br + rows_w, bq : bq + bo]
                ext = blk[g, r * br + rows_w : r * br + rows_w + EXTRA, :].astype(F32)
                vec[r * vrows : (r + 1) * vrows, g * vcols : (g + 1) * vcols] = ext[0:vrows, 0:vcols]
                at = (g * r_n + r) * bias
                fb[0:1, at : at + bias] = ext[vrows : vrows + 1, 0:bias]
                count += ext[vrows + 1 : vrows + 2, 0:128]
        lane = lax.broadcasted_iota(jnp.int32, (1, 128), 1)
        weight = jnp.where(lane == 0, 16.0, jnp.where(lane == 1, 1.0, 0.0))
        tot[...] = jnp.broadcast_to(jnp.sum(count * weight, -1, keepdims=True), (8, 128))

    outs = [
        like((r_n * rows_w, g_n * bq), BF16),
        like((r_n * rows_w, g_n * bo), BF16),
        like((r_n * vrows, g_n * vcols), F32),
        like((1, g_n * r_n * bias), F32),
        like((8, 128), F32),
    ]
    scratch = [pltpu.VMEM((g_n, r_n * br, bc), BF16), pltpu.SemaphoreType.DMA]
    return kernel_call(body, outs, [HB, HB], scratch)(held, other)


def ordered_slots(cube, blocks):
    me = my_number(cube)
    slots = jnp.stack([cube.scatter_slot(me, dest) for dest in range(cube.n)])
    return jnp.zeros_like(blocks).at[slots].set(blocks)


def stacked_t(parts, out):
    t = parts[0].shape[0]
    for i, part in enumerate(parts):
        out[:, i * t : (i + 1) * t] = part[...].astype(F32).T.astype(BF16)


def grad_fc_blocks(cube, c1, c0, df1, df0, br, bc):
    if not fits(br, bc):
        full = mm(c1, df1, TN) + mm(c0, df0, TN)
        full = full.astype(BF16).reshape(cube.rows, br, cube.groups, bc).transpose(2, 0, 1, 3)
        return ordered_slots(cube, full.reshape(cube.n, br, bc))
    t = c1.shape[0]

    def body(c1, c0, df1, df0, out, ct):
        me = my_number(cube)
        stacked_t((c1, c0), ct)
        for g in range(cube.groups):
            cols = slice(g * bc, (g + 1) * bc)
            full = mm(ct[:, 0:t], df1[:, cols], NN) + mm(ct[:, t : 2 * t], df0[:, cols], NN)
            full = full.astype(BF16)
            for r in range(cube.rows):
                slot = cube.scatter_slot(me, g * cube.rows + r)
                out[slot] = full[r * br : (r + 1) * br]

    outs = [like((cube.n, br, bc), BF16)]
    return kernel_call(body, outs, [VM] * 4, [pltpu.VMEM((D, 2 * t), BF16)])(c1, c0, df1, df0)[0]


def grad_proj_blocks(cube, dy1, dy0, g1, g0, br, bc):
    if not fits(br, bc):
        full = mm(dy1, g1, TN) + mm(dy0, g0, TN)
        full = full.astype(BF16).reshape(cube.groups, br, cube.rows, bc).transpose(0, 2, 1, 3)
        return ordered_slots(cube, full.reshape(cube.n, br, bc))
    t = dy1.shape[0]

    def body(dy1, dy0, g1, g0, out, dyt):
        me = my_number(cube)
        stacked_t((dy1, dy0), dyt)
        for r in range(cube.rows):
            cols = slice(r * bc, (r + 1) * bc)
            full = mm(dyt[:, 0:t], g1[:, cols], NN) + mm(dyt[:, t : 2 * t], g0[:, cols], NN)
            full = full.astype(BF16)
            for g in range(cube.groups):
                slot = cube.scatter_slot(me, g * cube.rows + r)
                out[slot] = full[g * br : (g + 1) * br]

    outs = [like((cube.n, br, bc), BF16)]
    return kernel_call(body, outs, [VM] * 4, [pltpu.VMEM((D, 2 * t), BF16)])(dy1, dy0, g1, g0)[0]


def grad_attn_blocks(cube, a1, a0, dq1, dq0, m1, m0, dh1, dh0, dvec, dfb, sizes, br, bc):
    bq, bo, rows_w, vrows, vcols, bias = sizes
    g_n, r_n = cube.groups, cube.rows
    if not fits(br, bc):
        dqkv = mm(a1, dq1, TN) + mm(a0, dq0, TN)
        dout = mm(m1, dh1, TN) + mm(m0, dh0, TN)
        wide = jnp.concatenate(
            [dqkv.reshape(r_n, rows_w, g_n, bq), dout.reshape(r_n, rows_w, g_n, bo)], -1
        ).transpose(2, 0, 1, 3)
        vecs = dvec.reshape(r_n, vrows, g_n, vcols).transpose(2, 0, 1, 3)
        biases = dfb.reshape(g_n, r_n, 1, bias)
        ext = jnp.zeros((g_n, r_n, EXTRA, bc), F32)
        ext = ext.at[:, :, :vrows, :vcols].set(vecs).at[:, :, vrows : vrows + 1, :bias].set(biases)
        full = jnp.concatenate([wide, ext], 2).astype(BF16)
        return ordered_slots(cube, full.reshape(cube.n, br, bc))
    t = a1.shape[0]

    def body(a1, a0, dq1, dq0, m1, m0, dh1, dh0, dvec, dfb, out, lt, wide):
        me = my_number(cube)
        stacked_t((a1, a0), lt)
        for j in range(0, 3 * D, NB):
            cols = slice(j, j + NB)
            full = mm(lt[:, 0:t], dq1[:, cols], NN) + mm(lt[:, t : 2 * t], dq0[:, cols], NN)
            wide[:, cols] = full.astype(BF16)
        stacked_t((m1, m0), lt)
        for j in range(0, D, NB):
            cols = slice(j, j + NB)
            full = mm(lt[:, 0:t], dh1[:, cols], NN) + mm(lt[:, t : 2 * t], dh0[:, cols], NN)
            wide[:, 3 * D + j : 3 * D + j + NB] = full.astype(BF16)
        for g in range(g_n):
            for r in range(r_n):
                slot = cube.scatter_slot(me, g * r_n + r)
                rows = slice(r * rows_w, (r + 1) * rows_w)
                out[slot, 0:rows_w, 0:bq] = wide[rows, g * bq : (g + 1) * bq]
                out[slot, 0:rows_w, bq : bq + bo] = wide[rows, 3 * D + g * bo : 3 * D + (g + 1) * bo]
                vecs = dvec[r * vrows : (r + 1) * vrows, g * vcols : (g + 1) * vcols]
                at = (g * r_n + r) * bias
                ext = jnp.concatenate(
                    [
                        jnp.concatenate([vecs, jnp.zeros((vrows, bc - vcols), F32)], 1),
                        jnp.concatenate([dfb[0:1, at : at + bias], jnp.zeros((1, bc - bias), F32)], 1),
                        jnp.zeros((EXTRA - vrows - 1, bc), F32),
                    ],
                    0,
                )
                out[slot, rows_w : rows_w + EXTRA, :] = ext.astype(BF16)

    outs = [like((cube.n, br, bc), BF16)]
    scratch = [pltpu.VMEM((D, 2 * t), BF16), pltpu.VMEM((D, 4 * D), BF16)]
    return kernel_call(body, outs, [VM] * 10, scratch)(a1, a0, dq1, dq0, m1, m0, dh1, dh0, dvec, dfb)[0]


def adam_update(weight, first, second, grad, keep_frac):
    t_step = float(STEP)
    first_new = 0.9 * first * keep_frac + 0.1 * grad
    second_new = 0.95 * second * keep_frac + 0.05 * grad * grad
    first_hat = first_new / (1.0 - 0.9**t_step)
    second_hat = second_new / (1.0 - 0.95**t_step)
    weight_new = weight.astype(F32) * (1.0 - LEARN_RATE * WEIGHT_DECAY) - LEARN_RATE * first_hat / (
        jnp.sqrt(second_hat) + 1e-08
    )
    return (weight_new.astype(BF16), first_new, second_new)


def body(
    hidden_in,
    cotangent,
    w_qkv,
    w_out,
    w_fc,
    w_proj,
    vectors,
    fc_bias,
    first_qkv,
    first_out,
    first_fc,
    first_proj,
    first_vectors,
    first_fc_bias,
    second_qkv,
    second_out,
    second_fc,
    second_proj,
    second_vectors,
    second_fc_bias,
    seg_ends,
    pass_counts,
    reset_flag,
):
    cube = Cube(lax.axis_size("grp"), lax.axis_size("row"))
    rows_w, bq = w_qkv.shape
    bo = w_out.shape[1]
    vrows, vcols = vectors.shape
    bias = fc_bias.shape[0]
    sizes = (bq, bo, rows_w, vrows, vcols, bias)
    wide = bq + bo
    length = hidden_in.shape[0]
    n_valid = seg_ends[0, -1]

    ext = jnp.zeros((EXTRA, wide), BF16)
    ext = lax.dynamic_update_slice(ext, vectors, (0, 0))
    ext = lax.dynamic_update_slice(ext, fc_bias[None], (vrows, 0))
    split = jnp.stack([n_valid // 16, n_valid % 16]).astype(BF16)[None]
    ext = lax.dynamic_update_slice(ext, split, (vrows + 1, 0))
    block_a = jnp.concatenate([jnp.concatenate([w_qkv, w_out], 1), ext], 0)
    wqkv, wout, vec, fb, tot = assemble_attn(cube, *cube.gather(block_a), sizes)
    wfc = assemble_fc(cube, *cube.gather(w_fc))
    wpt = assemble_proj(cube, *cube.gather(w_proj.T))
    total = tot[0, 0]

    active = pass_counts[0] > 1
    h0 = hidden_in
    a0, qkv0, lse0, mixed0, mid0 = attention_forward_call(seg_ends, h0, wqkv, wout, vec)
    c0, g0, gp0, h1 = ffn_forward_call(mid0, wfc, wpt, vec, fb)
    a1, qkv1, lse1, mixed1, mid1 = attention_forward_call(seg_ends, h1, wqkv, wout, vec)
    c1, g1, gp1, h2 = ffn_forward_call(mid1, wfc, wpt, vec, fb)
    hidden = jnp.where(active, h2, h1).astype(BF16)

    valid = (jnp.arange(length, dtype=jnp.int32) < n_valid)[:, None]
    d2 = jnp.where(valid, cotangent.astype(F32), 0.0)
    dy1 = jnp.where(active, d2, 0.0)
    dyl1, dfl1, dfb1, dhm1, dhl1, dvf1 = ffn_backward_call(dy1, mid1, gp1, wfc, wpt, vec)
    dqkv1, din1, dva1 = attention_backward_call(
        seg_ends, dhm1, dhl1, h1, qkv1, lse1, mixed1, wqkv, wout, vec
    )
    d1 = jnp.where(active, din1, d2)
    dyl0 = d1.astype(BF16)
    sum_p = cube.scatter(grad_proj_blocks(cube, dyl1, dyl0, g1, g0, vcols, w_proj.shape[0]))
    dyl0, dfl0, dfb0, dhm0, dhl0, dvf0 = ffn_backward_call(d1, mid0, gp0, wfc, wpt, vec)
    sum_f = cube.scatter(grad_fc_blocks(cube, c1, c0, dfl1, dfl0, *w_fc.shape))
    dqkv0, input_grad, dva0 = attention_backward_call(
        seg_ends, dhm0, dhl0, h0, qkv0, lse0, mixed0, wqkv, wout, vec
    )
    dvec = dvf1 + dva1 + dvf0 + dva0
    dfb = dfb1 + dfb0
    sum_a = cube.scatter(
        grad_attn_blocks(
            cube, a1, a0, dqkv1, dqkv0, mixed1, mixed0, dhl1, dhl0, dvec, dfb, sizes, rows_w + EXTRA, wide
        )
    )

    sum_a = sum_a.astype(F32)
    summed = (
        sum_a[:rows_w, :bq],
        sum_a[:rows_w, bq:],
        sum_f.astype(F32),
        sum_p.T.astype(F32),
        sum_a[rows_w : rows_w + vrows, :vcols],
        sum_a[rows_w + vrows, :bias],
    )
    grads = tuple(s / total for s in summed)
    keep_feat = 1.0 - reset_flag.astype(F32)
    keep_rows = lax.dynamic_slice_in_dim(keep_feat, lax.axis_index("row") * rows_w, rows_w)[:, None]
    keep_cols = lax.dynamic_slice_in_dim(keep_feat, lax.axis_index("grp") * vcols, vcols)[None, :]
    bias_index = (my_number(cube) * bias + jnp.arange(bias, dtype=jnp.int32)) % D
    keeps = (keep_rows, keep_rows, keep_rows, keep_cols, keep_cols, keep_feat[bias_index])
    weights = (w_qkv, w_out, w_fc, w_proj, vectors, fc_bias)
    firsts = (first_qkv, first_out, first_fc, first_proj, first_vectors, first_fc_bias)
    seconds = (second_qkv, second_out, second_fc, second_proj, second_vectors, second_fc_bias)
    updated = [
        adam_update(w, m, v, g, kp) for w, m, v, g, kp in zip(weights, firsts, seconds, grads, keeps)
    ]
    return (
        (hidden, input_grad)
        + grads
        + tuple(u[0] for u in updated)
        + tuple(u[1] for u in updated)
        + tuple(u[2] for u in updated)
    )


def solution(mesh):
    tokens = P(("grp", "row"), None)
    flat = P(("grp", "row"))
    tiles = P("row", "grp")
    six = (tiles, tiles, tiles, tiles, tiles, flat)
    return jax.shard_map(
        body,
        mesh=mesh,
        in_specs=(tokens, tokens) + six * 3 + (tokens, P("grp"), P()),
        out_specs=(tokens, tokens) + six * 4,
        check_vma=False,
    )
```

```python
import functools

import jax
import jax.numpy as jnp
from jax import lax
from jax.experimental import pallas as pl
from jax.experimental.pallas import tpu as pltpu
from jax.sharding import PartitionSpec as P

D = 768
HEADS = 12
HEAD = 64
FF = 3072
STEP = 10
LEARN_RATE = 0.03
WEIGHT_DECAY = 0.1
F32 = jnp.float32
BF16 = jnp.bfloat16
NN = (((1,), (0,)), ((), ()))
NT = (((1,), (1,)), ((), ()))
TN = (((0,), (0,)), ((), ()))
NB = 256
LN_ROWS = 32
EXTRA = 16
GELU_A = 0.7978845608028654
GELU_B = 0.044715
BOTH = ("grp", "row")

VM = pl.BlockSpec(memory_space=pltpu.VMEM)
SM = pl.BlockSpec(memory_space=pltpu.SMEM)
HB = pl.BlockSpec(memory_space=pl.ANY)
PARAMS = pltpu.CompilerParams(vmem_limit_bytes=60 * 2**20)


def like(shape, dtype):
    return jax.ShapeDtypeStruct(shape, dtype)


def mm(a, b, dims):
    return lax.dot_general(a, b, dims, preferred_element_type=F32)


def kernel_call(body, outs, specs, scratch=(), us=5):
    return pl.pallas_call(
        body,
        out_shape=outs,
        in_specs=specs,
        out_specs=[VM] * len(outs),
        scratch_shapes=list(scratch),
        compiler_params=PARAMS,
        cost_estimate=pl.CostEstimate(
            flops=int(us * 1e9), bytes_accessed=int(us * 3e6), transcendentals=0
        ),
    )


class Fetched:
    def __init__(self, src, dst, sems, axis):
        self.ref, n = dst, len(sems)
        size = dst.shape[axis] // n
        self.copies, self.begun, self.waited = [], 0, 0
        for i in range(n):
            at = tuple(pl.ds(i * size, size) if d == axis else slice(None) for d in range(len(dst.shape)))
            self.copies.append(pltpu.make_async_copy(src.at[at], dst.at[at], sems[i]))

    def start(self, n=None):
        for copy in self.copies[self.begun : n]:
            copy.start()
            self.begun += 1

    def get(self, n=None):
        self.start(n)
        for copy in self.copies[self.waited : n]:
            copy.wait()
            self.waited += 1
        return self.ref


class Flushed:
    def __init__(self, dst, src, sems):
        self.dst, self.ref, self.sems, self.copies = dst, src, list(sems), []

    def flush(self, *at):
        at = at or (slice(None),)
        copy = pltpu.make_async_copy(self.ref.at[at], self.dst.at[at], self.sems[len(self.copies)])
        copy.start()
        self.copies.append(copy)

    def finish(self):
        if not self.copies:
            self.flush()
        for copy in self.copies:
            copy.wait()


class Sink:
    def __init__(self, dst, sems):
        self.dst, self.sems, self.copies = dst, list(sems), []

    def put(self, src, slot):
        copy = pltpu.make_async_copy(src, self.dst.at[slot], self.sems[len(self.copies)])
        copy.start()
        self.copies.append(copy)

    def finish(self):
        for copy in self.copies:
            copy.wait()


def staged_call(body, ins, outs, scratch=(), us=5):
    n_in, n_out = len(ins), len(outs)
    spec_of = {"smem": SM, "vmem": VM, "any": HB, "fetch": HB, "flush": HB, "sink": HB}
    fetches = [i for i, how in enumerate(ins) if how[1] == "fetch"]
    flushes = [i for i, how in enumerate(outs) if how[2] == "flush"]
    sinks = [i for i, how in enumerate(outs) if how[2] == "sink"]
    extra = [pltpu.VMEM(ins[i][0].shape, ins[i][0].dtype) for i in fetches]
    extra += [pltpu.VMEM(outs[i][0], outs[i][1]) for i in flushes]
    counts = [(ins[i] + (0, 1))[3] if len(ins[i]) > 2 else 1 for i in fetches]
    counts += [outs[i][3] if len(outs[i]) > 3 else 1 for i in flushes + sinks]
    axes = [ins[i][2] if len(ins[i]) > 2 else 0 for i in fetches]
    extra += [pltpu.SemaphoreType.DMA((max(sum(counts), 1),))]

    def run(*refs):
        given, made = list(refs[:n_in]), list(refs[n_in : n_in + n_out])
        rest = refs[n_in + n_out :]
        own, mine = rest[: len(scratch)], rest[len(scratch) :]
        buffers, sem = mine[:-1], mine[-1]
        first = 0
        for j, i in enumerate(fetches + flushes + sinks):
            sems = [sem.at[first + k] for k in range(counts[j])]
            first += counts[j]
            if j < len(fetches):
                given[i] = Fetched(given[i], buffers[j], sems, axes[j])
            elif j < len(buffers):
                made[i] = Flushed(made[i], buffers[j], sems)
            else:
                made[i] = Sink(made[i], sems)
        body(*given, *made, *own)
        for i in fetches:
            given[i].get()
        for i in flushes + sinks:
            made[i].finish()

    return pl.pallas_call(
        run,
        out_shape=[like(out[0], out[1]) for out in outs],
        in_specs=[spec_of[how[1]] for how in ins],
        out_specs=[spec_of[how[2]] for how in outs],
        scratch_shapes=list(scratch) + extra,
        compiler_params=PARAMS,
        cost_estimate=pl.CostEstimate(
            flops=int(us * 1e9), bytes_accessed=int(us * 3e6), transcendentals=0
        ),
    )(*[how[0] for how in ins])


def norm_stats(x):
    centred = x - jnp.mean(x, -1, keepdims=True)
    inv = lax.rsqrt(jnp.mean(centred * centred, -1, keepdims=True) + 1e-5)
    return centred * inv, inv


def colsum(x):
    return jnp.sum(x, 0, keepdims=True)


def norm_forward(x, gain, bias, out):
    for i in range(0, x.shape[0], LN_ROWS):
        rows = slice(i, i + LN_ROWS)
        xhat, _ = norm_stats(x[rows, :].astype(F32))
        out[rows, :] = (xhat * gain + bias).astype(BF16)


def fold(x):
    return jnp.sum(x.reshape(x.shape[0] // 8, 8, x.shape[1]), 0)


def fill_mask(ends_ref, mask_ref):
    tokens = mask_ref.shape[0]
    n_ends = ends_ref.shape[1]

    def segments(pos):
        seg = jnp.zeros(pos.shape, jnp.int32)
        for e in range(n_ends):
            seg += (pos >= ends_ref[0, e]).astype(jnp.int32)
        return seg

    seg_keys = segments(lax.broadcasted_iota(jnp.int32, (1, tokens), 1))
    for i in range(0, tokens, 128):
        pos = lax.broadcasted_iota(jnp.int32, (128, 1), 0) + i
        key = lax.broadcasted_iota(jnp.int32, (128, tokens), 1)
        seen = (segments(pos) == seg_keys) & (key <= pos)
        mask_ref[i : i + 128, :] = jnp.where(seen, 0.0, -1e30)


def attention_forward(h, wqkv, wout, vec, mask, a, qkv, lse, mixed, h_mid, tile=256, done=None):
    tokens = h.shape[0]
    done = done or (lambda which: None)
    norm_forward(h, vec[0:1, :], vec[1:2, :], a)
    for part in range(3):
        for j in range(0, D, NB):
            o = part * D + j
            r = mm(a[...], wqkv[:, o : o + NB], NN)
            if part == 0:
                r = r + vec[2:3, j : j + NB]
            if part == 2:
                r = r + vec[3:4, j : j + NB]
            qkv[:, o : o + NB] = r.astype(BF16)
    done("qkv")
    lanes = lax.broadcasted_iota(jnp.int32, (tile, 128), 1)
    low = lanes < HEAD
    together = 2
    for i in range(tokens // tile):
        rows = slice(i * tile, (i + 1) * tile)
        seen = (i + 1) * tile
        logs = jnp.zeros((tile, 128), F32)
        for first in range(0, HEADS // 2, together):
            jobs = [(p, half) for p in range(first, first + together) for half in range(2)]
            scores = []
            for p, half in jobs:
                q = qkv[rows, 128 * p : 128 * p + 128] * BF16(HEAD**-0.5)
                k = qkv[0:seen, D + 128 * p : D + 128 * p + 128]
                own = low if half == 0 else ~low
                scores.append(mm(jnp.where(own, q, BF16(0)), k, NT) + mask[rows, 0:seen])
            tops = [jnp.max(x, -1, keepdims=True) for x in scores]
            expo = [jnp.exp(x - top) for x, top in zip(scores, tops)]
            dens = [jnp.sum(x, -1, keepdims=True) for x in expo]
            outs = []
            for (p, half), x, den, top in zip(jobs, expo, dens, tops):
                v = qkv[0:seen, 2 * D + 128 * p : 2 * D + 128 * p + 128]
                outs.append(mm(x.astype(BF16), v, NN) / den)
                logs = jnp.where(lanes == 2 * p + half, top + jnp.log(den), logs)
            for n, (p, half) in enumerate(jobs):
                if half == 1:
                    mixed[rows, 128 * p : 128 * p + 128] = jnp.where(low, outs[n - 1], outs[n]).astype(BF16)
        lse[rows, :] = logs
    done("mixed")
    for j in range(0, D, NB):
        r = mm(mixed[...], wout[:, j : j + NB], NN)
        h_mid[:, j : j + NB] = h[:, j : j + NB].astype(F32) + r + vec[4:5, j : j + NB]


def fc_forward(h_mid, wfc, vec, fb, c, g, gp):
    norm_forward(h_mid, vec[5:6, :], vec[6:7, :], c)
    for j in range(0, FF, NB):
        f = mm(c[...], wfc[:, j : j + NB], NN) + fb[0:1, j : j + NB]
        sq = f * f
        t = jnp.tanh(GELU_A * (f + GELU_B * sq * f))
        half = 0.5 * (1.0 + t)
        g[:, j : j + NB] = (f * half).astype(BF16)
        slope = half + (0.5 * GELU_A) * f * (1.0 - t * t) * (1.0 + (3 * GELU_B) * sq)
        gp[:, j : j + NB] = slope.astype(BF16)


def proj_forward(h_mid, g, wpt, vec, h_out):
    for j in range(0, D, NB):
        r = mm(g[...], wpt[j : j + NB, :], NT)
        h_out[:, j : j + NB] = h_mid[:, j : j + NB] + r + vec[7:8, j : j + NB]


def norm_backward(dout, x, gain, base, store):
    sums = [jnp.zeros((8, x.shape[1]), F32) for _ in range(3)]
    for i in range(0, x.shape[0], LN_ROWS):
        rows = slice(i, i + LN_ROWS)
        xhat, inv = norm_stats(x[rows, :].astype(F32))
        d = dout[rows, :]
        sums[0] += fold(d * xhat)
        sums[1] += fold(d)
        dx = d * gain
        m1 = jnp.mean(dx, -1, keepdims=True)
        m2 = jnp.mean(dx * xhat, -1, keepdims=True)
        total = base[rows, :] + inv * (dx - m1 - xhat * m2)
        sums[2] += fold(total)
        store(rows, total)
    return [colsum(x) for x in sums]


def ffn_backward(
    dy, h_mid, gp, wfc, wpt, vec, dy_low, df_low, dfb, dh_mid, dh_low, dvec, dc, use=None, done=None
):
    use = use or (lambda which, j=0: None)
    done = done or (lambda which: None)
    d_out = dy[...]
    dy_low[...] = d_out.astype(BF16)
    dvec[0:4, :] = jnp.zeros((4, D), F32)
    dvec[7:8, :] = colsum(d_out)
    for j in range(0, FF, NB):
        use("hidden", j)
        d = mm(dy_low[...], wpt[:, j : j + NB], NN)
        df = d * gp[:, j : j + NB].astype(F32)
        dfb[0:1, j : j + NB] = colsum(df)
        df_low[:, j : j + NB] = df.astype(BF16)
    done("df")
    for j in range(0, D, NB):
        use("wfc", j)
        dc[:, j : j + NB] = mm(df_low[...], wfc[j : j + NB, :], NT)
    use("h_mid")

    def store(rows, total):
        dh_mid[rows, :] = total
        dh_low[rows, :] = total.astype(BF16)

    dvec[5:6, :], dvec[6:7, :], dvec[4:5, :] = norm_backward(dc, h_mid, vec[5:6, :], dy, store)


def attention_backward(
    dh_mid, dh_low, h, qkv, lse, mixed, mask, wqkv, wout, vec, dmix, dqkv, da, d_in, dvec,
    use=None, done=None,
):
    use = use or (lambda which: None)
    done = done or (lambda which: None)
    tokens = h.shape[0]
    use("wout")
    use("dh_low")
    for j in range(0, D, NB):
        dmix[:, j : j + NB] = mm(dh_low[...], wout[j : j + NB, :], NT).astype(BF16)
    use("qkv")
    use("mixed")
    use("lse")
    tile = 256
    low = lax.broadcasted_iota(jnp.int32, (tokens, 128), 1) < HEAD
    low_rows = lax.broadcasted_iota(jnp.int32, (128, tokens), 0) < HEAD
    for p in range(HEADS // 2):
        c = 128 * p
        cs = slice(c, c + 128)
        q = qkv[:, cs] * BF16(HEAD**-0.5)
        k = qkv[:, D + c : D + c + 128]
        v = qkv[:, 2 * D + c : 2 * D + c + 128]
        dm = dmix[:, cs]
        prod = dm.astype(F32) * mixed[:, cs].astype(F32)
        dm_t = dm.astype(F32).T.astype(BF16)
        q_t = q.astype(F32).T.astype(BF16)
        masks = ((low, low_rows), (~low, ~low_rows))
        deltas = [jnp.sum(jnp.where(own, prod, 0.0), -1, keepdims=True) for own, _ in masks]
        q_own = [jnp.where(own, q, BF16(0)) for own, _ in masks]
        k_own = [jnp.where(own, k, BF16(0)) for own, _ in masks]
        dm_own = [jnp.where(own, dm, BF16(0)) for own, _ in masks]
        dm_t_own = [jnp.where(own, dm_t, BF16(0)) for _, own in masks]
        q_t_own = [jnp.where(own, q_t, BF16(0)) for _, own in masks]
        dq, dk_t, dv_t = [], [], []
        for i in range(tokens // tile):
            rows, seen = slice(i * tile, (i + 1) * tile), (i + 1) * tile
            scores = [mm(x[rows], k[0:seen], NT) + mask[rows, 0:seen] for x in q_own]
            probs = [jnp.exp(x - lse[rows, 2 * p + n : 2 * p + n + 1]) for n, x in enumerate(scores)]
            dps = [mm(x[rows], v[0:seen], NT) for x in dm_own]
            ds = [(x * (y - z[rows])).astype(BF16) for x, y, z in zip(probs, dps, deltas)]
            dv_t.append(sum(mm(x[:, rows], y.astype(BF16), NN) for x, y in zip(dm_t_own, probs)))
            dk_t.append(sum(mm(x[:, rows], y, NN) for x, y in zip(q_t_own, ds)))
            dq.append(sum(mm(x, y[0:seen], NN) for x, y in zip(ds, k_own)))

        def joined(parts):
            cols = []
            for n in range(len(parts)):
                cols.append(sum(part[:, n * tile : (n + 1) * tile] for part in parts[n:]))
            return jnp.concatenate(cols, 1)

        dq = jnp.concatenate(dq, 0) * HEAD**-0.5
        dv = joined(dv_t).T
        dk = joined(dk_t).T
        dvec[2:3, cs] = colsum(dq)
        dvec[3:4, cs] = colsum(dv)
        dqkv[:, cs] = dq.astype(BF16)
        dqkv[:, D + c : D + c + 128] = dk.astype(BF16)
        dqkv[:, 2 * D + c : 2 * D + c + 128] = dv.astype(BF16)
    done("dqkv")
    use("wqkv")
    for j in range(0, D, NB):
        da[:, j : j + NB] = mm(dqkv[...], wqkv[j : j + NB, :], NT)
    use("h")
    use("dh_mid")

    def store(rows, total):
        d_in[rows, :] = total

    dvec[0:1, :], dvec[1:2, :], _ = norm_backward(da, h, vec[0:1, :], dh_mid, store)
    dvec[4:8, :] = jnp.zeros((4, D), F32)


def attention_outs(t):
    return [
        like((t, D), BF16),
        like((t, 3 * D), BF16),
        like((t, 128), F32),
        like((t, D), BF16),
        like((t, D), F32),
    ]


def attention_forward_call(ends, h, wqkv, wout, vec):
    t = h.shape[0]

    def body(ends, h, wqkv, wout, vec, a, qkv, lse, mixed, h_mid, mask):
        fill_mask(ends, mask)
        attention_forward(h, wqkv, wout, vec, mask, a, qkv, lse, mixed, h_mid)

    specs = [SM, VM, VM, VM, VM]
    return kernel_call(body, attention_outs(t), specs, [pltpu.VMEM((t, t), F32)], us=13)(
        ends, h, wqkv, wout, vec
    )


def ffn_backward_call(dy, h_mid, gp, wfc, wpt, vec):
    t = dy.shape[0]
    outs = [
        like((t, FF), BF16),
        like((1, FF), F32),
        like((t, D), F32),
        like((t, D), BF16),
        like((8, D), F32),
    ]

    def body(dy, h_mid, gp, wfc, wpt, vec, df_low, dfb, dh_mid, dh_low, dvec, dy_low, dc):
        ffn_backward(dy, h_mid, gp, wfc, wpt, vec, dy_low, df_low, dfb, dh_mid, dh_low, dvec, dc)

    scratch = [pltpu.VMEM((t, D), BF16), pltpu.VMEM((t, D), F32)]
    return kernel_call(body, outs, [VM] * 6, scratch, us=13)(dy, h_mid, gp, wfc, wpt, vec)


def attention_backward_call(ends, dh_mid, dh_low, h, qkv, lse, mixed, wqkv, wout, vec):
    t = h.shape[0]

    def body(
        ends, dh_mid, dh_low, h, qkv, lse, mixed, wqkv, wout, vec, dqkv, d_in, dvec, mask, dmix, da
    ):
        fill_mask(ends, mask)
        attention_backward(
            dh_mid, dh_low, h, qkv, lse, mixed, mask, wqkv, wout, vec, dmix, dqkv, da, d_in, dvec
        )

    outs = [like((t, 3 * D), BF16), like((t, D), F32), like((8, D), F32)]
    scratch = [pltpu.VMEM((t, t), F32), pltpu.VMEM((t, D), BF16), pltpu.VMEM((t, D), F32)]
    return kernel_call(body, outs, [SM] + [VM] * 9, scratch, us=18)(
        ends, dh_mid, dh_low, h, qkv, lse, mixed, wqkv, wout, vec
    )


class Cube:
    def __init__(self, groups, rows):
        self.groups, self.rows = groups, rows
        self.n = groups * rows
        self.bits = self.n.bit_length() - 1
        far = list(range(self.bits - 1, 2, -1))
        self.gather_plans = (far + [2, 1], far + [1, 2])
        self.scatter_plans = tuple(list(reversed(p)) for p in self.gather_plans)
        self.half = self.n // 2

    def swap(self, x, plans, step):
        pairs = [(i, i ^ (1 << plans[i & 1][step])) for i in range(self.n)]
        return lax.ppermute(x, BOTH, pairs)

    def swap_core(self, x):
        return lax.ppermute(x, BOTH, [(i, i ^ 1) for i in range(self.n)])

    def gather_swap(self, held, step):
        return self.swap(held, self.gather_plans, step)

    def gather_steps(self, held, first, end):
        for step in range(first, end):
            held = jnp.concatenate([held, self.gather_swap(held, step)], 0)
        return held

    def scatter_swap(self, halves, step):
        return self.swap(halves[1], self.scatter_plans, step)

    def scatter_add(self, keep, got):
        mid = keep.shape[0] // 2
        if mid == 0:
            return (keep + got)[0]
        return keep[:mid] + got[:mid], keep[mid:] + got[mid:]

    def scatter_steps(self, halves, first, end):
        for step in range(first, end):
            halves = self.scatter_add(halves[0], self.scatter_swap(halves, step))
        return halves

    def gather_source(self, me, side, slot):
        core = (me & 1) ^ side
        dest = me ^ side
        for k in range(self.bits - 1):
            if (slot >> k) & 1:
                flip0, flip1 = 1 << self.gather_plans[0][k], 1 << self.gather_plans[1][k]
                dest = dest ^ jnp.where(core == 1, flip1, flip0)
        return dest

    def scatter_slot(self, me, dest):
        rel = me ^ dest
        core = dest & 1
        slot = 0
        for k in range(self.bits - 1):
            place = self.bits - 2 - k
            b0 = (rel >> self.scatter_plans[0][k]) & 1
            b1 = (rel >> self.scatter_plans[1][k]) & 1
            slot = slot + (jnp.where(core == 1, b1, b0) << place)
        return slot

    def row_of(self, me, side, pair):
        return 2 * pair + ((me & 1) ^ side)


lock = lax.optimization_barrier


def my_number(cube):
    return lax.axis_index("grp") * cube.rows + lax.axis_index("row")


def canonical(cube, pieces):
    me = my_number(cube)
    ids = [cube.gather_source(me, side, s) for side in (0, 1) for s in range(cube.half)]
    blocks = jnp.concatenate(pieces, 0)
    return jnp.zeros_like(blocks).at[jnp.stack(ids)].set(blocks)


def fits(rows, cols):
    return rows % 16 == 0 and cols % 128 == 0


def place_blocks(cube, pieces, sem, target):
    me = my_number(cube)
    part = cube.half // 2
    copies = []
    for i, piece in enumerate(pieces):
        for s in range(part):
            dev = cube.gather_source(me, i // 2, (i % 2) * part + s)
            copies.append(
                pltpu.make_async_copy(piece.at[s], target(dev // cube.rows, dev % cube.rows), sem)
            )
    for cp in copies:
        cp.start()

    def wait():
        for cp in copies:
            cp.wait()

    return wait


def fc_full(cube, pieces):
    br, bc = pieces[0].shape[1:]
    full = canonical(cube, pieces).reshape(cube.groups, cube.rows, br, bc)
    return full.transpose(1, 2, 0, 3).reshape(cube.rows * br, cube.groups * bc)


def proj_full(cube, pieces):
    br, bc = pieces[0].shape[1:]
    full = canonical(cube, pieces).reshape(cube.groups, cube.rows, br, bc)
    return full.transpose(0, 2, 1, 3).reshape(cube.groups * br, cube.rows * bc)


def attn_full(cube, pieces, sizes):
    bq, bo, rows_w, vrows, vcols, bias = sizes
    g_n, r_n = cube.groups, cube.rows
    br, bc = pieces[0].shape[1:]
    full = canonical(cube, pieces).reshape(g_n, r_n, br, bc)
    wide = full[:, :, :rows_w]
    wqkv = wide[..., :bq].transpose(1, 2, 0, 3).reshape(r_n * rows_w, g_n * bq)
    wout = wide[..., bq : bq + bo].transpose(1, 2, 0, 3).reshape(r_n * rows_w, g_n * bo)
    ext = full[:, :, rows_w:].astype(F32)
    vec = ext[:, :, :vrows, :vcols].transpose(1, 2, 0, 3).reshape(r_n * vrows, g_n * vcols)
    fb = ext[:, :, vrows, :bias].reshape(1, g_n * r_n * bias)
    total = jnp.sum(ext[:, :, vrows + 1, 0]) * 16.0 + jnp.sum(ext[:, :, vrows + 1, 1])
    return wqkv, wout, vec, fb, jnp.full((8, 128), total, F32)


def split_attn(cube, sizes, br, blk, wqkv, wout, vec, fb, tot):
    bq, bo, rows_w, vrows, vcols, bias = sizes
    count = jnp.zeros((1, 128), F32)
    for g in range(cube.groups):
        for r in range(cube.rows):
            rows = slice(r * rows_w, (r + 1) * rows_w)
            wqkv[rows, g * bq : (g + 1) * bq] = blk[g, r * br : r * br + rows_w, 0:bq]
            wout[rows, g * bo : (g + 1) * bo] = blk[g, r * br : r * br + rows_w, bq : bq + bo]
            ext = blk[g, r * br + rows_w : r * br + rows_w + EXTRA, :].astype(F32)
            vec[r * vrows : (r + 1) * vrows, g * vcols : (g + 1) * vcols] = ext[0:vrows, 0:vcols]
            at = (g * cube.rows + r) * bias
            fb[0:1, at : at + bias] = ext[vrows : vrows + 1, 0:bias]
            count += ext[vrows + 1 : vrows + 2, 0:128]
    lane = lax.broadcasted_iota(jnp.int32, (1, 128), 1)
    weight = jnp.where(lane == 0, 16.0, jnp.where(lane == 1, 1.0, 0.0))
    tot[...] = jnp.broadcast_to(jnp.sum(count * weight, -1, keepdims=True), (8, 128))


def open_attention(cube, ends, h, pieces, sizes):
    br, bc = pieces[0].shape[1:]
    if not fits(br, bc):
        full = attn_full(cube, pieces, sizes)
        return full, attention_forward_call(ends, h, *full[:3])
    bq, bo, rows_w, vrows, vcols, bias = sizes
    g_n, r_n = cube.groups, cube.rows
    t = h.shape[0]

    def body(ends, h, p0, p1, p2, p3, wqkv, wout, vec, fb, tot, a, qkv, lse, mixed, mid, mask, blk, sem):
        def target(g, r):
            return blk.at[g, pl.ds(pl.multiple_of(r * br, 16), br)]

        wait = place_blocks(cube, (p0, p1, p2, p3), sem, target)
        fill_mask(ends, mask)
        wait()
        split_attn(cube, sizes, br, blk, wqkv.ref, wout.ref, vec, fb, tot)
        wqkv.flush()
        wout.flush()
        whole = {"qkv": (a, qkv), "mixed": (mixed,)}
        attention_forward(
            h, wqkv.ref, wout.ref, vec, mask, a.ref, qkv.ref, lse, mixed.ref, mid,
            done=lambda which: [x.flush() for x in whole[which]],
        )

    outs = [
        ((r_n * rows_w, g_n * bq), BF16, "flush"),
        ((r_n * rows_w, g_n * bo), BF16, "flush"),
        ((r_n * vrows, g_n * vcols), F32, "vmem"),
        ((1, g_n * r_n * bias), F32, "vmem"),
        ((8, 128), F32, "vmem"),
        ((t, D), BF16, "flush"),
        ((t, 3 * D), BF16, "flush"),
        ((t, 128), F32, "vmem"),
        ((t, D), BF16, "flush"),
        ((t, D), F32, "vmem"),
    ]
    scratch = [
        pltpu.VMEM((t, t), F32),
        pltpu.VMEM((g_n, r_n * br, bc), BF16),
        pltpu.SemaphoreType.DMA,
    ]
    ins = [(ends, "smem"), (h, "vmem")] + [(x, "any") for x in pieces]
    got = staged_call(body, ins, outs, scratch, us=15)
    return got[:5], got[5:]


def open_fc(cube, mid, pieces, vec, fb):
    br, bc = pieces[0].shape[1:]
    t = mid.shape[0]
    if not fits(br, bc):
        wfc = fc_full(cube, pieces)
        outs = [like((t, D), BF16), like((t, FF), BF16), like((t, FF), BF16)]
        return wfc, kernel_call(fc_forward, outs, [VM] * 4, us=8)(mid, wfc, vec, fb)

    def body(mid, p0, p1, p2, p3, vec, fb, wfc, c, g, gp, sem):
        def target(g, r):
            rows, cols = pl.multiple_of(r * br, 16), pl.multiple_of(g * bc, 128)
            return wfc.ref.at[pl.ds(rows, br), pl.ds(cols, bc)]

        place_blocks(cube, (p0, p1, p2, p3), sem, target)()
        wfc.flush()
        fc_forward(mid, wfc.ref, vec, fb, c, g, gp)

    ins = [(mid, "vmem")] + [(x, "any") for x in pieces] + [(vec, "vmem"), (fb, "vmem")]
    outs = [
        ((cube.rows * br, cube.groups * bc), BF16, "flush"),
        ((t, D), BF16, "vmem"),
        ((t, FF), BF16, "vmem"),
        ((t, FF), BF16, "vmem"),
    ]
    got = staged_call(body, ins, outs, [pltpu.SemaphoreType.DMA], us=11)
    return got[0], got[1:]


def second_pass(cube, ends, passes, mid0, g0, pieces, cot, wqkv, wout, wfc, vec, fb):
    br, bc = pieces[0].shape[1:]
    t = cot.shape[0]
    whole = fits(br, bc)
    if not whole:
        pieces = (proj_full(cube, pieces),)
    n_p = len(pieces)

    def body(*refs):
        ends, passes, mid0, g0 = refs[:4]
        src = refs[4 : 4 + n_p]
        cot, wqkv, wout, wfc, vec, fb = refs[4 + n_p : 10 + n_p]
        wpt, h1, hidden, d1, a, mixed, c, dqkv, dhl, df, dvec, dfb = refs[10 + n_p : 22 + n_p]
        grad0, grad1 = refs[22 + n_p : 24 + n_p]
        mask, qkv, lse, mid, g, gp, dy, dyl, tmp, dhm, dmix, dvec2, dyt, grad, sem = refs[24 + n_p :]
        me = my_number(cube)

        def target(g, r):
            rows, cols = pl.multiple_of(g * br, 16), pl.multiple_of(r * bc, 128)
            return wpt.ref.at[pl.ds(rows, br), pl.ds(cols, bc)]

        if whole:
            wait = place_blocks(cube, src, sem, target)
        else:
            copy = pltpu.make_async_copy(src[0], wpt.ref, sem)
            copy.start()
            wait = copy.wait
        for x in (vec, fb, g0, mid0):
            x.start()
        vec, fb = vec.get(), fb.get()
        fill_mask(ends, mask)
        wait()
        g0.get()
        mid0.get()
        wqkv.start()
        wout.start()
        proj_forward(mid0.ref, g0.ref, wpt.ref, vec, h1.ref)
        wqkv.get()
        wout.get()
        wfc.start()
        cot.start()
        attention_forward(
            h1.ref, wqkv.ref, wout.ref, vec, mask, a.ref, qkv, lse, mixed.ref, mid,
            done=lambda which: {"qkv": a, "mixed": mixed}[which].flush(),
        )
        wfc.get()
        wpt.flush()
        h1.flush()
        fc_forward(mid, wfc.ref, vec, fb, c.ref, g, gp)
        c.flush()
        proj_forward(mid, g, wpt.ref, vec, dy)
        active = passes[0] > 1
        hidden.ref[...] = jnp.where(active, dy[...], h1.ref[...]).astype(BF16)
        hidden.flush()
        valid = lax.broadcasted_iota(jnp.int32, (t, 1), 0) < ends[0, ends.shape[1] - 1]
        cot.get()
        dy[...] = jnp.where(valid & active, cot.ref[...].astype(F32), 0.0)
        ffn_backward(
            dy, mid, gp, wfc.ref, wpt.ref, vec, dyl, df.ref, dfb.ref, dhm, dhl.ref, dvec2, tmp,
            done=lambda which: df.flush(),
        )
        dhl.flush()
        attention_backward(
            dhm, dhl.ref, h1.ref, qkv, lse, mixed.ref, mask, wqkv.ref, wout.ref, vec,
            dmix, dqkv.ref, tmp, dy, dvec.ref, done=lambda which: dqkv.flush(),
        )
        dvec.ref[...] += dvec2[...]
        dvec.flush()
        dfb.flush()
        d1.ref[...] = jnp.where(active, dy[...], jnp.where(valid, cot.ref[...].astype(F32), 0.0))
        d1.flush()
        dyt[:, 0:t] = dyl[...].astype(F32).T.astype(BF16)
        dyt[:, t : 2 * t] = d1.ref[...].T.astype(BF16)
        if not whole:
            grad0[...] = mm(dyt[:, 0:t], g[...], NN) + mm(dyt[:, t : 2 * t], g0.ref[...], NN)
            return
        n = 0
        for side, out in ((1, grad1), (0, grad0)):
            for pair in range(cube.rows // 2):
                r = cube.row_of(me, side, pair)
                cols = pl.ds(pl.multiple_of(r * bc, 128), bc)
                both = mm(dyt[:, 0:t], g[:, cols], NN) + mm(dyt[:, t : 2 * t], g0.ref[:, cols], NN)
                grad[:, n * bc : (n + 1) * bc] = both.astype(BF16)
                for group in range(cube.groups):
                    block = grad.at[pl.ds(group * br, br), pl.ds(n * bc, bc)]
                    out.put(block, cube.scatter_slot(me, group * cube.rows + r))
                n += 1

    ins = [(ends, "smem"), (passes, "smem"), (mid0, "fetch"), (g0, "fetch")]
    ins += [(x, "any") for x in pieces]
    ins += [(x, "fetch") for x in (cot, wqkv, wout, wfc, vec, fb)]
    outs = [
        ((D, FF), BF16, "flush"),
        ((t, D), F32, "flush"),
        ((t, D), BF16, "flush"),
        ((t, D), F32, "flush"),
        ((t, D), BF16, "flush"),
        ((t, D), BF16, "flush"),
        ((t, D), BF16, "flush"),
        ((t, 3 * D), BF16, "flush"),
        ((t, D), BF16, "flush"),
        ((t, FF), BF16, "flush"),
        ((8, D), F32, "flush"),
        ((1, FF), F32, "flush"),
    ]
    if whole:
        outs += [((cube.half, br, bc), BF16, "sink", cube.half)] * 2
    else:
        outs += [((D, FF), F32, "vmem"), ((8, 128), F32, "vmem")]
    scratch = [
        pltpu.VMEM((t, t), F32),
        pltpu.VMEM((t, 3 * D), BF16),
        pltpu.VMEM((t, 128), F32),
        pltpu.VMEM((t, D), F32),
        pltpu.VMEM((t, FF), BF16),
        pltpu.VMEM((t, FF), BF16),
        pltpu.VMEM((t, D), F32),
        pltpu.VMEM((t, D), BF16),
        pltpu.VMEM((t, D), F32),
        pltpu.VMEM((t, D), F32),
        pltpu.VMEM((t, D), BF16),
        pltpu.VMEM((8, D), F32),
        pltpu.VMEM((D, 2 * t), BF16),
        pltpu.VMEM((D, FF), BF16),
        pltpu.SemaphoreType.DMA,
    ]
    got = staged_call(body, ins, outs, scratch, us=50)
    slots = got[12:]
    if not whole:
        full = slots[0].astype(BF16).reshape(cube.groups, br, cube.rows, bc).transpose(0, 2, 1, 3)
        slots = ordered_slots(cube, full.reshape(cube.n, br, bc))
    return got[:12], slots


def pack_attn(w_qkv, w_out, vectors, fc_bias, seg_ends):
    rows_w, bq = w_qkv.shape
    bo = w_out.shape[1]
    vrows, vcols = vectors.shape
    bias = fc_bias.shape[0]
    wide = bq + bo

    def body(wq, wo, vec, fb, ends, out):
        out[0:rows_w, 0:bq] = wq[...]
        out[0:rows_w, bq:wide] = wo[...]
        n_valid = ends[0, ends.shape[1] - 1]
        lane = lax.broadcasted_iota(jnp.int32, (1, wide), 1)
        n_high = n_valid // 16
        count = jnp.where(lane == 0, n_high, jnp.where(lane == 1, n_valid - 16 * n_high, 0))
        ext = jnp.concatenate(
            [
                jnp.concatenate([vec[...].astype(F32), jnp.zeros((vrows, wide - vcols), F32)], 1),
                jnp.concatenate([fb[...].astype(F32), jnp.zeros((1, wide - bias), F32)], 1),
                count.astype(F32),
                jnp.zeros((EXTRA - vrows - 2, wide), F32),
            ],
            0,
        )
        out[rows_w : rows_w + EXTRA, :] = ext.astype(BF16)

    outs = [like((rows_w + EXTRA, wide), BF16)]
    return kernel_call(body, outs, [VM] * 4 + [SM], us=2)(
        w_qkv, w_out, vectors, fc_bias[None], seg_ends
    )[0]


def ordered_slots(cube, blocks):
    me = my_number(cube)
    order = [cube.scatter_slot(me, dest) + cube.half * ((me ^ dest) & 1) for dest in range(cube.n)]
    slots = jnp.zeros_like(blocks).at[jnp.stack(order)].set(blocks)
    return slots[: cube.half], slots[cube.half :]


def stacked_t(parts, out):
    t = parts[0].shape[0]
    for i, part in enumerate(parts):
        out[:, i * t : (i + 1) * t] = part[...].astype(F32).T.astype(BF16)


def ffn_backward_and_grad(cube, dy, h_mid, gp, wfc, wpt, vec, c1, c0, df1, br, bc):
    t = dy.shape[0]
    if not fits(br, bc):
        df0, *rest = ffn_backward_call(dy, h_mid, gp, wfc, wpt, vec)
        full = mm(c1, df1, TN) + mm(c0, df0, TN)
        full = full.astype(BF16).reshape(cube.rows, br, cube.groups, bc).transpose(2, 0, 1, 3)
        return rest, ordered_slots(cube, full.reshape(cube.n, br, bc))

    def body(
        dy, h_mid, gp, wfc, wpt, vec, c1, c0, df1, dfb, dh_mid, dh_low, dvec, keep, send,
        dy_low, dc, df0, ct, grad,
    ):
        me = my_number(cube)
        order = {"dy": dy, "wpt": wpt, "gp": gp, "wfc": wfc, "h_mid": h_mid}
        for x in (*order.values(), vec, c1, c0, df1):
            x.start()

        def use(which, j=0):
            if which == "hidden":
                if j == 0:
                    wpt.get()
                gp.get(j // (FF // 4) + 1)
            else:
                order[which].get()
                vec.get()

        ffn_backward(
            dy.get(), h_mid.ref, gp.ref, wfc.ref, wpt.ref, vec.ref, dy_low, df0, dfb.ref, dh_mid.ref, dh_low.ref,
            dvec.ref, dc, use=use,
        )
        for x in (dh_mid, dh_low, dvec, dfb):
            x.flush()
        stacked_t((c1.get(), c0.get()), ct)
        df1.get()
        for first in range(0, cube.groups, 2):
            cols = slice(first * bc, (first + 2) * bc)
            both = mm(ct[:, 0:t], df1.ref[:, cols], NN) + mm(ct[:, t : 2 * t], df0[:, cols], NN)
            grad[:, cols] = both.astype(BF16)
            for side, out in ((1, send), (0, keep)):
                for g in (first, first + 1):
                    for pair in range(cube.rows // 2):
                        r = cube.row_of(me, side, pair)
                        rows = pl.ds(pl.multiple_of(r * br, 16), br)
                        block = grad.at[rows, pl.ds(g * bc, bc)]
                        out.put(block, cube.scatter_slot(me, g * cube.rows + r))

    ins = [
        (dy, "fetch"), (h_mid, "fetch"), (gp, "fetch", 1, 4), (wfc, "fetch"), (wpt, "fetch"), (vec, "fetch"),
        (c1, "fetch"), (c0, "fetch"), (df1, "fetch"),
    ]
    outs = [
        ((1, FF), F32, "flush"),
        ((t, D), F32, "flush"),
        ((t, D), BF16, "flush"),
        ((8, D), F32, "flush"),
        ((cube.half, br, bc), BF16, "sink", cube.half),
        ((cube.half, br, bc), BF16, "sink", cube.half),
    ]
    scratch = [
        pltpu.VMEM((t, D), BF16),
        pltpu.VMEM((t, D), F32),
        pltpu.VMEM((t, FF), BF16),
        pltpu.VMEM((D, 2 * t), BF16),
        pltpu.VMEM((D, FF), BF16),
    ]
    got = staged_call(body, ins, outs, scratch, us=15)
    return got[:4], got[4:]


def attention_backward_and_grad(
    cube, ends, dh_mid, dh0, h, qkv, lse, m0, wqkv, wout, vec, a1, a0, dq1, m1, dh1, dvecs, dfbs, sizes, br, bc
):
    bq, bo, rows_w, vrows, vcols, bias = sizes
    g_n, r_n = cube.groups, cube.rows
    t = h.shape[0]
    if not fits(br, bc):
        dq0, d_in, dvec = attention_backward_call(ends, dh_mid, dh0, h, qkv, lse, m0, wqkv, wout, vec)
        dvec, dfb = dvec + dvecs[0] + dvecs[1], dfbs[0] + dfbs[1]
        dqkv = mm(a1, dq1, TN) + mm(a0, dq0, TN)
        dout = mm(m1, dh1, TN) + mm(m0, dh0, TN)
        wide = jnp.concatenate(
            [dqkv.reshape(r_n, rows_w, g_n, bq), dout.reshape(r_n, rows_w, g_n, bo)], -1
        ).transpose(2, 0, 1, 3)
        vecs = dvec.reshape(r_n, vrows, g_n, vcols).transpose(2, 0, 1, 3)
        biases = dfb.reshape(g_n, r_n, 1, bias)
        ext = jnp.zeros((g_n, r_n, EXTRA, bc), F32)
        ext = ext.at[:, :, :vrows, :vcols].set(vecs).at[:, :, vrows : vrows + 1, :bias].set(biases)
        full = jnp.concatenate([wide, ext], 2).astype(BF16)
        return d_in, ordered_slots(cube, full.reshape(cube.n, br, bc))

    def body(
        ends, dh_mid, dh0, h, qkv, lse, m0, wqkv, wout, vec, a1, a0, dq1, m1, dh1, dvec1, dvec0, dfb1, dfb0,
        d_in, keep, send, mask, dmix, dq0, da, dvec, dfb, lt, wide, blocks,
    ):
        me = my_number(cube)
        waits = {
            "dh_low": dh0, "wout": wout, "qkv": qkv, "mixed": m0, "lse": lse, "wqkv": wqkv, "h": h,
            "dh_mid": dh_mid,
        }
        for x in (*waits.values(), vec, m1, dh1, a1, a0, dq1, dvec1, dvec0, dfb1, dfb0):
            x.start()
        fill_mask(ends, mask)
        attention_backward(
            dh_mid.ref, dh0.ref, h.ref, qkv.ref, lse.ref, m0.ref, mask, wqkv.ref, wout.ref, vec.get(),
            dmix, dq0, da, d_in.ref, dvec, use=lambda which: waits[which].get(),
        )
        d_in.flush()
        dvec[...] += dvec1.get()[...] + dvec0.get()[...]
        dfb[...] = dfb1.get()[...] + dfb0.get()[...]
        stacked_t((m1.get(), m0.ref), lt)
        dh1.get()
        for j in range(0, D, NB):
            cols = slice(j, j + NB)
            full = mm(lt[:, 0:t], dh1.ref[:, cols], NN) + mm(lt[:, t : 2 * t], dh0.ref[:, cols], NN)
            wide[:, 3 * D + j : 3 * D + j + NB] = full.astype(BF16)
        stacked_t((a1.get(), a0.get()), lt)
        dq1.get()
        for j in range(0, 3 * D, NB):
            cols = slice(j, j + NB)
            full = mm(lt[:, 0:t], dq1.ref[:, cols], NN) + mm(lt[:, t : 2 * t], dq0[:, cols], NN)
            wide[:, cols] = full.astype(BF16)

        def extra(g, r):
            vecs = dvec[r * vrows : (r + 1) * vrows, g * vcols : (g + 1) * vcols]
            at = (g * r_n + r) * bias
            return jnp.concatenate(
                [
                    jnp.concatenate([vecs, jnp.zeros((vrows, bc - vcols), F32)], 1),
                    jnp.concatenate([dfb[0:1, at : at + bias], jnp.zeros((1, bc - bias), F32)], 1),
                    jnp.zeros((EXTRA - vrows - 1, bc), F32),
                ],
                0,
            )

        for g in range(g_n):
            for r in range(r_n):
                rows = slice(r * rows_w, (r + 1) * rows_w)
                o = 3 * D + g * bo
                blocks[g * r_n + r, 0:rows_w, 0:bq] = wide[rows, g * bq : (g + 1) * bq]
                blocks[g * r_n + r, 0:rows_w, bq : bq + bo] = wide[rows, o : o + bo]
                blocks[g * r_n + r, rows_w : rows_w + EXTRA, :] = extra(g, r).astype(BF16)
            for side, out in ((1, send), (0, keep)):
                for pair in range(r_n // 2):
                    dest = g * r_n + cube.row_of(me, side, pair)
                    out.put(blocks.at[dest], cube.scatter_slot(me, dest))

    ins = [(ends, "smem")] + [(x, "fetch") for x in (dh_mid, dh0, h, qkv, lse, m0, wqkv, wout)]
    ins += [(x, "fetch") for x in (vec, a1, a0, dq1, m1, dh1, *dvecs, *dfbs)]
    outs = [((t, D), F32, "flush")] + [((cube.half, br, bc), BF16, "sink", cube.half)] * 2
    scratch = [
        pltpu.VMEM((t, t), F32),
        pltpu.VMEM((t, D), BF16),
        pltpu.VMEM((t, 3 * D), BF16),
        pltpu.VMEM((t, D), F32),
        pltpu.VMEM((8, D), F32),
        pltpu.VMEM((1, FF), F32),
        pltpu.VMEM((D, 2 * t), BF16),
        pltpu.VMEM((D, 4 * D), BF16),
        pltpu.VMEM((cube.n, br, bc), BF16),
    ]
    got = staged_call(body, ins, outs, scratch, us=20)
    return got[0], got[1:]


def adam_update(weight, first, second, grad, keep_frac):
    t_step = float(STEP)
    first_new = 0.9 * first * keep_frac + 0.1 * grad
    second_new = 0.95 * second * keep_frac + 0.05 * grad * grad
    first_hat = first_new / (1.0 - 0.9**t_step)
    second_hat = second_new / (1.0 - 0.95**t_step)
    weight_new = weight.astype(F32) * (1.0 - LEARN_RATE * WEIGHT_DECAY) - LEARN_RATE * first_hat / (
        jnp.sqrt(second_hat) + 1e-08
    )
    return (weight_new.astype(BF16), first_new, second_new)


def body(
    hidden_in,
    cotangent,
    w_qkv,
    w_out,
    w_fc,
    w_proj,
    vectors,
    fc_bias,
    first_qkv,
    first_out,
    first_fc,
    first_proj,
    first_vectors,
    first_fc_bias,
    second_qkv,
    second_out,
    second_fc,
    second_proj,
    second_vectors,
    second_fc_bias,
    seg_ends,
    pass_counts,
    reset_flag,
):
    cube = Cube(lax.axis_size("grp"), lax.axis_size("row"))
    rows_w, bq = w_qkv.shape
    bo = w_out.shape[1]
    vrows, vcols = vectors.shape
    bias = fc_bias.shape[0]
    sizes = (bq, bo, rows_w, vrows, vcols, bias)
    wide = bq + bo

    far = cube.bits - 3
    near, last = far, far + 1
    join = lambda x, y: jnp.concatenate([x, y], 0)
    a = cube.gather_steps(pack_attn(w_qkv, w_out, vectors, fc_bias, seg_ends)[None], 0, far)

    a, f = lock((a, w_fc[None]))
    got, f = lock((cube.gather_swap(a, near), cube.gather_steps(f, 0, 1)))
    a = join(a, got)

    a, f, p = lock((a, f, w_proj.T[None]))
    last_a, f, p = lock(
        (cube.gather_swap(a, last), cube.gather_steps(f, 1, far), cube.gather_steps(p, 0, 1))
    )

    core_a0, core_a1, got, p = lock(
        (
            cube.swap_core(a),
            cube.swap_core(last_a),
            cube.gather_swap(f, near),
            cube.gather_steps(p, 1, far),
        )
    )
    f = join(f, got)

    h0, f, p = lock((hidden_in, f, p))
    full, acts = open_attention(cube, seg_ends, h0, (a, last_a, core_a0, core_a1), sizes)
    full, acts, last_f, core_f0, got = lock(
        (full, acts, cube.gather_swap(f, last), cube.swap_core(f), cube.gather_swap(p, near))
    )
    wqkv, wout, vec, fb, tot = full
    a0, qkv0, lse0, mixed0, mid0 = acts
    p = join(p, got)

    core_f1 = cube.swap_core(last_f)
    core_f1, p = lock((core_f1, p))
    wfc, (c0, g0, gp0) = open_fc(cube, mid0, (f, last_f, core_f0, core_f1), vec, fb)
    c0, g0, gp0, wfc, last_p, core_p0 = lock(
        (c0, g0, gp0, wfc, cube.gather_swap(p, last), cube.swap_core(p))
    )
    core_p1 = cube.swap_core(last_p)
    made, slots = second_pass(
        cube, seg_ends, pass_counts, mid0, g0, (p, last_p, core_p0, core_p1), cotangent, wqkv, wout, wfc, vec, fb
    )
    wpt, h1, hidden, d1, a1, mixed1, c1, dqkv1, dhl1, dfl1, dvec1, dfb1 = made
    keep_p, send_p = slots
    total = tot[0, 0]
    end = cube.bits - 1

    p = cube.scatter_add(keep_p, cube.swap_core(send_p))

    d1, p = lock((d1, p))
    back, slots = ffn_backward_and_grad(cube, d1, mid0, gp0, wfc, wpt, vec, c1, c0, dfl1, *w_fc.shape)
    back, slots, got = lock((back, slots, cube.scatter_swap(p, 0)))
    dfb0, dhm0, dhl0, dvec0 = back
    p = cube.scatter_add(p[0], got)

    slots, p = lock((slots, p))
    keep_f, send_f = slots
    got_f, got = lock((cube.swap_core(send_f), cube.scatter_swap(p, 1)))
    f = cube.scatter_add(keep_f, got_f)
    p = cube.scatter_add(p[0], got)

    dhl0, f, p = lock((dhl0, f, p))
    input_grad, slots = attention_backward_and_grad(
        cube, seg_ends, dhm0, dhl0, h0, qkv0, lse0, mixed0, wqkv, wout, vec, a1, a0, dqkv1, mixed1, dhl1,
        (dvec1, dvec0), (dfb1, dfb0), sizes, rows_w + EXTRA, wide,
    )
    slots, got_f, p = lock((slots, cube.scatter_swap(f, 0), cube.scatter_steps(p, 2, 3)))
    keep_a, send_a = slots
    f = cube.scatter_add(f[0], got_f)

    send_a, f, p = lock((send_a, f, p))
    got_a, got_f, sum_p = lock(
        (cube.swap_core(send_a), cube.scatter_swap(f, 1), cube.scatter_steps(p, 3, end))
    )
    a = cube.scatter_add(keep_a, got_a)
    f = cube.scatter_add(f[0], got_f)

    a, f = lock((a, f))
    got_a, sum_f = lock((cube.scatter_swap(a, 0), cube.scatter_steps(f, 2, end)))
    a = cube.scatter_add(a[0], got_a)
    sum_a = cube.scatter_steps(a, 1, end)

    sum_a = sum_a.astype(F32)
    summed = (
        sum_a[:rows_w, :bq],
        sum_a[:rows_w, bq:],
        sum_f.astype(F32),
        sum_p.T.astype(F32),
        sum_a[rows_w : rows_w + vrows, :vcols],
        sum_a[rows_w + vrows, :bias],
    )
    grads = tuple(s / total for s in summed)
    keep_feat = 1.0 - reset_flag.astype(F32)
    keep_rows = lax.dynamic_slice_in_dim(keep_feat, lax.axis_index("row") * rows_w, rows_w)[:, None]
    keep_cols = lax.dynamic_slice_in_dim(keep_feat, lax.axis_index("grp") * vcols, vcols)[None, :]
    bias_index = (my_number(cube) * bias + jnp.arange(bias, dtype=jnp.int32)) % D
    keeps = (keep_rows, keep_rows, keep_rows, keep_cols, keep_cols, keep_feat[bias_index])
    weights = (w_qkv, w_out, w_fc, w_proj, vectors, fc_bias)
    firsts = (first_qkv, first_out, first_fc, first_proj, first_vectors, first_fc_bias)
    seconds = (second_qkv, second_out, second_fc, second_proj, second_vectors, second_fc_bias)
    updated = [
        adam_update(w, m, v, g, kp) for w, m, v, g, kp in zip(weights, firsts, seconds, grads, keeps)
    ]
    return (
        (hidden, input_grad)
        + grads
        + tuple(u[0] for u in updated)
        + tuple(u[1] for u in updated)
        + tuple(u[2] for u in updated)
    )


def solution(mesh):
    tokens = P(("grp", "row"), None)
    flat = P(("grp", "row"))
    tiles = P("row", "grp")
    six = (tiles, tiles, tiles, tiles, tiles, flat)
    return jax.shard_map(
        body,
        mesh=mesh,
        in_specs=(tokens, tokens) + six * 3 + (tokens, P("grp"), P()),
        out_specs=(tokens, tokens) + six * 4,
        check_vma=False,
    )
```

```python
import functools

import jax
import jax.numpy as jnp
from jax import lax
from jax.experimental import pallas as pl
from jax.experimental.pallas import tpu as pltpu
from jax.sharding import PartitionSpec as P

D = 768
HEADS = 12
HEAD = 64
FF = 3072
STEP = 10
LEARN_RATE = 0.03
WEIGHT_DECAY = 0.1
F32 = jnp.float32
BF16 = jnp.bfloat16
NN = (((1,), (0,)), ((), ()))
NT = (((1,), (1,)), ((), ()))
TN = (((0,), (0,)), ((), ()))
NB = 256
LN_ROWS = 32
EXTRA = 16
GELU_A = 0.7978845608028654
GELU_B = 0.044715
BOTH = ("grp", "row")

VM = pl.BlockSpec(memory_space=pltpu.VMEM)
SM = pl.BlockSpec(memory_space=pltpu.SMEM)
HB = pl.BlockSpec(memory_space=pl.ANY)


def params(mib):
    return pltpu.CompilerParams(vmem_limit_bytes=mib * 2**20)


def like(shape, dtype):
    return jax.ShapeDtypeStruct(shape, dtype)


def mm(a, b, dims):
    return lax.dot_general(a, b, dims, preferred_element_type=F32)


def kernel_call(body, outs, specs, scratch=(), us=5, mib=60):
    return pl.pallas_call(
        body,
        out_shape=outs,
        in_specs=specs,
        out_specs=[VM] * len(outs),
        scratch_shapes=list(scratch),
        compiler_params=params(mib),
        cost_estimate=pl.CostEstimate(
            flops=int(us * 1e9), bytes_accessed=int(us * 3e6), transcendentals=0
        ),
    )


class Fetched:
    def __init__(self, src, dst, sems, axis):
        self.ref, n = dst, len(sems)
        size = dst.shape[axis] // n
        self.copies, self.begun, self.waited = [], 0, 0
        for i in range(n):
            at = tuple(pl.ds(i * size, size) if d == axis else slice(None) for d in range(len(dst.shape)))
            self.copies.append(pltpu.make_async_copy(src.at[at], dst.at[at], sems[i]))

    def start(self, n=None):
        for copy in self.copies[self.begun : n]:
            copy.start()
            self.begun += 1

    def get(self, n=None):
        self.start(n)
        for copy in self.copies[self.waited : n]:
            copy.wait()
            self.waited += 1
        return self.ref


class Flushed:
    def __init__(self, dst, src, sems):
        self.dst, self.ref, self.sems, self.copies = dst, src, list(sems), []

    def flush(self, *at):
        at = at or (slice(None),)
        copy = pltpu.make_async_copy(self.ref.at[at], self.dst.at[at], self.sems[len(self.copies)])
        copy.start()
        self.copies.append(copy)

    def finish(self):
        if not self.copies:
            self.flush()
        for copy in self.copies:
            copy.wait()


class Sink:
    def __init__(self, dst, sems):
        self.dst, self.sems, self.copies = dst, list(sems), []

    def put(self, src, *at):
        copy = pltpu.make_async_copy(src, self.dst.at[at], self.sems[len(self.copies)])
        copy.start()
        self.copies.append(copy)

    def finish(self):
        for copy in self.copies:
            copy.wait()


def staged_call(body, ins, outs, scratch=(), us=5, mib=60):
    n_in, n_out = len(ins), len(outs)
    spec_of = {"smem": SM, "vmem": VM, "any": HB, "fetch": HB, "flush": HB, "sink": HB}
    fetches = [i for i, how in enumerate(ins) if how[1] == "fetch"]
    flushes = [i for i, how in enumerate(outs) if how[2] == "flush"]
    sinks = [i for i, how in enumerate(outs) if how[2] == "sink"]
    extra = [pltpu.VMEM(ins[i][0].shape, ins[i][0].dtype) for i in fetches]
    extra += [pltpu.VMEM(outs[i][0], outs[i][1]) for i in flushes]
    counts = [(ins[i] + (0, 1))[3] if len(ins[i]) > 2 else 1 for i in fetches]
    counts += [outs[i][3] if len(outs[i]) > 3 else 1 for i in flushes + sinks]
    axes = [ins[i][2] if len(ins[i]) > 2 else 0 for i in fetches]
    extra += [pltpu.SemaphoreType.DMA((max(sum(counts), 1),))]

    def run(*refs):
        given, made = list(refs[:n_in]), list(refs[n_in : n_in + n_out])
        rest = refs[n_in + n_out :]
        own, mine = rest[: len(scratch)], rest[len(scratch) :]
        buffers, sem = mine[:-1], mine[-1]
        first = 0
        for j, i in enumerate(fetches + flushes + sinks):
            sems = [sem.at[first + k] for k in range(counts[j])]
            first += counts[j]
            if j < len(fetches):
                given[i] = Fetched(given[i], buffers[j], sems, axes[j])
            elif j < len(buffers):
                made[i] = Flushed(made[i], buffers[j], sems)
            else:
                made[i] = Sink(made[i], sems)
        body(*given, *made, *own)
        for i in fetches:
            given[i].get()
        for i in flushes + sinks:
            made[i].finish()

    return pl.pallas_call(
        run,
        out_shape=[like(out[0], out[1]) for out in outs],
        in_specs=[spec_of[how[1]] for how in ins],
        out_specs=[spec_of[how[2]] for how in outs],
        scratch_shapes=list(scratch) + extra,
        compiler_params=params(mib),
        cost_estimate=pl.CostEstimate(
            flops=int(us * 1e9), bytes_accessed=int(us * 3e6), transcendentals=0
        ),
    )(*[how[0] for how in ins])


def norm_stats(x):
    centred = x - jnp.mean(x, -1, keepdims=True)
    inv = lax.rsqrt(jnp.mean(centred * centred, -1, keepdims=True) + 1e-5)
    return centred * inv, inv


def colsum(x):
    return jnp.sum(x, 0, keepdims=True)


def norm_forward(x, gain, bias, out):
    for i in range(0, x.shape[0], LN_ROWS):
        rows = slice(i, i + LN_ROWS)
        xhat, _ = norm_stats(x[rows, :].astype(F32))
        out[rows, :] = (xhat * gain + bias).astype(BF16)


def fold(x):
    return jnp.sum(x.reshape(x.shape[0] // 8, 8, x.shape[1]), 0)


def fill_mask(ends_ref, mask_ref):
    tokens = mask_ref.shape[0]
    n_ends = ends_ref.shape[1]

    def segments(pos):
        seg = jnp.zeros(pos.shape, jnp.int32)
        for e in range(n_ends):
            seg += (pos >= ends_ref[0, e]).astype(jnp.int32)
        return seg

    seg_keys = segments(lax.broadcasted_iota(jnp.int32, (1, tokens), 1))
    for i in range(0, tokens, 128):
        pos = lax.broadcasted_iota(jnp.int32, (128, 1), 0) + i
        key = lax.broadcasted_iota(jnp.int32, (128, tokens), 1)
        seen = (segments(pos) == seg_keys) & (key <= pos)
        mask_ref[i : i + 128, :] = jnp.where(seen, 0.0, -1e30)


def attention_forward(h, wqkv, vec, mask, a, qkv, lse, mixed, tile=256, done=None):
    tokens = h.shape[0]
    done = done or (lambda which: None)
    norm_forward(h, vec[0:1, :], vec[1:2, :], a)
    for part in range(3):
        for j in range(0, D, NB):
            o = part * D + j
            r = mm(a[...], wqkv[:, o : o + NB], NN)
            if part == 0:
                r = r + vec[2:3, j : j + NB]
            if part == 2:
                r = r + vec[3:4, j : j + NB]
            qkv[:, o : o + NB] = r.astype(BF16)
    done("qkv")
    lanes = lax.broadcasted_iota(jnp.int32, (tile, 128), 1)
    low = lanes < HEAD
    together = 2
    for i in range(tokens // tile):
        rows = slice(i * tile, (i + 1) * tile)
        seen = (i + 1) * tile
        logs = jnp.zeros((tile, 128), F32)
        for first in range(0, HEADS // 2, together):
            jobs = [(p, half) for p in range(first, first + together) for half in range(2)]
            scores = []
            for p, half in jobs:
                q = qkv[rows, 128 * p : 128 * p + 128] * BF16(HEAD**-0.5)
                k = qkv[0:seen, D + 128 * p : D + 128 * p + 128]
                own = low if half == 0 else ~low
                scores.append(mm(jnp.where(own, q, BF16(0)), k, NT) + mask[rows, 0:seen])
            tops = [jnp.max(x, -1, keepdims=True) for x in scores]
            expo = [jnp.exp(x - top) for x, top in zip(scores, tops)]
            dens = [jnp.sum(x, -1, keepdims=True) for x in expo]
            outs = []
            for (p, half), x, den, top in zip(jobs, expo, dens, tops):
                v = qkv[0:seen, 2 * D + 128 * p : 2 * D + 128 * p + 128]
                outs.append(mm(x.astype(BF16), v, NN) / den)
                logs = jnp.where(lanes == 2 * p + half, top + jnp.log(den), logs)
            for n, (p, half) in enumerate(jobs):
                if half == 1:
                    mixed[rows, 128 * p : 128 * p + 128] = jnp.where(low, outs[n - 1], outs[n]).astype(BF16)
        lse[rows, :] = logs
    done("mixed")


def out_forward(h, mixed, wout, vec, h_mid):
    for j in range(0, D, NB):
        r = mm(mixed[...], wout[:, j : j + NB], NN)
        h_mid[:, j : j + NB] = h[:, j : j + NB].astype(F32) + r + vec[4:5, j : j + NB]


def fc_forward(h_mid, wfc, vec, fb, c, g, gp):
    norm_forward(h_mid, vec[5:6, :], vec[6:7, :], c)
    for j in range(0, FF, NB):
        f = mm(c[...], wfc[:, j : j + NB], NN) + fb[0:1, j : j + NB]
        sq = f * f
        t = jnp.tanh(GELU_A * (f + GELU_B * sq * f))
        half = 0.5 * (1.0 + t)
        g[:, j : j + NB] = (f * half).astype(BF16)
        slope = half + (0.5 * GELU_A) * f * (1.0 - t * t) * (1.0 + (3 * GELU_B) * sq)
        gp[:, j : j + NB] = slope.astype(BF16)


def proj_forward(h_mid, g, wpt, vec, h_out):
    for j in range(0, D, NB):
        r = mm(g[...], wpt[j : j + NB, :], NT)
        h_out[:, j : j + NB] = h_mid[:, j : j + NB] + r + vec[7:8, j : j + NB]


def norm_backward(dout, x, gain, base, store):
    sums = [jnp.zeros((8, x.shape[1]), F32) for _ in range(3)]
    for i in range(0, x.shape[0], LN_ROWS):
        rows = slice(i, i + LN_ROWS)
        xhat, inv = norm_stats(x[rows, :].astype(F32))
        d = dout[rows, :]
        sums[0] += fold(d * xhat)
        sums[1] += fold(d)
        dx = d * gain
        m1 = jnp.mean(dx, -1, keepdims=True)
        m2 = jnp.mean(dx * xhat, -1, keepdims=True)
        total = base[rows, :] + inv * (dx - m1 - xhat * m2)
        sums[2] += fold(total)
        store(rows, total)
    return [colsum(x) for x in sums]


def ffn_backward(
    dy, h_mid, gp, wfc, wpt, vec, dy_low, df_low, dfb, dh_mid, dh_low, dvec, dc, use=None, done=None
):
    use = use or (lambda which, j=0: None)
    done = done or (lambda which: None)
    d_out = dy[...]
    dy_low[...] = d_out.astype(BF16)
    dvec[0:4, :] = jnp.zeros((4, D), F32)
    dvec[7:8, :] = colsum(d_out)
    for j in range(0, FF, NB):
        use("hidden", j)
        d = mm(dy_low[...], wpt[:, j : j + NB], NN)
        df = d * gp[:, j : j + NB].astype(F32)
        dfb[0:1, j : j + NB] = colsum(df)
        df_low[:, j : j + NB] = df.astype(BF16)
    done("df")
    for j in range(0, D, NB):
        use("wfc", j)
        dc[:, j : j + NB] = mm(df_low[...], wfc[j : j + NB, :], NT)
    use("h_mid")

    def store(rows, total):
        dh_mid[rows, :] = total
        dh_low[rows, :] = total.astype(BF16)

    dvec[5:6, :], dvec[6:7, :], dvec[4:5, :] = norm_backward(dc, h_mid, vec[5:6, :], dy, store)


def attention_backward(
    dh_mid, dh_low, h, qkv, lse, mixed, mask, wqkv, wout, vec, dmix, dqkv, da, d_in, dvec,
    use=None, done=None,
):
    use = use or (lambda which: None)
    done = done or (lambda which: None)
    tokens = h.shape[0]
    use("wout")
    use("dh_low")
    for j in range(0, D, NB):
        dmix[:, j : j + NB] = mm(dh_low[...], wout[j : j + NB, :], NT).astype(BF16)
    use("qkv")
    use("mixed")
    use("lse")
    tile = 256
    low = lax.broadcasted_iota(jnp.int32, (tokens, 128), 1) < HEAD
    low_rows = lax.broadcasted_iota(jnp.int32, (128, tokens), 0) < HEAD
    for p in range(HEADS // 2):
        c = 128 * p
        cs = slice(c, c + 128)
        q = qkv[:, cs] * BF16(HEAD**-0.5)
        k = qkv[:, D + c : D + c + 128]
        v = qkv[:, 2 * D + c : 2 * D + c + 128]
        dm = dmix[:, cs]
        prod = dm.astype(F32) * mixed[:, cs].astype(F32)
        dm_t = dm.astype(F32).T.astype(BF16)
        q_t = q.astype(F32).T.astype(BF16)
        masks = ((low, low_rows), (~low, ~low_rows))
        deltas = [jnp.sum(jnp.where(own, prod, 0.0), -1, keepdims=True) for own, _ in masks]
        q_own = [jnp.where(own, q, BF16(0)) for own, _ in masks]
        k_own = [jnp.where(own, k, BF16(0)) for own, _ in masks]
        dm_own = [jnp.where(own, dm, BF16(0)) for own, _ in masks]
        dm_t_own = [jnp.where(own, dm_t, BF16(0)) for _, own in masks]
        q_t_own = [jnp.where(own, q_t, BF16(0)) for _, own in masks]
        dq, dk_t, dv_t = [], [], []
        for i in range(tokens // tile):
            rows, seen = slice(i * tile, (i + 1) * tile), (i + 1) * tile
            scores = [mm(x[rows], k[0:seen], NT) + mask[rows, 0:seen] for x in q_own]
            probs = [jnp.exp(x - lse[rows, 2 * p + n : 2 * p + n + 1]) for n, x in enumerate(scores)]
            dps = [mm(x[rows], v[0:seen], NT) for x in dm_own]
            ds = [(x * (y - z[rows])).astype(BF16) for x, y, z in zip(probs, dps, deltas)]
            dv_t.append(sum(mm(x[:, rows], y.astype(BF16), NN) for x, y in zip(dm_t_own, probs)))
            dk_t.append(sum(mm(x[:, rows], y, NN) for x, y in zip(q_t_own, ds)))
            dq.append(sum(mm(x, y[0:seen], NN) for x, y in zip(ds, k_own)))

        def joined(parts):
            cols = []
            for n in range(len(parts)):
                cols.append(sum(part[:, n * tile : (n + 1) * tile] for part in parts[n:]))
            return jnp.concatenate(cols, 1)

        dq = jnp.concatenate(dq, 0) * HEAD**-0.5
        dv = joined(dv_t).T
        dk = joined(dk_t).T
        dvec[2:3, cs] = colsum(dq)
        dvec[3:4, cs] = colsum(dv)
        dqkv[:, cs] = dq.astype(BF16)
        dqkv[:, D + c : D + c + 128] = dk.astype(BF16)
        dqkv[:, 2 * D + c : 2 * D + c + 128] = dv.astype(BF16)
    done("dqkv")
    use("wqkv")
    for j in range(0, D, NB):
        da[:, j : j + NB] = mm(dqkv[...], wqkv[j : j + NB, :], NT)
    use("h")
    use("dh_mid")

    def store(rows, total):
        d_in[rows, :] = total

    dvec[0:1, :], dvec[1:2, :], _ = norm_backward(da, h, vec[0:1, :], dh_mid, store)
    dvec[4:8, :] = jnp.zeros((4, D), F32)


def attention_forward_call(ends, h, wqkv, vec):
    t = h.shape[0]
    outs = [like((t, D), BF16), like((t, 3 * D), BF16), like((t, 128), F32), like((t, D), BF16)]

    def body(ends, h, wqkv, vec, a, qkv, lse, mixed, mask):
        fill_mask(ends, mask)
        attention_forward(h, wqkv, vec, mask, a, qkv, lse, mixed)

    return kernel_call(body, outs, [SM, VM, VM, VM], [pltpu.VMEM((t, t), F32)], us=13)(ends, h, wqkv, vec)


def fc_forward_call(h, mixed, wout, wfc, vec, fb):
    t = h.shape[0]
    outs = [like((t, D), F32), like((t, D), BF16), like((t, FF), BF16), like((t, FF), BF16)]

    def body(h, mixed, wout, wfc, vec, fb, mid, c, g, gp):
        out_forward(h, mixed, wout, vec, mid)
        fc_forward(mid, wfc, vec, fb, c, g, gp)

    return kernel_call(body, outs, [VM] * 6, us=9)(h, mixed, wout, wfc, vec, fb)


def ffn_backward_call(dy, h_mid, gp, wfc, wpt, vec):
    t = dy.shape[0]
    outs = [
        like((t, FF), BF16),
        like((1, FF), F32),
        like((t, D), F32),
        like((t, D), BF16),
        like((8, D), F32),
    ]

    def body(dy, h_mid, gp, wfc, wpt, vec, df_low, dfb, dh_mid, dh_low, dvec, dy_low, dc):
        ffn_backward(dy, h_mid, gp, wfc, wpt, vec, dy_low, df_low, dfb, dh_mid, dh_low, dvec, dc)

    scratch = [pltpu.VMEM((t, D), BF16), pltpu.VMEM((t, D), F32)]
    return kernel_call(body, outs, [VM] * 6, scratch, us=13)(dy, h_mid, gp, wfc, wpt, vec)


def attention_backward_call(ends, dh_mid, dh_low, h, qkv, lse, mixed, wqkv, wout, vec):
    t = h.shape[0]

    def body(
        ends, dh_mid, dh_low, h, qkv, lse, mixed, wqkv, wout, vec, dqkv, d_in, dvec, mask, dmix, da
    ):
        fill_mask(ends, mask)
        attention_backward(
            dh_mid, dh_low, h, qkv, lse, mixed, mask, wqkv, wout, vec, dmix, dqkv, da, d_in, dvec
        )

    outs = [like((t, 3 * D), BF16), like((t, D), F32), like((8, D), F32)]
    scratch = [pltpu.VMEM((t, t), F32), pltpu.VMEM((t, D), BF16), pltpu.VMEM((t, D), F32)]
    return kernel_call(body, outs, [SM] + [VM] * 9, scratch, us=18)(
        ends, dh_mid, dh_low, h, qkv, lse, mixed, wqkv, wout, vec
    )


class Cube:
    def __init__(self, groups, rows):
        self.groups, self.rows = groups, rows
        self.n = groups * rows
        self.bits = self.n.bit_length() - 1
        far = list(range(self.bits - 1, 2, -1))
        self.gather_plans = (far + [2, 1], far + [1, 2])
        self.mixed_plans = ([2] + far + [1], [1] + far + [2])
        self.scatter_plans = tuple(list(reversed(p)) for p in self.gather_plans)
        self.half = self.n // 2

    def swap(self, x, plans, step):
        pairs = [(i, i ^ (1 << plans[i & 1][step])) for i in range(self.n)]
        return lax.ppermute(x, BOTH, pairs)

    def swap_core(self, x):
        return lax.ppermute(x, BOTH, [(i, i ^ 1) for i in range(self.n)])

    def gather_swap(self, held, step, plans=None):
        return self.swap(held, plans or self.gather_plans, step)

    def gather_steps(self, held, first, end, plans=None):
        for step in range(first, end):
            held = jnp.concatenate([held, self.gather_swap(held, step, plans)], 0)
        return held

    def scatter_swap(self, halves, step):
        return self.swap(halves[1], self.scatter_plans, step)

    def scatter_add(self, keep, got):
        mid = keep.shape[0] // 2
        if mid == 0:
            return (keep + got)[0]
        return keep[:mid] + got[:mid], keep[mid:] + got[mid:]

    def scatter_steps(self, halves, first, end):
        for step in range(first, end):
            halves = self.scatter_add(halves[0], self.scatter_swap(halves, step))
        return halves

    def gather_source(self, me, side, slot, plans):
        core = (me & 1) ^ side
        dest = me ^ side
        for k in range(self.bits - 1):
            if (slot >> k) & 1:
                flip0, flip1 = 1 << plans[0][k], 1 << plans[1][k]
                dest = dest ^ jnp.where(core == 1, flip1, flip0)
        return dest

    def scatter_slot(self, me, dest):
        rel = me ^ dest
        core = dest & 1
        slot = 0
        for k in range(self.bits - 1):
            place = self.bits - 2 - k
            b0 = (rel >> self.scatter_plans[0][k]) & 1
            b1 = (rel >> self.scatter_plans[1][k]) & 1
            slot = slot + (jnp.where(core == 1, b1, b0) << place)
        return slot

    def row_of(self, me, side, pair):
        return 2 * pair + ((me & 1) ^ side)


lock = lax.optimization_barrier


def my_number(cube):
    return lax.axis_index("grp") * cube.rows + lax.axis_index("row")


def canonical(cube, pieces, plans):
    me = my_number(cube)
    ids = [cube.gather_source(me, side, s, plans) for side in (0, 1) for s in range(cube.half)]
    blocks = jnp.concatenate(pieces, 0)
    return jnp.zeros_like(blocks).at[jnp.stack(ids)].set(blocks)


def fits(rows, cols):
    return rows % 16 == 0 and cols % 128 == 0


def place_blocks(cube, pieces, plans, sem, *targets):
    me = my_number(cube)
    part = cube.half // 2
    copies = []
    for i, piece in enumerate(pieces):
        for s in range(part):
            dev = cube.gather_source(me, i // 2, (i % 2) * part + s, plans)
            for target in targets:
                rows, place = target(dev // cube.rows, dev % cube.rows)
                copies.append(pltpu.make_async_copy(piece.at[s, rows], place, sem))
    for cp in copies:
        cp.start()

    def wait():
        for cp in copies:
            cp.wait()

    return wait


def tiled(x, n):
    r, c = x.shape[-2] // 4, x.shape[-1] // n
    x = x.reshape(x.shape[:-2] + (4, r, n, c))
    return jnp.moveaxis(x, (-4, -2), (-2, -4)).reshape(x.shape[:-4] + (n * r, 4 * c))


def untiled(x, n):
    r, c = x.shape[-2] // n, x.shape[-1] // 4
    x = x.reshape(x.shape[:-2] + (n, r, 4, c))
    return jnp.moveaxis(x, (-4, -2), (-2, -4)).reshape(x.shape[:-4] + (4 * r, n * c))


def copy_tiles(src, dst, n, r, c, src_at=(0, 0), dst_at=(0, 0), to_wide=True):
    for i in range(4):
        for j in range(n):
            p, q = ((i, j), (j, i)) if to_wide else ((j, i), (i, j))
            rows = slice(src_at[0] + p[0] * r, src_at[0] + (p[0] + 1) * r)
            cols = slice(src_at[1] + p[1] * c, src_at[1] + (p[1] + 1) * c)
            rows_to = slice(dst_at[0] + q[0] * r, dst_at[0] + (q[0] + 1) * r)
            cols_to = slice(dst_at[1] + q[1] * c, dst_at[1] + (q[1] + 1) * c)
            dst[rows_to, cols_to] = src[rows, cols]


def blocks_of(cube, pieces, plans):
    return canonical(cube, pieces, plans).reshape((cube.groups, cube.rows) + pieces[0].shape[1:])


def unblocked(x):
    g_n, r_n, br, bc = x.shape
    return x.transpose(1, 2, 0, 3).reshape(r_n * br, g_n * bc)


def blocked(x, g_n, r_n):
    return x.reshape(r_n, x.shape[0] // r_n, g_n, x.shape[1] // g_n).transpose(2, 0, 1, 3)


def proj_full(cube, pieces):
    br, bc = pieces[0].shape[1:]
    full = blocks_of(cube, pieces, cube.mixed_plans)
    return full.transpose(0, 2, 1, 3).reshape(cube.groups * br, cube.rows * bc)


def attn_full(cube, pieces, sizes):
    tr, tc, vrows, vcols, bias = sizes
    full = blocks_of(cube, pieces, cube.gather_plans)
    wqkv = unblocked(untiled(full[:, :, : 3 * tr], 3))
    ext = full[:, :, 3 * tr :].astype(F32)
    vec = unblocked(ext[:, :, :vrows, :vcols])
    fb = ext[:, :, vrows, :bias].reshape(1, cube.n * bias)
    total = jnp.sum(ext[:, :, vrows + 1, 0]) * 16.0 + jnp.sum(ext[:, :, vrows + 1, 1])
    return wqkv, vec, fb, jnp.full((8, 128), total, F32)


def open_attention(cube, ends, h, pieces, sizes):
    br, bc = pieces[0].shape[1:]
    if not fits(br, bc):
        full = attn_full(cube, pieces, sizes)
        return full, attention_forward_call(ends, h, *full[:2])
    tr, tc, vrows, vcols, bias = sizes
    g_n, r_n = cube.groups, cube.rows
    t = h.shape[0]

    def body(ends, h, p0, p1, p2, p3, wqkv, vec, fb, tot, a, qkv, lse, mixed, mask, blk, sem):
        def target(g, r):
            return slice(None), blk.at[g, r]

        wait = place_blocks(cube, (p0, p1, p2, p3), cube.gather_plans, sem, target)
        fill_mask(ends, mask)
        wait()
        count = jnp.zeros((1, 128), F32)
        for g in range(g_n):
            for r in range(r_n):
                copy_tiles(
                    blk.at[g, r], wqkv.ref, 3, tr, tc, dst_at=(r * 4 * tr, g * 3 * tc), to_wide=False
                )
                ext = blk[g, r, 3 * tr : br, :].astype(F32)
                vec[r * vrows : (r + 1) * vrows, g * vcols : (g + 1) * vcols] = ext[0:vrows, 0:vcols]
                at = (g * r_n + r) * bias
                fb[0:1, at : at + bias] = ext[vrows : vrows + 1, 0:bias]
                count += ext[vrows + 1 : vrows + 2, 0:128]
        lane = lax.broadcasted_iota(jnp.int32, (1, 128), 1)
        weight = jnp.where(lane == 0, 16.0, jnp.where(lane == 1, 1.0, 0.0))
        tot[...] = jnp.broadcast_to(jnp.sum(count * weight, -1, keepdims=True), (8, 128))
        wqkv.flush()
        whole = {"qkv": (a, qkv), "mixed": ()}
        attention_forward(
            h, wqkv.ref, vec, mask, a.ref, qkv.ref, lse, mixed,
            done=lambda which: [x.flush() for x in whole[which]],
        )

    outs = [
        ((D, 3 * D), BF16, "flush"),
        ((8, D), F32, "vmem"),
        ((1, FF), F32, "vmem"),
        ((8, 128), F32, "vmem"),
        ((t, D), BF16, "flush"),
        ((t, 3 * D), BF16, "flush"),
        ((t, 128), F32, "vmem"),
        ((t, D), BF16, "vmem"),
    ]
    scratch = [
        pltpu.VMEM((t, t), F32),
        pltpu.VMEM((g_n, r_n, br, bc), BF16),
        pltpu.SemaphoreType.DMA,
    ]
    ins = [(ends, "smem"), (h, "vmem")] + [(x, "any") for x in pieces]
    got = staged_call(body, ins, outs, scratch, us=15)
    return got[:4], got[4:]


def open_fc(cube, h, mixed, pieces, vec, fb, sizes):
    br, bc = pieces[0].shape[1:]
    tr, tc = sizes[:2]
    t = h.shape[0]
    if not fits(br, bc):
        full = blocks_of(cube, pieces, cube.gather_plans)
        wfc, wout = unblocked(full[:, :, : 4 * tr]), unblocked(untiled(full[:, :, 4 * tr :], 1))
        return (wfc, wout), fc_forward_call(h, mixed, wout, wfc, vec, fb)

    def body(h, mixed, p0, p1, p2, p3, vec, fb, wfc, wout, mid, c, g, gp, blk, sem):
        def target_fc(g, r):
            rows, cols = pl.multiple_of(r * 4 * tr, 16), pl.multiple_of(g * bc, 128)
            return pl.ds(0, 4 * tr), wfc.ref.at[pl.ds(rows, 4 * tr), pl.ds(cols, bc)]

        def target_out(g, r):
            return pl.ds(4 * tr, tr), blk.at[g, r]

        place_blocks(cube, (p0, p1, p2, p3), cube.gather_plans, sem, target_fc, target_out)()
        wfc.flush()
        for g_i in range(cube.groups):
            for r in range(cube.rows):
                copy_tiles(
                    blk.at[g_i, r], wout.ref, 1, tr, tc, dst_at=(r * 4 * tr, g_i * tc), to_wide=False
                )
        wout.flush()
        out_forward(h, mixed, wout.ref, vec, mid.ref)
        mid.flush()
        fc_forward(mid.ref, wfc.ref, vec, fb, c, g, gp)

    ins = [(h, "vmem"), (mixed, "vmem")] + [(x, "any") for x in pieces] + [(vec, "vmem"), (fb, "vmem")]
    outs = [
        ((D, FF), BF16, "flush"),
        ((D, D), BF16, "flush"),
        ((t, D), F32, "flush"),
        ((t, D), BF16, "vmem"),
        ((t, FF), BF16, "vmem"),
        ((t, FF), BF16, "vmem"),
    ]
    scratch = [pltpu.VMEM((cube.groups, cube.rows, tr, bc), BF16), pltpu.SemaphoreType.DMA]
    got = staged_call(body, ins, outs, scratch, us=12)
    return got[:2], got[2:]


def second_pass(cube, ends, passes, mid0, g0, pieces, cot, wqkv, wout, wfc, vec, fb):
    br, bc = pieces[0].shape[1:]
    t = cot.shape[0]
    whole = fits(br, bc)
    if not whole:
        pieces = (proj_full(cube, pieces),)
    n_p = len(pieces)

    def body(*refs):
        ends, passes, mid0, g0 = refs[:4]
        src = refs[4 : 4 + n_p]
        cot, wqkv, wout, wfc, vec, fb = refs[4 + n_p : 10 + n_p]
        wpt, h1, hidden, d1, a, mixed, c, dqkv, dhl, df, dvec, dfb = refs[10 + n_p : 22 + n_p]
        grad0, grad1 = refs[22 + n_p : 24 + n_p]
        mask, qkv, lse, mid, g, gp, dy, dyl, tmp, dhm, dmix, dvec2, dyt, grad, sem = refs[24 + n_p :]
        me = my_number(cube)

        def target(g, r):
            rows, cols = pl.multiple_of(g * br, 16), pl.multiple_of(r * bc, 128)
            return slice(None), wpt.ref.at[pl.ds(rows, br), pl.ds(cols, bc)]

        if whole:
            wait = place_blocks(cube, src, cube.mixed_plans, sem, target)
        else:
            copy = pltpu.make_async_copy(src[0], wpt.ref, sem)
            copy.start()
            wait = copy.wait
        for x in (vec, fb, g0, mid0):
            x.start()
        vec, fb = vec.get(), fb.get()
        fill_mask(ends, mask)
        wait()
        g0.get()
        mid0.get()
        wqkv.start()
        wout.start()
        proj_forward(mid0.ref, g0.ref, wpt.ref, vec, h1.ref)
        wqkv.get()
        wout.get()
        wfc.start()
        cot.start()
        attention_forward(
            h1.ref, wqkv.ref, vec, mask, a.ref, qkv, lse, mixed.ref,
            done=lambda which: {"qkv": a, "mixed": mixed}[which].flush(),
        )
        out_forward(h1.ref, mixed.ref, wout.ref, vec, mid)
        wfc.get()
        wpt.flush()
        h1.flush()
        fc_forward(mid, wfc.ref, vec, fb, c.ref, g, gp)
        c.flush()
        proj_forward(mid, g, wpt.ref, vec, dy)
        active = passes[0] > 1
        hidden.ref[...] = jnp.where(active, dy[...], h1.ref[...]).astype(BF16)
        hidden.flush()
        valid = lax.broadcasted_iota(jnp.int32, (t, 1), 0) < ends[0, ends.shape[1] - 1]
        cot.get()
        dy[...] = jnp.where(valid & active, cot.ref[...].astype(F32), 0.0)
        ffn_backward(
            dy, mid, gp, wfc.ref, wpt.ref, vec, dyl, df.ref, dfb.ref, dhm, dhl.ref, dvec2, tmp,
            done=lambda which: df.flush(),
        )
        dhl.flush()
        attention_backward(
            dhm, dhl.ref, h1.ref, qkv, lse, mixed.ref, mask, wqkv.ref, wout.ref, vec,
            dmix, dqkv.ref, tmp, dy, dvec.ref, done=lambda which: dqkv.flush(),
        )
        dvec.ref[...] += dvec2[...]
        dvec.flush()
        dfb.flush()
        d1.ref[...] = jnp.where(active, dy[...], jnp.where(valid, cot.ref[...].astype(F32), 0.0))
        d1.flush()
        dyt[:, 0:t] = dyl[...].astype(F32).T.astype(BF16)
        dyt[:, t : 2 * t] = d1.ref[...].T.astype(BF16)
        if not whole:
            grad0[...] = mm(dyt[:, 0:t], g[...], NN) + mm(dyt[:, t : 2 * t], g0.ref[...], NN)
            return
        n = 0
        for side, out in ((1, grad1), (0, grad0)):
            for pair in range(cube.rows // 2):
                r = cube.row_of(me, side, pair)
                cols = pl.ds(pl.multiple_of(r * bc, 128), bc)
                both = mm(dyt[:, 0:t], g[:, cols], NN) + mm(dyt[:, t : 2 * t], g0.ref[:, cols], NN)
                grad[:, n * bc : (n + 1) * bc] = both.astype(BF16)
                for group in range(cube.groups):
                    block = grad.at[pl.ds(group * br, br), pl.ds(n * bc, bc)]
                    out.put(block, cube.scatter_slot(me, group * cube.rows + r))
                n += 1

    ins = [(ends, "smem"), (passes, "smem"), (mid0, "fetch"), (g0, "fetch")]
    ins += [(x, "any") for x in pieces]
    ins += [(x, "fetch") for x in (cot, wqkv, wout, wfc, vec, fb)]
    outs = [
        ((D, FF), BF16, "flush"),
        ((t, D), F32, "flush"),
        ((t, D), BF16, "flush"),
        ((t, D), F32, "flush"),
        ((t, D), BF16, "flush"),
        ((t, D), BF16, "flush"),
        ((t, D), BF16, "flush"),
        ((t, 3 * D), BF16, "flush"),
        ((t, D), BF16, "flush"),
        ((t, FF), BF16, "flush"),
        ((8, D), F32, "flush"),
        ((1, FF), F32, "flush"),
    ]
    if whole:
        outs += [((cube.half, br, bc), BF16, "sink", cube.half)] * 2
    else:
        outs += [((D, FF), F32, "vmem"), ((8, 128), F32, "vmem")]
    scratch = [
        pltpu.VMEM((t, t), F32),
        pltpu.VMEM((t, 3 * D), BF16),
        pltpu.VMEM((t, 128), F32),
        pltpu.VMEM((t, D), F32),
        pltpu.VMEM((t, FF), BF16),
        pltpu.VMEM((t, FF), BF16),
        pltpu.VMEM((t, D), F32),
        pltpu.VMEM((t, D), BF16),
        pltpu.VMEM((t, D), F32),
        pltpu.VMEM((t, D), F32),
        pltpu.VMEM((t, D), BF16),
        pltpu.VMEM((8, D), F32),
        pltpu.VMEM((D, 2 * t), BF16),
        pltpu.VMEM((D, FF), BF16),
        pltpu.SemaphoreType.DMA,
    ]
    got = staged_call(body, ins, outs, scratch, us=50)
    slots = got[12:]
    if not whole:
        full = slots[0].astype(BF16).reshape(cube.groups, br, cube.rows, bc).transpose(0, 2, 1, 3)
        slots = ordered_slots(cube, full.reshape(cube.n, br, bc))
    return got[:12], slots


def pack(w_qkv, w_out, w_fc, vectors, fc_bias, seg_ends, sizes):
    tr, tc, vrows, vcols, bias = sizes
    wide = 4 * tc

    def extra(vec, fb, n_valid):
        lane = lax.broadcasted_iota(jnp.int32, (1, wide), 1)
        n_high = n_valid // 16
        count = jnp.where(lane == 0, n_high, jnp.where(lane == 1, n_valid - 16 * n_high, 0))
        rows = [
            jnp.concatenate([vec.astype(F32), jnp.zeros((vrows, wide - vcols), F32)], 1),
            jnp.concatenate([fb.astype(F32), jnp.zeros((1, wide - bias), F32)], 1),
            count.astype(F32),
            jnp.zeros((EXTRA - vrows - 2, wide), F32),
        ]
        return jnp.concatenate(rows, 0).astype(BF16)

    if not fits(tr, wide):
        ext = extra(vectors, fc_bias[None], seg_ends[0, -1])
        return (
            jnp.concatenate([tiled(w_qkv, 3), ext], 0),
            jnp.concatenate([w_fc, tiled(w_out, 1)], 0),
        )

    def body(wq, wo, wf, vec, fb, ends, out_a, out_f):
        copy_tiles(wq, out_a, 3, tr, tc)
        out_a[3 * tr : 3 * tr + EXTRA, :] = extra(vec[...], fb[...], ends[0, ends.shape[1] - 1])
        out_f[0 : 4 * tr, :] = wf[...]
        copy_tiles(wo, out_f, 1, tr, tc, dst_at=(4 * tr, 0))

    outs = [like((3 * tr + EXTRA, wide), BF16), like((5 * tr, wide), BF16)]
    return kernel_call(body, outs, [VM] * 5 + [SM], us=2)(
        w_qkv, w_out, w_fc, vectors, fc_bias[None], seg_ends
    )


def ordered_slots(cube, blocks):
    me = my_number(cube)
    order = [cube.scatter_slot(me, dest) + cube.half * ((me ^ dest) & 1) for dest in range(cube.n)]
    slots = jnp.zeros_like(blocks).at[jnp.stack(order)].set(blocks)
    return slots[: cube.half], slots[cube.half :]


def stacked_t(parts, out):
    t = parts[0].shape[0]
    for i, part in enumerate(parts):
        out[:, i * t : (i + 1) * t] = part[...].astype(F32).T.astype(BF16)


def side_rows(cube, me, side, src, out, height):
    for pair in range(cube.rows // 2):
        r = cube.row_of(me, side, pair)
        out[pair * height : (pair + 1) * height, :] = src[pl.ds(pl.multiple_of(r * height, 16), height), :]


def ffn_grad_side(cube, me, side, sizes, operands, lt, lhs, grad, wide, blocks, out):
    m1, m0, dh1, dh0, c1, c0, df1, df0 = operands
    tr, tc = sizes[:2]
    bc = 4 * tc
    t = lt.shape[1] // 2
    pairs = cube.rows // 2
    stacked_t((m1(), m0()), lt)
    side_rows(cube, me, side, lt, lhs, 4 * tr)
    dh1, dh0 = dh1(), dh0()
    for j in range(0, D, NB):
        cols = slice(j, j + NB)
        both = mm(lhs[:, 0:t], dh1[:, cols], NN) + mm(lhs[:, t : 2 * t], dh0[:, cols], NN)
        wide[:, cols] = both.astype(BF16)
    for g in range(cube.groups):
        for pair in range(pairs):
            copy_tiles(wide, blocks.at[g * pairs + pair], 1, tr, tc, src_at=(pair * 4 * tr, g * tc))
    stacked_t((c1(), c0()), lt)
    side_rows(cube, me, side, lt, lhs, 4 * tr)
    df1, df0 = df1(), df0()
    for first in range(0, cube.groups, 2):
        cols = slice(first * bc, (first + 2) * bc)
        both = mm(lhs[:, 0:t], df1[:, cols], NN) + mm(lhs[:, t : 2 * t], df0[:, cols], NN)
        grad[:, cols] = both.astype(BF16)
        for g in (first, first + 1):
            for pair in range(pairs):
                slot = cube.scatter_slot(me, g * cube.rows + cube.row_of(me, side, pair))
                rows = pl.ds(pair * 4 * tr, 4 * tr)
                out.put(grad.at[rows, pl.ds(g * bc, bc)], slot, pl.ds(0, 4 * tr))
                out.put(blocks.at[g * pairs + pair], slot, pl.ds(4 * tr, tr))


def ffn_grad_scratch(cube, sizes, t):
    tr, tc = sizes[:2]
    return [
        pltpu.VMEM((D, 2 * t), BF16),
        pltpu.VMEM((D // 2, 2 * t), BF16),
        pltpu.VMEM((D // 2, FF), BF16),
        pltpu.VMEM((D // 2, D), BF16),
        pltpu.VMEM((cube.half, tr, 4 * tc), BF16),
    ]


def ffn_backward_and_grad(cube, dy, h_mid, gp, wfc, wpt, vec, c1, c0, df1, m1, m0, dh1, sizes):
    t = dy.shape[0]
    tr, tc = sizes[:2]
    br, bc = 5 * tr, 4 * tc
    if not fits(br, bc):
        df0, *rest = ffn_backward_call(dy, h_mid, gp, wfc, wpt, vec)
        dfc = blocked(mm(c1, df1, TN) + mm(c0, df0, TN), cube.groups, cube.rows)
        dout = blocked(mm(m1, dh1, TN) + mm(m0, rest[2], TN), cube.groups, cube.rows)
        full = jnp.concatenate([dfc, tiled(dout, 1)], 2).astype(BF16)
        keep, send = ordered_slots(cube, full.reshape(cube.n, br, bc))
        return rest, send, keep

    def body(
        dy, h_mid, gp, wfc, wpt, vec, c1, c0, df1, m1, m0, dh1, dfb, dh_mid, dh_low, dvec, df0, send,
        dy_low, dc, *scratch,
    ):
        me = my_number(cube)
        order = {"dy": dy, "wpt": wpt, "gp": gp, "wfc": wfc, "h_mid": h_mid}
        for x in (vec, dy, wpt, gp):
            x.start()

        def use(which, j=0):
            if which == "hidden":
                if j == 0:
                    wpt.get()
                    wfc.start()
                    h_mid.start()
                if j == FF // 2:
                    for x in (m1, m0, dh1, c1, c0, df1):
                        x.start()
                gp.get(j // (FF // 4) + 1)
            else:
                order[which].get()
                vec.get()

        ffn_backward(
            dy.get(), h_mid.ref, gp.ref, wfc.ref, wpt.ref, vec.ref, dy_low, df0.ref, dfb.ref, dh_mid.ref,
            dh_low.ref, dvec.ref, dc, use=use, done=lambda which: df0.flush(),
        )
        for x in (dh_mid, dh_low, dvec, dfb):
            x.flush()
        operands = (m1.get, m0.get, dh1.get, lambda: dh_low.ref, c1.get, c0.get, df1.get, lambda: df0.ref)
        ffn_grad_side(cube, me, 1, sizes, operands, *scratch, send)

    ins = [
        (dy, "fetch"), (h_mid, "fetch"), (gp, "fetch", 1, 4), (wfc, "fetch"), (wpt, "fetch"), (vec, "fetch"),
        (c1, "fetch"), (c0, "fetch"), (df1, "fetch"), (m1, "fetch"), (m0, "fetch"), (dh1, "fetch"),
    ]
    outs = [
        ((1, FF), F32, "flush"),
        ((t, D), F32, "flush"),
        ((t, D), BF16, "flush"),
        ((8, D), F32, "flush"),
        ((t, FF), BF16, "flush"),
        ((cube.half, br, bc), BF16, "sink", 2 * cube.half),
    ]
    scratch = [pltpu.VMEM((t, D), BF16), pltpu.VMEM((t, D), F32)] + ffn_grad_scratch(cube, sizes, t)
    got = staged_call(body, ins, outs, scratch, us=18)
    return got[:4], got[5], (m1, m0, dh1, got[2], c1, c0, df1, got[4])


def ffn_grad_keep(cube, operands, sizes):
    tr, tc = sizes[:2]
    br, bc = 5 * tr, 4 * tc
    if not fits(br, bc):
        return operands
    t = operands[0].shape[0]

    def body(*refs):
        given, keep, scratch = refs[:8], refs[8], refs[9:]
        for x in given:
            x.start()
        ffn_grad_side(cube, my_number(cube), 0, sizes, [x.get for x in given], *scratch, keep)

    ins = [(x, "fetch") for x in operands]
    outs = [((cube.half, br, bc), BF16, "sink", 2 * cube.half)]
    return staged_call(body, ins, outs, ffn_grad_scratch(cube, sizes, t), us=8)[0]


def attention_grad_side(cube, me, side, sizes, operands, lt, lhs, wide, blocks, out):
    a1, a0, dq1, dq0, dvec, dfb = operands
    tr, tc, vrows, vcols, bias = sizes
    br, bc = 3 * tr + EXTRA, 4 * tc
    g_n, pairs = cube.groups, cube.rows // 2
    t = lt.shape[1] // 2
    stacked_t((a1(), a0()), lt)
    side_rows(cube, me, side, lt, lhs, 4 * tr)
    dq1, dq0 = dq1(), dq0()
    for j in range(0, 3 * D, NB):
        cols = slice(j, j + NB)
        full = mm(lhs[:, 0:t], dq1[:, cols], NN) + mm(lhs[:, t : 2 * t], dq0[:, cols], NN)
        wide[:, cols] = full.astype(BF16)
    dvec, dfb = dvec(), dfb()

    def extra(g, r):
        vecs = dvec[r * vrows : (r + 1) * vrows, g * vcols : (g + 1) * vcols]
        at = (g * cube.rows + r) * bias
        rows = [
            jnp.concatenate([vecs, jnp.zeros((vrows, bc - vcols), F32)], 1),
            jnp.concatenate([dfb[0:1, at : at + bias], jnp.zeros((1, bc - bias), F32)], 1),
            jnp.zeros((EXTRA - vrows - 1, bc), F32),
        ]
        return jnp.concatenate(rows, 0)

    first = ((me & 1) ^ side) == 0
    for g in range(g_n):
        for pair in range(pairs):
            n = g * pairs + pair
            block = blocks.at[n]
            copy_tiles(wide, block, 3, tr, tc, src_at=(pair * 4 * tr, g * 3 * tc))
            ext = jnp.where(first, extra(g, 2 * pair), extra(g, 2 * pair + 1))
            block[3 * tr : br, :] = ext.astype(BF16)
            out.put(blocks.at[n], cube.scatter_slot(me, g * cube.rows + cube.row_of(me, side, pair)))


def attention_grad_scratch(cube, sizes, t):
    tr, tc = sizes[:2]
    return [
        pltpu.VMEM((D, 2 * t), BF16),
        pltpu.VMEM((D // 2, 2 * t), BF16),
        pltpu.VMEM((D // 2, 3 * D), BF16),
        pltpu.VMEM((cube.half, 3 * tr + EXTRA, 4 * tc), BF16),
    ]


def attention_backward_and_grad(
    cube, ends, dh_mid, dh0, h, qkv, lse, m0, wqkv, wout, vec, a1, a0, dq1, dvecs, dfbs, sizes
):
    tr, tc, vrows, vcols, bias = sizes
    br, bc = 3 * tr + EXTRA, 4 * tc
    g_n, r_n = cube.groups, cube.rows
    t = h.shape[0]
    if not fits(br, bc):
        dq0, d_in, dvec = attention_backward_call(ends, dh_mid, dh0, h, qkv, lse, m0, wqkv, wout, vec)
        dvec, dfb = dvec + dvecs[0] + dvecs[1], dfbs[0] + dfbs[1]
        dqkv = tiled(blocked(mm(a1, dq1, TN) + mm(a0, dq0, TN), g_n, r_n), 3)
        vecs = blocked(dvec, g_n, r_n)
        biases = dfb.reshape(g_n, r_n, 1, bias)
        ext = jnp.zeros((g_n, r_n, EXTRA, bc), F32)
        ext = ext.at[:, :, :vrows, :vcols].set(vecs).at[:, :, vrows : vrows + 1, :bias].set(biases)
        full = jnp.concatenate([dqkv, ext], 2).astype(BF16)
        keep, send = ordered_slots(cube, full.reshape(cube.n, br, bc))
        return d_in, send, keep

    def body(
        ends, dh_mid, dh0, h, qkv, lse, m0, wqkv, wout, vec, a1, a0, dq1, dvec1, dvec0, dfb1, dfb0,
        d_in, dq0, dvec, dfb, send, mask, dmix, da, *scratch,
    ):
        waits = {
            "dh_low": dh0, "wout": wout, "qkv": qkv, "mixed": m0, "lse": lse, "wqkv": wqkv, "h": h,
            "dh_mid": dh_mid,
        }
        for x in (*waits.values(), vec, a1, a0, dq1, dvec1, dvec0, dfb1, dfb0):
            x.start()
        fill_mask(ends, mask)
        attention_backward(
            dh_mid.ref, dh0.ref, h.ref, qkv.ref, lse.ref, m0.ref, mask, wqkv.ref, wout.ref, vec.get(),
            dmix, dq0.ref, da, d_in.ref, dvec.ref, use=lambda which: waits[which].get(),
            done=lambda which: dq0.flush(),
        )
        d_in.flush()
        dvec.ref[...] += dvec1.get()[...] + dvec0.get()[...]
        dfb.ref[...] = dfb1.get()[...] + dfb0.get()[...]
        dvec.flush()
        dfb.flush()
        operands = (a1.get, a0.get, dq1.get, lambda: dq0.ref, lambda: dvec.ref, lambda: dfb.ref)
        attention_grad_side(cube, my_number(cube), 1, sizes, operands, *scratch, send)

    ins = [(ends, "smem")] + [(x, "fetch") for x in (dh_mid, dh0, h, qkv, lse, m0, wqkv, wout)]
    ins += [(x, "fetch") for x in (vec, a1, a0, dq1, *dvecs, *dfbs)]
    outs = [
        ((t, D), F32, "flush"),
        ((t, 3 * D), BF16, "flush"),
        ((8, D), F32, "flush"),
        ((1, FF), F32, "flush"),
        ((cube.half, br, bc), BF16, "sink", cube.half),
    ]
    scratch = [pltpu.VMEM((t, t), F32), pltpu.VMEM((t, D), BF16), pltpu.VMEM((t, D), F32)]
    scratch += attention_grad_scratch(cube, sizes, t)
    got = staged_call(body, ins, outs, scratch, us=17, mib=48)
    return got[0], got[4], (a1, a0, dq1, got[1], got[2], got[3])


def attention_grad_keep(cube, operands, sizes):
    tr, tc = sizes[:2]
    br, bc = 3 * tr + EXTRA, 4 * tc
    if not fits(br, bc):
        return operands
    t = operands[0].shape[0]

    def body(*refs):
        given, keep, scratch = refs[:6], refs[6], refs[7:]
        for x in given:
            x.start()
        attention_grad_side(cube, my_number(cube), 0, sizes, [x.get for x in given], *scratch, keep)

    ins = [(x, "fetch") for x in operands]
    outs = [((cube.half, br, bc), BF16, "sink", cube.half)]
    return staged_call(body, ins, outs, attention_grad_scratch(cube, sizes, t), us=8, mib=48)[0]


def adam_update(weight, first, second, grad, keep_frac):
    t_step = float(STEP)
    first_new = 0.9 * first * keep_frac + 0.1 * grad
    second_new = 0.95 * second * keep_frac + 0.05 * grad * grad
    first_hat = first_new / (1.0 - 0.9**t_step)
    second_hat = second_new / (1.0 - 0.95**t_step)
    weight_new = weight.astype(F32) * (1.0 - LEARN_RATE * WEIGHT_DECAY) - LEARN_RATE * first_hat / (
        jnp.sqrt(second_hat) + 1e-08
    )
    return (weight_new.astype(BF16), first_new, second_new)


def body(
    hidden_in,
    cotangent,
    w_qkv,
    w_out,
    w_fc,
    w_proj,
    vectors,
    fc_bias,
    first_qkv,
    first_out,
    first_fc,
    first_proj,
    first_vectors,
    first_fc_bias,
    second_qkv,
    second_out,
    second_fc,
    second_proj,
    second_vectors,
    second_fc_bias,
    seg_ends,
    pass_counts,
    reset_flag,
):
    cube = Cube(lax.axis_size("grp"), lax.axis_size("row"))
    rows_w = w_qkv.shape[0]
    vrows, vcols = vectors.shape
    bias = fc_bias.shape[0]
    tr, tc = rows_w // 4, w_out.shape[1]
    sizes = (tr, tc, vrows, vcols, bias)

    far = cube.bits - 3
    near, last = far, far + 1
    join = lambda x, y: jnp.concatenate([x, y], 0)
    a, f = pack(w_qkv, w_out, w_fc, vectors, fc_bias, seg_ends, sizes)
    mixed = cube.mixed_plans
    a, p = lock((cube.gather_steps(a[None], 0, 1), cube.gather_steps(w_proj.T[None], 0, 1, mixed)))
    a = cube.gather_steps(a, 1, far)

    a, f = lock((a, f[None]))
    got, f = lock((cube.gather_swap(a, near), cube.gather_steps(f, 0, 1)))
    a = join(a, got)

    a, f = lock((a, f))
    last_a, f = lock((cube.gather_swap(a, last), cube.gather_steps(f, 1, far)))

    f, p = lock((f, p))
    core_a0, core_a1, got, p = lock(
        (
            cube.swap_core(a),
            cube.swap_core(last_a),
            cube.gather_swap(f, near),
            cube.gather_steps(p, 1, far, mixed),
        )
    )
    f = join(f, got)

    h0, f, p = lock((hidden_in, f, p))
    full, acts = open_attention(cube, seg_ends, h0, (a, last_a, core_a0, core_a1), sizes)
    full, acts, last_f, core_f0, p = lock(
        (
            full,
            acts,
            cube.gather_swap(f, last),
            cube.swap_core(f),
            cube.gather_steps(p, far, last, mixed),
        )
    )
    wqkv, vec, fb, tot = full
    a0, qkv0, lse0, mixed0 = acts

    core_f1 = cube.swap_core(last_f)
    core_f1, p = lock((core_f1, p))
    opened = open_fc(cube, h0, mixed0, (f, last_f, core_f0, core_f1), vec, fb, sizes)
    opened, last_p, core_p0 = lock((opened, cube.gather_swap(p, last, mixed), cube.swap_core(p)))
    (wfc, wout), (mid0, c0, g0, gp0) = opened
    core_p1 = cube.swap_core(last_p)
    made, slots = second_pass(
        cube, seg_ends, pass_counts, mid0, g0, (p, last_p, core_p0, core_p1), cotangent, wqkv, wout, wfc, vec, fb
    )
    wpt, h1, hidden, d1, a1, mixed1, c1, dqkv1, dhl1, dfl1, dvec1, dfb1 = made
    keep_p, send_p = slots
    total = tot[0, 0]
    end = cube.bits - 1

    p = cube.scatter_add(keep_p, cube.swap_core(send_p))

    d1, p = lock((d1, p))
    back, send_f, rest = ffn_backward_and_grad(
        cube, d1, mid0, gp0, wfc, wpt, vec, c1, c0, dfl1, mixed1, mixed0, dhl1, sizes
    )
    back, send_f, rest, got = lock((back, send_f, rest, cube.scatter_swap(p, 0)))
    dfb0, dhm0, dhl0, dvec0 = back
    p = cube.scatter_add(p[0], got)

    send_f, rest, p = lock((send_f, rest, p))
    keep_f = ffn_grad_keep(cube, rest, sizes)
    keep_f, got_f, got = lock((keep_f, cube.swap_core(send_f), cube.scatter_swap(p, 1)))
    f = cube.scatter_add(keep_f, got_f)
    p = cube.scatter_add(p[0], got)

    dhl0, f, p = lock((dhl0, f, p))
    input_grad, send_a, rest = attention_backward_and_grad(
        cube, seg_ends, dhm0, dhl0, h0, qkv0, lse0, mixed0, wqkv, wout, vec, a1, a0, dqkv1,
        (dvec1, dvec0), (dfb1, dfb0), sizes,
    )
    send_a, rest, got_f, p = lock((send_a, rest, cube.scatter_swap(f, 0), cube.scatter_steps(p, 2, 3)))
    f = cube.scatter_add(f[0], got_f)

    send_a, rest, f, p = lock((send_a, rest, f, p))
    keep_a = attention_grad_keep(cube, rest, sizes)
    keep_a, got_a, got_f, sum_p = lock(
        (keep_a, cube.swap_core(send_a), cube.scatter_swap(f, 1), cube.scatter_steps(p, 3, end))
    )
    a = cube.scatter_add(keep_a, got_a)
    f = cube.scatter_add(f[0], got_f)

    a, f = lock((a, f))
    got_a, f = lock((cube.scatter_swap(a, 0), cube.scatter_steps(f, 2, 3)))
    a = cube.scatter_add(a[0], got_a)

    a, f = lock((a, f))
    got_a, sum_f = lock((cube.scatter_swap(a, 1), cube.scatter_steps(f, 3, end)))
    a = cube.scatter_add(a[0], got_a)
    sum_a = cube.scatter_steps(a, 2, end)

    sum_a, sum_f = sum_a.astype(F32), sum_f.astype(F32)
    summed = (
        untiled(sum_a[: 3 * tr], 3),
        untiled(sum_f[rows_w:], 1),
        sum_f[:rows_w],
        sum_p.T.astype(F32),
        sum_a[3 * tr : 3 * tr + vrows, :vcols],
        sum_a[3 * tr + vrows, :bias],
    )
    grads = tuple(s / total for s in summed)
    keep_feat = 1.0 - reset_flag.astype(F32)
    keep_rows = lax.dynamic_slice_in_dim(keep_feat, lax.axis_index("row") * rows_w, rows_w)[:, None]
    keep_cols = lax.dynamic_slice_in_dim(keep_feat, lax.axis_index("grp") * vcols, vcols)[None, :]
    bias_index = (my_number(cube) * bias + jnp.arange(bias, dtype=jnp.int32)) % D
    keeps = (keep_rows, keep_rows, keep_rows, keep_cols, keep_cols, keep_feat[bias_index])
    weights = (w_qkv, w_out, w_fc, w_proj, vectors, fc_bias)
    firsts = (first_qkv, first_out, first_fc, first_proj, first_vectors, first_fc_bias)
    seconds = (second_qkv, second_out, second_fc, second_proj, second_vectors, second_fc_bias)
    updated = [
        adam_update(w, m, v, g, kp) for w, m, v, g, kp in zip(weights, firsts, seconds, grads, keeps)
    ]
    return (
        (hidden, input_grad)
        + grads
        + tuple(u[0] for u in updated)
        + tuple(u[1] for u in updated)
        + tuple(u[2] for u in updated)
    )


def solution(mesh):
    tokens = P(("grp", "row"), None)
    flat = P(("grp", "row"))
    tiles = P("row", "grp")
    six = (tiles, tiles, tiles, tiles, tiles, flat)
    return jax.shard_map(
        body,
        mesh=mesh,
        in_specs=(tokens, tokens) + six * 3 + (tokens, P("grp"), P()),
        out_specs=(tokens, tokens) + six * 4,
        check_vma=False,
    )
```

```python
import functools

import jax
import jax.numpy as jnp
from jax import lax
from jax.experimental import pallas as pl
from jax.experimental.pallas import tpu as pltpu
from jax.sharding import PartitionSpec as P

D = 768
HEADS = 12
HEAD = 64
FF = 3072
STEP = 10
LEARN_RATE = 0.03
WEIGHT_DECAY = 0.1
F32 = jnp.float32
BF16 = jnp.bfloat16
NN = (((1,), (0,)), ((), ()))
NT = (((1,), (1,)), ((), ()))
TN = (((0,), (0,)), ((), ()))
NB = 256
LN_ROWS = 32
EXTRA = 16
GELU_A = 0.7978845608028654
GELU_B = 0.044715
BOTH = ("grp", "row")

VM = pl.BlockSpec(memory_space=pltpu.VMEM)
SM = pl.BlockSpec(memory_space=pltpu.SMEM)
HB = pl.BlockSpec(memory_space=pl.ANY)


def params(mib):
    return pltpu.CompilerParams(vmem_limit_bytes=mib * 2**20)


def like(shape, dtype):
    return jax.ShapeDtypeStruct(shape, dtype)


def mm(a, b, dims):
    return lax.dot_general(a, b, dims, preferred_element_type=F32)


def kernel_call(body, outs, specs, scratch=(), us=5, mib=60):
    return pl.pallas_call(
        body,
        out_shape=outs,
        in_specs=specs,
        out_specs=[VM] * len(outs),
        scratch_shapes=list(scratch),
        compiler_params=params(mib),
        cost_estimate=pl.CostEstimate(
            flops=int(us * 1e9), bytes_accessed=int(us * 3e6), transcendentals=0
        ),
    )


class Fetched:
    def __init__(self, src, dst, sems, axis):
        self.ref, n = dst, len(sems)
        size = dst.shape[axis] // n
        self.copies, self.begun, self.waited = [], 0, 0
        for i in range(n):
            at = tuple(pl.ds(i * size, size) if d == axis else slice(None) for d in range(len(dst.shape)))
            self.copies.append(pltpu.make_async_copy(src.at[at], dst.at[at], sems[i]))

    def start(self, n=None):
        for copy in self.copies[self.begun : n]:
            copy.start()
            self.begun += 1

    def get(self, n=None):
        self.start(n)
        for copy in self.copies[self.waited : n]:
            copy.wait()
            self.waited += 1
        return self.ref


class Flushed:
    def __init__(self, dst, src, sems):
        self.dst, self.ref, self.sems, self.copies = dst, src, list(sems), []

    def flush(self, *at):
        at = at or (slice(None),)
        copy = pltpu.make_async_copy(self.ref.at[at], self.dst.at[at], self.sems[len(self.copies)])
        copy.start()
        self.copies.append(copy)

    def finish(self):
        if not self.copies:
            self.flush()
        for copy in self.copies:
            copy.wait()


class Sink:
    def __init__(self, dst, sems):
        self.dst, self.sems, self.copies = dst, list(sems), []

    def put(self, src, *at):
        copy = pltpu.make_async_copy(src, self.dst.at[at], self.sems[len(self.copies)])
        copy.start()
        self.copies.append(copy)

    def finish(self):
        for copy in self.copies:
            copy.wait()


def staged_call(body, ins, outs, scratch=(), us=5, mib=60):
    n_in, n_out = len(ins), len(outs)
    spec_of = {"smem": SM, "vmem": VM, "any": HB, "fetch": HB, "flush": HB, "sink": HB}
    fetches = [i for i, how in enumerate(ins) if how[1] == "fetch"]
    flushes = [i for i, how in enumerate(outs) if how[2] == "flush"]
    sinks = [i for i, how in enumerate(outs) if how[2] == "sink"]
    extra = [pltpu.VMEM(ins[i][0].shape, ins[i][0].dtype) for i in fetches]
    extra += [pltpu.VMEM(outs[i][0], outs[i][1]) for i in flushes]
    counts = [(ins[i] + (0, 1))[3] if len(ins[i]) > 2 else 1 for i in fetches]
    counts += [outs[i][3] if len(outs[i]) > 3 else 1 for i in flushes + sinks]
    axes = [ins[i][2] if len(ins[i]) > 2 else 0 for i in fetches]
    extra += [pltpu.SemaphoreType.DMA((max(sum(counts), 1),))]

    def run(*refs):
        given, made = list(refs[:n_in]), list(refs[n_in : n_in + n_out])
        rest = refs[n_in + n_out :]
        own, mine = rest[: len(scratch)], rest[len(scratch) :]
        buffers, sem = mine[:-1], mine[-1]
        first = 0
        for j, i in enumerate(fetches + flushes + sinks):
            sems = [sem.at[first + k] for k in range(counts[j])]
            first += counts[j]
            if j < len(fetches):
                given[i] = Fetched(given[i], buffers[j], sems, axes[j])
            elif j < len(buffers):
                made[i] = Flushed(made[i], buffers[j], sems)
            else:
                made[i] = Sink(made[i], sems)
        body(*given, *made, *own)
        for i in fetches:
            given[i].get()
        for i in flushes + sinks:
            made[i].finish()

    return pl.pallas_call(
        run,
        out_shape=[like(out[0], out[1]) for out in outs],
        in_specs=[spec_of[how[1]] for how in ins],
        out_specs=[spec_of[how[2]] for how in outs],
        scratch_shapes=list(scratch) + extra,
        compiler_params=params(mib),
        cost_estimate=pl.CostEstimate(
            flops=int(us * 1e9), bytes_accessed=int(us * 3e6), transcendentals=0
        ),
    )(*[how[0] for how in ins])


def norm_stats(x):
    centred = x - jnp.mean(x, -1, keepdims=True)
    inv = lax.rsqrt(jnp.mean(centred * centred, -1, keepdims=True) + 1e-5)
    return centred * inv, inv


def colsum(x):
    return jnp.sum(x, 0, keepdims=True)


def norm_forward(x, gain, bias, out):
    for i in range(0, x.shape[0], LN_ROWS):
        rows = slice(i, i + LN_ROWS)
        xhat, _ = norm_stats(x[rows, :].astype(F32))
        out[rows, :] = (xhat * gain + bias).astype(BF16)


def fold(x):
    return jnp.sum(x.reshape(x.shape[0] // 8, 8, x.shape[1]), 0)


def fill_mask(ends_ref, mask_ref):
    tokens = mask_ref.shape[0]
    n_ends = ends_ref.shape[1]

    def segments(pos):
        seg = jnp.zeros(pos.shape, jnp.int32)
        for e in range(n_ends):
            seg += (pos >= ends_ref[0, e]).astype(jnp.int32)
        return seg

    seg_keys = segments(lax.broadcasted_iota(jnp.int32, (1, tokens), 1))
    for i in range(0, tokens, 128):
        pos = lax.broadcasted_iota(jnp.int32, (128, 1), 0) + i
        key = lax.broadcasted_iota(jnp.int32, (128, tokens), 1)
        seen = (segments(pos) == seg_keys) & (key <= pos)
        mask_ref[i : i + 128, :] = jnp.where(seen, 0.0, -1e30)


def attention_forward(h, wqkv, vec, mask, a, qkv, lse, mixed, tile=256, done=None):
    tokens = h.shape[0]
    done = done or (lambda which: None)
    norm_forward(h, vec[0:1, :], vec[1:2, :], a)
    for part in range(3):
        for j in range(0, D, NB):
            o = part * D + j
            r = mm(a[...], wqkv[:, o : o + NB], NN)
            if part == 0:
                r = r + vec[2:3, j : j + NB]
            if part == 2:
                r = r + vec[3:4, j : j + NB]
            qkv[:, o : o + NB] = r.astype(BF16)
    done("qkv")
    lanes = lax.broadcasted_iota(jnp.int32, (tile, 128), 1)
    low = lanes < HEAD
    together = 2
    for i in range(tokens // tile):
        rows = slice(i * tile, (i + 1) * tile)
        seen = (i + 1) * tile
        logs = jnp.zeros((tile, 128), F32)
        for first in range(0, HEADS // 2, together):
            jobs = [(p, half) for p in range(first, first + together) for half in range(2)]
            scores = []
            for p, half in jobs:
                q = qkv[rows, 128 * p : 128 * p + 128] * BF16(HEAD**-0.5)
                k = qkv[0:seen, D + 128 * p : D + 128 * p + 128]
                own = low if half == 0 else ~low
                scores.append(mm(jnp.where(own, q, BF16(0)), k, NT) + mask[rows, 0:seen])
            tops = [jnp.max(x, -1, keepdims=True) for x in scores]
            expo = [jnp.exp(x - top) for x, top in zip(scores, tops)]
            dens = [jnp.sum(x, -1, keepdims=True) for x in expo]
            outs = []
            for (p, half), x, den, top in zip(jobs, expo, dens, tops):
                v = qkv[0:seen, 2 * D + 128 * p : 2 * D + 128 * p + 128]
                outs.append(mm(x.astype(BF16), v, NN) / den)
                logs = jnp.where(lanes == 2 * p + half, top + jnp.log(den), logs)
            for n, (p, half) in enumerate(jobs):
                if half == 1:
                    mixed[rows, 128 * p : 128 * p + 128] = jnp.where(low, outs[n - 1], outs[n]).astype(BF16)
        lse[rows, :] = logs
    done("mixed")


def out_forward(h, mixed, wout, vec, h_mid):
    for j in range(0, D, NB):
        r = mm(mixed[...], wout[:, j : j + NB], NN)
        h_mid[:, j : j + NB] = h[:, j : j + NB].astype(F32) + r + vec[4:5, j : j + NB]


def fc_forward(h_mid, wfc, vec, fb, c, g, gp, done=None):
    done = done or (lambda j: None)
    norm_forward(h_mid, vec[5:6, :], vec[6:7, :], c)
    for j in range(0, FF, NB):
        f = mm(c[...], wfc[:, j : j + NB], NN) + fb[0:1, j : j + NB]
        sq = f * f
        t = jnp.tanh(GELU_A * (f + GELU_B * sq * f))
        half = 0.5 * (1.0 + t)
        g[:, j : j + NB] = (f * half).astype(BF16)
        slope = half + (0.5 * GELU_A) * f * (1.0 - t * t) * (1.0 + (3 * GELU_B) * sq)
        gp[:, j : j + NB] = slope.astype(BF16)
        done(j + NB)


def proj_forward(h_mid, g, wpt, vec, h_out):
    for j in range(0, D, NB):
        r = mm(g[...], wpt[j : j + NB, :], NT)
        h_out[:, j : j + NB] = h_mid[:, j : j + NB] + r + vec[7:8, j : j + NB]


def norm_backward(dout, x, gain, base, store):
    sums = [jnp.zeros((8, x.shape[1]), F32) for _ in range(3)]
    for i in range(0, x.shape[0], LN_ROWS):
        rows = slice(i, i + LN_ROWS)
        xhat, inv = norm_stats(x[rows, :].astype(F32))
        d = dout[rows, :]
        sums[0] += fold(d * xhat)
        sums[1] += fold(d)
        dx = d * gain
        m1 = jnp.mean(dx, -1, keepdims=True)
        m2 = jnp.mean(dx * xhat, -1, keepdims=True)
        total = base[rows, :] + inv * (dx - m1 - xhat * m2)
        sums[2] += fold(total)
        store(rows, total)
    return [colsum(x) for x in sums]


def ffn_backward(
    dy, h_mid, gp, wfc, wpt, vec, dy_low, df_low, dfb, dh_mid, dh_low, dvec, dc, use=None, done=None
):
    use = use or (lambda which, j=0: None)
    done = done or (lambda which: None)
    d_out = dy[...]
    dy_low[...] = d_out.astype(BF16)
    dvec[0:4, :] = jnp.zeros((4, D), F32)
    dvec[7:8, :] = colsum(d_out)
    for j in range(0, FF, NB):
        use("hidden", j)
        d = mm(dy_low[...], wpt[:, j : j + NB], NN)
        df = d * gp[:, j : j + NB].astype(F32)
        dfb[0:1, j : j + NB] = colsum(df)
        df_low[:, j : j + NB] = df.astype(BF16)
    done("df")
    for j in range(0, D, NB):
        use("wfc", j)
        dc[:, j : j + NB] = mm(df_low[...], wfc[j : j + NB, :], NT)
    use("h_mid")

    def store(rows, total):
        dh_mid[rows, :] = total
        dh_low[rows, :] = total.astype(BF16)

    dvec[5:6, :], dvec[6:7, :], dvec[4:5, :] = norm_backward(dc, h_mid, vec[5:6, :], dy, store)


def attention_backward(
    dh_mid, dh_low, h, qkv, lse, mixed, mask, wqkv, wout, vec, dmix, dqkv, da, d_in, dvec,
    use=None, done=None,
):
    use = use or (lambda which: None)
    done = done or (lambda which: None)
    tokens = h.shape[0]
    use("wout")
    use("dh_low")
    for j in range(0, D, NB):
        dmix[:, j : j + NB] = mm(dh_low[...], wout[j : j + NB, :], NT).astype(BF16)
    use("qkv")
    use("mixed")
    use("lse")
    tile = 256
    low = lax.broadcasted_iota(jnp.int32, (tokens, 128), 1) < HEAD
    low_rows = lax.broadcasted_iota(jnp.int32, (128, tokens), 0) < HEAD
    for p in range(HEADS // 2):
        c = 128 * p
        cs = slice(c, c + 128)
        q = qkv[:, cs] * BF16(HEAD**-0.5)
        k = qkv[:, D + c : D + c + 128]
        v = qkv[:, 2 * D + c : 2 * D + c + 128]
        dm = dmix[:, cs]
        prod = dm.astype(F32) * mixed[:, cs].astype(F32)
        dm_t = dm.astype(F32).T.astype(BF16)
        q_t = q.astype(F32).T.astype(BF16)
        masks = ((low, low_rows), (~low, ~low_rows))
        deltas = [jnp.sum(jnp.where(own, prod, 0.0), -1, keepdims=True) for own, _ in masks]
        q_own = [jnp.where(own, q, BF16(0)) for own, _ in masks]
        k_own = [jnp.where(own, k, BF16(0)) for own, _ in masks]
        dm_own = [jnp.where(own, dm, BF16(0)) for own, _ in masks]
        dm_t_own = [jnp.where(own, dm_t, BF16(0)) for _, own in masks]
        q_t_own = [jnp.where(own, q_t, BF16(0)) for _, own in masks]
        dq, dk_t, dv_t = [], [], []
        for i in range(tokens // tile):
            rows, seen = slice(i * tile, (i + 1) * tile), (i + 1) * tile
            scores = [mm(x[rows], k[0:seen], NT) + mask[rows, 0:seen] for x in q_own]
            probs = [jnp.exp(x - lse[rows, 2 * p + n : 2 * p + n + 1]) for n, x in enumerate(scores)]
            dps = [mm(x[rows], v[0:seen], NT) for x in dm_own]
            ds = [(x * (y - z[rows])).astype(BF16) for x, y, z in zip(probs, dps, deltas)]
            dv_t.append(sum(mm(x[:, rows], y.astype(BF16), NN) for x, y in zip(dm_t_own, probs)))
            dk_t.append(sum(mm(x[:, rows], y, NN) for x, y in zip(q_t_own, ds)))
            dq.append(sum(mm(x, y[0:seen], NN) for x, y in zip(ds, k_own)))

        def joined(parts):
            cols = []
            for n in range(len(parts)):
                cols.append(sum(part[:, n * tile : (n + 1) * tile] for part in parts[n:]))
            return jnp.concatenate(cols, 1)

        dq = jnp.concatenate(dq, 0) * HEAD**-0.5
        dv = joined(dv_t).T
        dk = joined(dk_t).T
        dvec[2:3, cs] = colsum(dq)
        dvec[3:4, cs] = colsum(dv)
        dqkv[:, cs] = dq.astype(BF16)
        dqkv[:, D + c : D + c + 128] = dk.astype(BF16)
        dqkv[:, 2 * D + c : 2 * D + c + 128] = dv.astype(BF16)
    done("dqkv")
    use("wqkv")
    for j in range(0, D, NB):
        da[:, j : j + NB] = mm(dqkv[...], wqkv[j : j + NB, :], NT)
    use("h")
    use("dh_mid")

    def store(rows, total):
        d_in[rows, :] = total

    dvec[0:1, :], dvec[1:2, :], _ = norm_backward(da, h, vec[0:1, :], dh_mid, store)
    dvec[4:8, :] = jnp.zeros((4, D), F32)


def attention_forward_call(ends, h, wqkv, vec):
    t = h.shape[0]
    outs = [like((t, D), BF16), like((t, 3 * D), BF16), like((t, 128), F32), like((t, D), BF16)]

    def body(ends, h, wqkv, vec, a, qkv, lse, mixed, mask):
        fill_mask(ends, mask)
        attention_forward(h, wqkv, vec, mask, a, qkv, lse, mixed)

    return kernel_call(body, outs, [SM, VM, VM, VM], [pltpu.VMEM((t, t), F32)], us=13)(ends, h, wqkv, vec)


def fc_forward_call(h, mixed, wout, wfc, vec, fb):
    t = h.shape[0]
    outs = [like((t, D), F32), like((t, D), BF16), like((t, FF), BF16), like((t, FF), BF16)]

    def body(h, mixed, wout, wfc, vec, fb, mid, c, g, gp):
        out_forward(h, mixed, wout, vec, mid)
        fc_forward(mid, wfc, vec, fb, c, g, gp)

    return kernel_call(body, outs, [VM] * 6, us=9)(h, mixed, wout, wfc, vec, fb)


def ffn_backward_call(dy, h_mid, gp, wfc, wpt, vec):
    t = dy.shape[0]
    outs = [
        like((t, FF), BF16),
        like((1, FF), F32),
        like((t, D), F32),
        like((t, D), BF16),
        like((8, D), F32),
    ]

    def body(dy, h_mid, gp, wfc, wpt, vec, df_low, dfb, dh_mid, dh_low, dvec, dy_low, dc):
        ffn_backward(dy, h_mid, gp, wfc, wpt, vec, dy_low, df_low, dfb, dh_mid, dh_low, dvec, dc)

    scratch = [pltpu.VMEM((t, D), BF16), pltpu.VMEM((t, D), F32)]
    return kernel_call(body, outs, [VM] * 6, scratch, us=13)(dy, h_mid, gp, wfc, wpt, vec)


def attention_backward_call(ends, dh_mid, dh_low, h, qkv, lse, mixed, wqkv, wout, vec):
    t = h.shape[0]

    def body(
        ends, dh_mid, dh_low, h, qkv, lse, mixed, wqkv, wout, vec, dqkv, d_in, dvec, mask, dmix, da
    ):
        fill_mask(ends, mask)
        attention_backward(
            dh_mid, dh_low, h, qkv, lse, mixed, mask, wqkv, wout, vec, dmix, dqkv, da, d_in, dvec
        )

    outs = [like((t, 3 * D), BF16), like((t, D), F32), like((8, D), F32)]
    scratch = [pltpu.VMEM((t, t), F32), pltpu.VMEM((t, D), BF16), pltpu.VMEM((t, D), F32)]
    return kernel_call(body, outs, [SM] + [VM] * 9, scratch, us=18)(
        ends, dh_mid, dh_low, h, qkv, lse, mixed, wqkv, wout, vec
    )


class Cube:
    def __init__(self, groups, rows):
        self.groups, self.rows = groups, rows
        self.n = groups * rows
        self.bits = self.n.bit_length() - 1
        far = list(range(self.bits - 1, 2, -1))
        self.gather_plans = (far + [2, 1], far + [1, 2])
        self.mixed_plans = ([2] + far + [1], [1] + far + [2])
        self.scatter_plans = tuple(list(reversed(p)) for p in self.gather_plans)
        self.half = self.n // 2

    def swap(self, x, plans, step):
        pairs = [(i, i ^ (1 << plans[i & 1][step])) for i in range(self.n)]
        return lax.ppermute(x, BOTH, pairs)

    def swap_core(self, x):
        return lax.ppermute(x, BOTH, [(i, i ^ 1) for i in range(self.n)])

    def gather_swap(self, held, step, plans=None):
        return self.swap(held, plans or self.gather_plans, step)

    def gather_steps(self, held, first, end, plans=None):
        for step in range(first, end):
            held = jnp.concatenate([held, self.gather_swap(held, step, plans)], 0)
        return held

    def scatter_swap(self, halves, step):
        return self.swap(halves[1], self.scatter_plans, step)

    def scatter_add(self, keep, got):
        mid = keep.shape[0] // 2
        if mid == 0:
            return (keep + got)[0]
        return keep[:mid] + got[:mid], keep[mid:] + got[mid:]

    def scatter_steps(self, halves, first, end):
        for step in range(first, end):
            halves = self.scatter_add(halves[0], self.scatter_swap(halves, step))
        return halves

    def gather_source(self, me, side, slot, plans):
        core = (me & 1) ^ side
        dest = me ^ side
        for k in range(self.bits - 1):
            if (slot >> k) & 1:
                flip0, flip1 = 1 << plans[0][k], 1 << plans[1][k]
                dest = dest ^ jnp.where(core == 1, flip1, flip0)
        return dest

    def scatter_slot(self, me, dest):
        rel = me ^ dest
        core = dest & 1
        slot = 0
        for k in range(self.bits - 1):
            place = self.bits - 2 - k
            b0 = (rel >> self.scatter_plans[0][k]) & 1
            b1 = (rel >> self.scatter_plans[1][k]) & 1
            slot = slot + (jnp.where(core == 1, b1, b0) << place)
        return slot

    def row_of(self, me, side, pair):
        return 2 * pair + ((me & 1) ^ side)


lock = lax.optimization_barrier


def my_number(cube):
    return lax.axis_index("grp") * cube.rows + lax.axis_index("row")


def canonical(cube, pieces, plans):
    me = my_number(cube)
    ids = [cube.gather_source(me, side, s, plans) for side in (0, 1) for s in range(cube.half)]
    blocks = jnp.concatenate(pieces, 0)
    return jnp.zeros_like(blocks).at[jnp.stack(ids)].set(blocks)


def fits(rows, cols):
    return rows % 16 == 0 and cols % 128 == 0


def place_blocks(cube, pieces, plans, sem, *targets):
    me = my_number(cube)
    part = cube.half // 2
    copies = []
    for i, piece in enumerate(pieces):
        for s in range(part):
            dev = cube.gather_source(me, i // 2, (i % 2) * part + s, plans)
            for target in targets:
                rows, place = target(dev // cube.rows, dev % cube.rows)
                copies.append(pltpu.make_async_copy(piece.at[s, rows], place, sem))
    for cp in copies:
        cp.start()

    def wait():
        for cp in copies:
            cp.wait()

    return wait


def tiled(x, n):
    r, c = x.shape[-2] // 4, x.shape[-1] // n
    x = x.reshape(x.shape[:-2] + (4, r, n, c))
    return jnp.moveaxis(x, (-4, -2), (-2, -4)).reshape(x.shape[:-4] + (n * r, 4 * c))


def untiled(x, n):
    r, c = x.shape[-2] // n, x.shape[-1] // 4
    x = x.reshape(x.shape[:-2] + (n, r, 4, c))
    return jnp.moveaxis(x, (-4, -2), (-2, -4)).reshape(x.shape[:-4] + (4 * r, n * c))


def copy_tiles(src, dst, n, r, c, src_at=(0, 0), dst_at=(0, 0), to_wide=True):
    for i in range(4):
        for j in range(n):
            p, q = ((i, j), (j, i)) if to_wide else ((j, i), (i, j))
            rows = slice(src_at[0] + p[0] * r, src_at[0] + (p[0] + 1) * r)
            cols = slice(src_at[1] + p[1] * c, src_at[1] + (p[1] + 1) * c)
            rows_to = slice(dst_at[0] + q[0] * r, dst_at[0] + (q[0] + 1) * r)
            cols_to = slice(dst_at[1] + q[1] * c, dst_at[1] + (q[1] + 1) * c)
            dst[rows_to, cols_to] = src[rows, cols]


def blocks_of(cube, pieces, plans):
    return canonical(cube, pieces, plans).reshape((cube.groups, cube.rows) + pieces[0].shape[1:])


def unblocked(x):
    g_n, r_n, br, bc = x.shape
    return x.transpose(1, 2, 0, 3).reshape(r_n * br, g_n * bc)


def blocked(x, g_n, r_n):
    return x.reshape(r_n, x.shape[0] // r_n, g_n, x.shape[1] // g_n).transpose(2, 0, 1, 3)


def proj_full(cube, pieces):
    br, bc = pieces[0].shape[1:]
    full = blocks_of(cube, pieces, cube.mixed_plans)
    return full.transpose(0, 2, 1, 3).reshape(cube.groups * br, cube.rows * bc)


def attn_full(cube, pieces, sizes):
    tr, tc, vrows, vcols, bias = sizes
    full = blocks_of(cube, pieces, cube.gather_plans)
    wqkv = unblocked(untiled(full[:, :, : 3 * tr], 3))
    ext = full[:, :, 3 * tr :].astype(F32)
    vec = unblocked(ext[:, :, :vrows, :vcols])
    fb = ext[:, :, vrows, :bias].reshape(1, cube.n * bias)
    total = jnp.sum(ext[:, :, vrows + 1, 0]) * 16.0 + jnp.sum(ext[:, :, vrows + 1, 1])
    return wqkv, vec, fb, jnp.full((8, 128), total, F32)


def open_attention(cube, ends, h, pieces, sizes):
    br, bc = pieces[0].shape[1:]
    if not fits(br, bc):
        full = attn_full(cube, pieces, sizes)
        return full, attention_forward_call(ends, h, *full[:2])
    tr, tc, vrows, vcols, bias = sizes
    g_n, r_n = cube.groups, cube.rows
    t = h.shape[0]

    def body(ends, h, p0, p1, p2, p3, wqkv, vec, fb, tot, a, qkv, lse, mixed, mask, blk, sem):
        def target(g, r):
            return slice(None), blk.at[g, r]

        wait = place_blocks(cube, (p0, p1, p2, p3), cube.gather_plans, sem, target)
        fill_mask(ends, mask)
        wait()
        count = jnp.zeros((1, 128), F32)
        for g in range(g_n):
            for r in range(r_n):
                copy_tiles(
                    blk.at[g, r], wqkv.ref, 3, tr, tc, dst_at=(r * 4 * tr, g * 3 * tc), to_wide=False
                )
                ext = blk[g, r, 3 * tr : br, :].astype(F32)
                vec[r * vrows : (r + 1) * vrows, g * vcols : (g + 1) * vcols] = ext[0:vrows, 0:vcols]
                at = (g * r_n + r) * bias
                fb[0:1, at : at + bias] = ext[vrows : vrows + 1, 0:bias]
                count += ext[vrows + 1 : vrows + 2, 0:128]
        lane = lax.broadcasted_iota(jnp.int32, (1, 128), 1)
        weight = jnp.where(lane == 0, 16.0, jnp.where(lane == 1, 1.0, 0.0))
        tot[...] = jnp.broadcast_to(jnp.sum(count * weight, -1, keepdims=True), (8, 128))
        wqkv.flush()
        whole = {"qkv": (a, qkv), "mixed": ()}
        attention_forward(
            h, wqkv.ref, vec, mask, a.ref, qkv.ref, lse, mixed,
            done=lambda which: [x.flush() for x in whole[which]],
        )

    outs = [
        ((D, 3 * D), BF16, "flush"),
        ((8, D), F32, "vmem"),
        ((1, FF), F32, "vmem"),
        ((8, 128), F32, "vmem"),
        ((t, D), BF16, "flush"),
        ((t, 3 * D), BF16, "flush"),
        ((t, 128), F32, "vmem"),
        ((t, D), BF16, "vmem"),
    ]
    scratch = [
        pltpu.VMEM((t, t), F32),
        pltpu.VMEM((g_n, r_n, br, bc), BF16),
        pltpu.SemaphoreType.DMA,
    ]
    ins = [(ends, "smem"), (h, "vmem")] + [(x, "any") for x in pieces]
    got = staged_call(body, ins, outs, scratch, us=15)
    return got[:4], got[4:]


def open_fc(cube, h, mixed, pieces, vec, fb, sizes):
    br, bc = pieces[0].shape[1:]
    tr, tc = sizes[:2]
    t = h.shape[0]
    if not fits(br, bc):
        full = blocks_of(cube, pieces, cube.gather_plans)
        wfc, wout = unblocked(full[:, :, : 4 * tr]), unblocked(untiled(full[:, :, 4 * tr :], 1))
        return (wfc, wout), fc_forward_call(h, mixed, wout, wfc, vec, fb)

    def body(h, mixed, p0, p1, p2, p3, vec, fb, wfc, wout, mid, c, g, gp, blk, sem):
        def target_fc(g, r):
            rows, cols = pl.multiple_of(r * 4 * tr, 16), pl.multiple_of(g * bc, 128)
            return pl.ds(0, 4 * tr), wfc.ref.at[pl.ds(rows, 4 * tr), pl.ds(cols, bc)]

        def target_out(g, r):
            return pl.ds(4 * tr, tr), blk.at[g, r]

        place_blocks(cube, (p0, p1, p2, p3), cube.gather_plans, sem, target_fc, target_out)()
        wfc.flush()
        for g_i in range(cube.groups):
            for r in range(cube.rows):
                copy_tiles(
                    blk.at[g_i, r], wout.ref, 1, tr, tc, dst_at=(r * 4 * tr, g_i * tc), to_wide=False
                )
        wout.flush()
        out_forward(h, mixed, wout.ref, vec, mid.ref)
        mid.flush()

        def done(end):
            if end % D == 0:
                for x in (g, gp):
                    x.flush(slice(None), pl.ds(end - D, D))

        fc_forward(mid.ref, wfc.ref, vec, fb, c.ref, g.ref, gp.ref, done)
        c.flush()

    ins = [(h, "vmem"), (mixed, "vmem")] + [(x, "any") for x in pieces] + [(vec, "vmem"), (fb, "vmem")]
    outs = [
        ((D, FF), BF16, "flush"),
        ((D, D), BF16, "flush"),
        ((t, D), F32, "flush"),
        ((t, D), BF16, "flush"),
        ((t, FF), BF16, "flush", FF // D),
        ((t, FF), BF16, "flush", FF // D),
    ]
    scratch = [pltpu.VMEM((cube.groups, cube.rows, tr, bc), BF16), pltpu.SemaphoreType.DMA]
    got = staged_call(body, ins, outs, scratch, us=12)
    return got[:2], got[2:]


def second_pass(cube, ends, passes, mid0, g0, pieces, cot, wqkv, wout, wfc, vec, fb):
    br, bc = pieces[0].shape[1:]
    t = cot.shape[0]
    whole = fits(br, bc)
    if not whole:
        pieces = (proj_full(cube, pieces),)
    n_p = len(pieces)

    def body(*refs):
        ends, passes, mid0, g0 = refs[:4]
        src = refs[4 : 4 + n_p]
        cot, wqkv, wout, wfc, vec, fb = refs[4 + n_p : 10 + n_p]
        wpt, hidden, d1, a, mixed, c, dqkv, dhl, df, dvec, dfb = refs[10 + n_p : 21 + n_p]
        grad0, grad1 = refs[21 + n_p : 23 + n_p]
        mask, qkv, lse, mid, g, gp, dy, dyl, tmp, dhm, dmix, dvec2, dyt, h1, sem = refs[23 + n_p :]
        grad = wfc.ref
        me = my_number(cube)

        def target(g, r):
            rows, cols = pl.multiple_of(g * br, 16), pl.multiple_of(r * bc, 128)
            return slice(None), wpt.ref.at[pl.ds(rows, br), pl.ds(cols, bc)]

        if whole:
            wait = place_blocks(cube, src, cube.mixed_plans, sem, target)
        else:
            copy = pltpu.make_async_copy(src[0], wpt.ref, sem)
            copy.start()
            wait = copy.wait
        for x in (vec, fb, g0, mid0):
            x.start()
        vec, fb = vec.get(), fb.get()
        fill_mask(ends, mask)
        wait()
        g0.get()
        mid0.get()
        wqkv.start()
        wout.start()
        proj_forward(mid0.ref, g0.ref, wpt.ref, vec, h1)
        wqkv.get()
        wout.get()
        wfc.start()
        cot.start()
        attention_forward(
            h1, wqkv.ref, vec, mask, a.ref, qkv, lse, mixed.ref,
            done=lambda which: {"qkv": a, "mixed": mixed}[which].flush(),
        )
        out_forward(h1, mixed.ref, wout.ref, vec, mid)
        wfc.get()
        wpt.flush()
        fc_forward(mid, wfc.ref, vec, fb, c.ref, g, gp)
        c.flush()
        proj_forward(mid, g, wpt.ref, vec, dy)
        active = passes[0] > 1
        hidden.ref[...] = jnp.where(active, dy[...], h1[...]).astype(BF16)
        hidden.flush()
        valid = lax.broadcasted_iota(jnp.int32, (t, 1), 0) < ends[0, ends.shape[1] - 1]
        cot.get()
        dy[...] = jnp.where(valid & active, cot.ref[...].astype(F32), 0.0)
        ffn_backward(
            dy, mid, gp, wfc.ref, wpt.ref, vec, dyl, df.ref, dfb.ref, dhm, dhl.ref, dvec2, tmp,
            done=lambda which: df.flush(),
        )
        dhl.flush()
        attention_backward(
            dhm, dhl.ref, h1, qkv, lse, mixed.ref, mask, wqkv.ref, wout.ref, vec,
            dmix, dqkv.ref, tmp, dy, dvec.ref, done=lambda which: dqkv.flush(),
        )
        dvec.ref[...] += dvec2[...]
        dvec.flush()
        dfb.flush()
        d1.ref[...] = jnp.where(active, dy[...], jnp.where(valid, cot.ref[...].astype(F32), 0.0))
        d1.flush()
        dyt[:, 0:t] = dyl[...].astype(F32).T.astype(BF16)
        dyt[:, t : 2 * t] = d1.ref[...].T.astype(BF16)
        if not whole:
            grad0[...] = mm(dyt[:, 0:t], g[...], NN) + mm(dyt[:, t : 2 * t], g0.ref[...], NN)
            return
        n = 0
        for side, out in ((1, grad1), (0, grad0)):
            for pair in range(cube.rows // 2):
                r = cube.row_of(me, side, pair)
                cols = pl.ds(pl.multiple_of(r * bc, 128), bc)
                both = mm(dyt[:, 0:t], g[:, cols], NN) + mm(dyt[:, t : 2 * t], g0.ref[:, cols], NN)
                grad[:, n * bc : (n + 1) * bc] = both.astype(BF16)
                for group in range(cube.groups):
                    block = grad.at[pl.ds(group * br, br), pl.ds(n * bc, bc)]
                    out.put(block, cube.scatter_slot(me, group * cube.rows + r))
                n += 1

    ins = [(ends, "smem"), (passes, "smem"), (mid0, "fetch"), (g0, "fetch")]
    ins += [(x, "any") for x in pieces]
    ins += [(x, "fetch") for x in (cot, wqkv, wout, wfc, vec, fb)]
    outs = [
        ((D, FF), BF16, "flush"),
        ((t, D), BF16, "flush"),
        ((t, D), F32, "flush"),
        ((t, D), BF16, "flush"),
        ((t, D), BF16, "flush"),
        ((t, D), BF16, "flush"),
        ((t, 3 * D), BF16, "flush"),
        ((t, D), BF16, "flush"),
        ((t, FF), BF16, "flush"),
        ((8, D), F32, "flush"),
        ((1, FF), F32, "flush"),
    ]
    if whole:
        outs += [((cube.half, br, bc), BF16, "sink", cube.half)] * 2
    else:
        outs += [((D, FF), F32, "vmem"), ((8, 128), F32, "vmem")]
    scratch = [
        pltpu.VMEM((t, t), F32),
        pltpu.VMEM((t, 3 * D), BF16),
        pltpu.VMEM((t, 128), F32),
        pltpu.VMEM((t, D), F32),
        pltpu.VMEM((t, FF), BF16),
        pltpu.VMEM((t, FF), BF16),
        pltpu.VMEM((t, D), F32),
        pltpu.VMEM((t, D), BF16),
        pltpu.VMEM((t, D), F32),
        pltpu.VMEM((t, D), F32),
        pltpu.VMEM((t, D), BF16),
        pltpu.VMEM((8, D), F32),
        pltpu.VMEM((D, 2 * t), BF16),
        pltpu.VMEM((t, D), F32),
        pltpu.SemaphoreType.DMA,
    ]
    got = staged_call(body, ins, outs, scratch, us=50)
    slots = got[11:]
    if not whole:
        full = slots[0].astype(BF16).reshape(cube.groups, br, cube.rows, bc).transpose(0, 2, 1, 3)
        slots = ordered_slots(cube, full.reshape(cube.n, br, bc))
    return got[:11], slots


def pack(w_qkv, w_out, w_fc, vectors, fc_bias, seg_ends, sizes):
    tr, tc, vrows, vcols, bias = sizes
    wide = 4 * tc

    def extra(vec, fb, n_valid):
        lane = lax.broadcasted_iota(jnp.int32, (1, wide), 1)
        n_high = n_valid // 16
        count = jnp.where(lane == 0, n_high, jnp.where(lane == 1, n_valid - 16 * n_high, 0))
        rows = [
            jnp.concatenate([vec.astype(F32), jnp.zeros((vrows, wide - vcols), F32)], 1),
            jnp.concatenate([fb.astype(F32), jnp.zeros((1, wide - bias), F32)], 1),
            count.astype(F32),
            jnp.zeros((EXTRA - vrows - 2, wide), F32),
        ]
        return jnp.concatenate(rows, 0).astype(BF16)

    if not fits(tr, wide):
        ext = extra(vectors, fc_bias[None], seg_ends[0, -1])
        return (
            jnp.concatenate([tiled(w_qkv, 3), ext], 0),
            jnp.concatenate([w_fc, tiled(w_out, 1)], 0),
        )

    def body(wq, wo, wf, vec, fb, ends, out_a, out_f):
        copy_tiles(wq, out_a, 3, tr, tc)
        out_a[3 * tr : 3 * tr + EXTRA, :] = extra(vec[...], fb[...], ends[0, ends.shape[1] - 1])
        out_f[0 : 4 * tr, :] = wf[...]
        copy_tiles(wo, out_f, 1, tr, tc, dst_at=(4 * tr, 0))

    outs = [like((3 * tr + EXTRA, wide), BF16), like((5 * tr, wide), BF16)]
    return kernel_call(body, outs, [VM] * 5 + [SM], us=2)(
        w_qkv, w_out, w_fc, vectors, fc_bias[None], seg_ends
    )


def ordered_slots(cube, blocks):
    me = my_number(cube)
    order = [cube.scatter_slot(me, dest) + cube.half * ((me ^ dest) & 1) for dest in range(cube.n)]
    slots = jnp.zeros_like(blocks).at[jnp.stack(order)].set(blocks)
    return slots[: cube.half], slots[cube.half :]


def stacked_t(parts, out):
    t = parts[0].shape[0]
    for i, part in enumerate(parts):
        out[:, i * t : (i + 1) * t] = part[...].astype(F32).T.astype(BF16)


def side_rows(cube, me, side, src, out, height):
    for pair in range(cube.rows // 2):
        r = cube.row_of(me, side, pair)
        out[pair * height : (pair + 1) * height, :] = src[pl.ds(pl.multiple_of(r * height, 16), height), :]


def ffn_grad_side(cube, me, side, sizes, operands, lt, lhs, grad, wide, blocks, out):
    m1, m0, dh1, dh0, c1, c0, df1, df0 = operands
    tr, tc = sizes[:2]
    bc = 4 * tc
    t = lt.shape[1] // 2
    pairs = cube.rows // 2
    stacked_t((m1(), m0()), lt)
    side_rows(cube, me, side, lt, lhs, 4 * tr)
    dh1, dh0 = dh1(), dh0()
    for j in range(0, D, NB):
        cols = slice(j, j + NB)
        both = mm(lhs[:, 0:t], dh1[:, cols], NN) + mm(lhs[:, t : 2 * t], dh0[:, cols], NN)
        wide[:, cols] = both.astype(BF16)
    for g in range(cube.groups):
        for pair in range(pairs):
            copy_tiles(wide, blocks.at[g * pairs + pair], 1, tr, tc, src_at=(pair * 4 * tr, g * tc))
    stacked_t((c1(), c0()), lt)
    side_rows(cube, me, side, lt, lhs, 4 * tr)
    df1, df0 = df1(), df0()
    for first in range(0, cube.groups, 2):
        cols = slice(first * bc, (first + 2) * bc)
        both = mm(lhs[:, 0:t], df1[:, cols], NN) + mm(lhs[:, t : 2 * t], df0[:, cols], NN)
        grad[:, cols] = both.astype(BF16)
        for g in (first, first + 1):
            for pair in range(pairs):
                slot = cube.scatter_slot(me, g * cube.rows + cube.row_of(me, side, pair))
                rows = pl.ds(pair * 4 * tr, 4 * tr)
                out.put(grad.at[rows, pl.ds(g * bc, bc)], slot, pl.ds(0, 4 * tr))
                out.put(blocks.at[g * pairs + pair], slot, pl.ds(4 * tr, tr))


def ffn_grad_scratch(cube, sizes, t):
    tr, tc = sizes[:2]
    return [
        pltpu.VMEM((D, 2 * t), BF16),
        pltpu.VMEM((D // 2, 2 * t), BF16),
        pltpu.VMEM((D // 2, FF), BF16),
        pltpu.VMEM((D // 2, D), BF16),
        pltpu.VMEM((cube.half, tr, 4 * tc), BF16),
    ]


def ffn_backward_and_grad(cube, dy, h_mid, gp, wfc, wpt, vec, c1, c0, df1, m1, m0, dh1, sizes):
    t = dy.shape[0]
    tr, tc = sizes[:2]
    br, bc = 5 * tr, 4 * tc
    if not fits(br, bc):
        df0, *rest = ffn_backward_call(dy, h_mid, gp, wfc, wpt, vec)
        dfc = blocked(mm(c1, df1, TN) + mm(c0, df0, TN), cube.groups, cube.rows)
        dout = blocked(mm(m1, dh1, TN) + mm(m0, rest[2], TN), cube.groups, cube.rows)
        full = jnp.concatenate([dfc, tiled(dout, 1)], 2).astype(BF16)
        keep, send = ordered_slots(cube, full.reshape(cube.n, br, bc))
        return rest, send, keep

    def body(
        dy, h_mid, gp, wfc, wpt, vec, c1, c0, df1, m1, m0, dh1, dfb, dh_mid, dh_low, dvec, df0, send,
        dy_low, dc, *scratch,
    ):
        me = my_number(cube)
        order = {"dy": dy, "wpt": wpt, "gp": gp, "wfc": wfc, "h_mid": h_mid}
        for x in (vec, dy, wpt, gp):
            x.start()

        def use(which, j=0):
            if which == "hidden":
                if j == 0:
                    wpt.get()
                    wfc.start()
                    h_mid.start()
                if j == FF // 2:
                    for x in (m1, m0, dh1, c1, c0, df1):
                        x.start()
                gp.get(j // (FF // 4) + 1)
            else:
                order[which].get()
                vec.get()

        ffn_backward(
            dy.get(), h_mid.ref, gp.ref, wfc.ref, wpt.ref, vec.ref, dy_low, df0.ref, dfb.ref, dh_mid.ref,
            dh_low.ref, dvec.ref, dc, use=use, done=lambda which: df0.flush(),
        )
        for x in (dh_mid, dh_low, dvec, dfb):
            x.flush()
        operands = (m1.get, m0.get, dh1.get, lambda: dh_low.ref, c1.get, c0.get, df1.get, lambda: df0.ref)
        ffn_grad_side(cube, me, 1, sizes, operands, *scratch, send)

    ins = [
        (dy, "fetch"), (h_mid, "fetch"), (gp, "fetch", 1, 4), (wfc, "fetch"), (wpt, "fetch"), (vec, "fetch"),
        (c1, "fetch"), (c0, "fetch"), (df1, "fetch"), (m1, "fetch"), (m0, "fetch"), (dh1, "fetch"),
    ]
    outs = [
        ((1, FF), F32, "flush"),
        ((t, D), F32, "flush"),
        ((t, D), BF16, "flush"),
        ((8, D), F32, "flush"),
        ((t, FF), BF16, "flush"),
        ((cube.half, br, bc), BF16, "sink", 2 * cube.half),
    ]
    scratch = [pltpu.VMEM((t, D), BF16), pltpu.VMEM((t, D), F32)] + ffn_grad_scratch(cube, sizes, t)
    got = staged_call(body, ins, outs, scratch, us=18)
    return got[:4], got[5], (m1, m0, dh1, got[2], c1, c0, df1, got[4])


def ffn_grad_keep(cube, operands, sizes):
    tr, tc = sizes[:2]
    br, bc = 5 * tr, 4 * tc
    if not fits(br, bc):
        return operands
    t = operands[0].shape[0]

    def body(*refs):
        given, keep, scratch = refs[:8], refs[8], refs[9:]
        for x in given:
            x.start()
        ffn_grad_side(cube, my_number(cube), 0, sizes, [x.get for x in given], *scratch, keep)

    ins = [(x, "fetch") for x in operands]
    outs = [((cube.half, br, bc), BF16, "sink", 2 * cube.half)]
    return staged_call(body, ins, outs, ffn_grad_scratch(cube, sizes, t), us=8)[0]


def attention_grad_side(cube, me, side, sizes, operands, lt, lhs, wide, blocks, out):
    a1, a0, dq1, dq0, dvec, dfb = operands
    tr, tc, vrows, vcols, bias = sizes
    br, bc = 3 * tr + EXTRA, 4 * tc
    g_n, pairs = cube.groups, cube.rows // 2
    t = lt.shape[1] // 2
    stacked_t((a1(), a0()), lt)
    side_rows(cube, me, side, lt, lhs, 4 * tr)
    dq1, dq0 = dq1(), dq0()
    for j in range(0, 3 * D, NB):
        cols = slice(j, j + NB)
        full = mm(lhs[:, 0:t], dq1[:, cols], NN) + mm(lhs[:, t : 2 * t], dq0[:, cols], NN)
        wide[:, cols] = full.astype(BF16)
    dvec, dfb = dvec(), dfb()

    def extra(g, r):
        vecs = dvec[r * vrows : (r + 1) * vrows, g * vcols : (g + 1) * vcols]
        at = (g * cube.rows + r) * bias
        rows = [
            jnp.concatenate([vecs, jnp.zeros((vrows, bc - vcols), F32)], 1),
            jnp.concatenate([dfb[0:1, at : at + bias], jnp.zeros((1, bc - bias), F32)], 1),
            jnp.zeros((EXTRA - vrows - 1, bc), F32),
        ]
        return jnp.concatenate(rows, 0)

    first = ((me & 1) ^ side) == 0
    for g in range(g_n):
        for pair in range(pairs):
            n = g * pairs + pair
            block = blocks.at[n]
            copy_tiles(wide, block, 3, tr, tc, src_at=(pair * 4 * tr, g * 3 * tc))
            ext = jnp.where(first, extra(g, 2 * pair), extra(g, 2 * pair + 1))
            block[3 * tr : br, :] = ext.astype(BF16)
            out.put(blocks.at[n], cube.scatter_slot(me, g * cube.rows + cube.row_of(me, side, pair)))


def attention_grad_scratch(cube, sizes, t):
    tr, tc = sizes[:2]
    return [
        pltpu.VMEM((D, 2 * t), BF16),
        pltpu.VMEM((D // 2, 2 * t), BF16),
        pltpu.VMEM((D // 2, 3 * D), BF16),
        pltpu.VMEM((cube.half, 3 * tr + EXTRA, 4 * tc), BF16),
    ]


def attention_backward_and_grad(
    cube, ends, dh_mid, dh0, h, qkv, lse, m0, wqkv, wout, vec, a1, a0, dq1, dvecs, dfbs, sizes
):
    tr, tc, vrows, vcols, bias = sizes
    br, bc = 3 * tr + EXTRA, 4 * tc
    g_n, r_n = cube.groups, cube.rows
    t = h.shape[0]
    if not fits(br, bc):
        dq0, d_in, dvec = attention_backward_call(ends, dh_mid, dh0, h, qkv, lse, m0, wqkv, wout, vec)
        dvec, dfb = dvec + dvecs[0] + dvecs[1], dfbs[0] + dfbs[1]
        dqkv = tiled(blocked(mm(a1, dq1, TN) + mm(a0, dq0, TN), g_n, r_n), 3)
        vecs = blocked(dvec, g_n, r_n)
        biases = dfb.reshape(g_n, r_n, 1, bias)
        ext = jnp.zeros((g_n, r_n, EXTRA, bc), F32)
        ext = ext.at[:, :, :vrows, :vcols].set(vecs).at[:, :, vrows : vrows + 1, :bias].set(biases)
        full = jnp.concatenate([dqkv, ext], 2).astype(BF16)
        keep, send = ordered_slots(cube, full.reshape(cube.n, br, bc))
        return d_in, send, keep

    def body(
        ends, dh_mid, dh0, h, qkv, lse, m0, wqkv, wout, vec, a1, a0, dq1, dvec1, dvec0, dfb1, dfb0,
        d_in, dq0, dvec, dfb, send, mask, dmix, da, *scratch,
    ):
        waits = {
            "dh_low": dh0, "wout": wout, "qkv": qkv, "mixed": m0, "lse": lse, "wqkv": wqkv, "h": h,
            "dh_mid": dh_mid,
        }
        for x in (*waits.values(), vec, a1, a0, dq1, dvec1, dvec0, dfb1, dfb0):
            x.start()
        fill_mask(ends, mask)
        attention_backward(
            dh_mid.ref, dh0.ref, h.ref, qkv.ref, lse.ref, m0.ref, mask, wqkv.ref, wout.ref, vec.get(),
            dmix, dq0.ref, da, d_in.ref, dvec.ref, use=lambda which: waits[which].get(),
            done=lambda which: dq0.flush(),
        )
        d_in.flush()
        dvec.ref[...] += dvec1.get()[...] + dvec0.get()[...]
        dfb.ref[...] = dfb1.get()[...] + dfb0.get()[...]
        dvec.flush()
        dfb.flush()
        operands = (a1.get, a0.get, dq1.get, lambda: dq0.ref, lambda: dvec.ref, lambda: dfb.ref)
        attention_grad_side(cube, my_number(cube), 1, sizes, operands, *scratch, send)

    ins = [(ends, "smem")] + [(x, "fetch") for x in (dh_mid, dh0, h, qkv, lse, m0, wqkv, wout)]
    ins += [(x, "fetch") for x in (vec, a1, a0, dq1, *dvecs, *dfbs)]
    outs = [
        ((t, D), F32, "flush"),
        ((t, 3 * D), BF16, "flush"),
        ((8, D), F32, "flush"),
        ((1, FF), F32, "flush"),
        ((cube.half, br, bc), BF16, "sink", cube.half),
    ]
    scratch = [pltpu.VMEM((t, t), F32), pltpu.VMEM((t, D), BF16), pltpu.VMEM((t, D), F32)]
    scratch += attention_grad_scratch(cube, sizes, t)
    got = staged_call(body, ins, outs, scratch, us=17, mib=48)
    return got[0], got[4], (a1, a0, dq1, got[1], got[2], got[3])


def attention_grad_keep(cube, operands, sizes):
    tr, tc = sizes[:2]
    br, bc = 3 * tr + EXTRA, 4 * tc
    if not fits(br, bc):
        return operands
    t = operands[0].shape[0]

    def body(*refs):
        given, keep, scratch = refs[:6], refs[6], refs[7:]
        for x in given:
            x.start()
        attention_grad_side(cube, my_number(cube), 0, sizes, [x.get for x in given], *scratch, keep)

    ins = [(x, "fetch") for x in operands]
    outs = [((cube.half, br, bc), BF16, "sink", cube.half)]
    return staged_call(body, ins, outs, attention_grad_scratch(cube, sizes, t), us=8, mib=32)[0]


def adam_update(weight, first, second, grad, keep_frac):
    t_step = float(STEP)
    first_new = 0.9 * first * keep_frac + 0.1 * grad
    second_new = 0.95 * second * keep_frac + 0.05 * grad * grad
    first_hat = first_new / (1.0 - 0.9**t_step)
    second_hat = second_new / (1.0 - 0.95**t_step)
    weight_new = weight.astype(F32) * (1.0 - LEARN_RATE * WEIGHT_DECAY) - LEARN_RATE * first_hat / (
        jnp.sqrt(second_hat) + 1e-08
    )
    return (weight_new.astype(BF16), first_new, second_new)


def body(
    hidden_in,
    cotangent,
    w_qkv,
    w_out,
    w_fc,
    w_proj,
    vectors,
    fc_bias,
    first_qkv,
    first_out,
    first_fc,
    first_proj,
    first_vectors,
    first_fc_bias,
    second_qkv,
    second_out,
    second_fc,
    second_proj,
    second_vectors,
    second_fc_bias,
    seg_ends,
    pass_counts,
    reset_flag,
):
    cube = Cube(lax.axis_size("grp"), lax.axis_size("row"))
    rows_w = w_qkv.shape[0]
    vrows, vcols = vectors.shape
    bias = fc_bias.shape[0]
    tr, tc = rows_w // 4, w_out.shape[1]
    sizes = (tr, tc, vrows, vcols, bias)

    far = cube.bits - 3
    near, last = far, far + 1
    join = lambda x, y: jnp.concatenate([x, y], 0)
    a, f = pack(w_qkv, w_out, w_fc, vectors, fc_bias, seg_ends, sizes)
    mixed = cube.mixed_plans
    a, p = lock((cube.gather_steps(a[None], 0, 1), cube.gather_steps(w_proj.T[None], 0, 1, mixed)))
    a = cube.gather_steps(a, 1, far)

    a, f = lock((a, f[None]))
    got, f = lock((cube.gather_swap(a, near), cube.gather_steps(f, 0, 1)))
    a = join(a, got)

    a, f, p = lock((a, f, p))
    part = p.shape[1] // 3
    last_a, f, got_p0 = lock(
        (
            cube.gather_swap(a, last),
            cube.gather_steps(f, 1, far),
            cube.gather_swap(p[:, :part], 1, mixed),
        )
    )

    f, p1 = lock((f, p[:, part:]))
    core_a0, core_a1, got, got_p1 = lock(
        (
            cube.swap_core(a),
            cube.swap_core(last_a),
            cube.gather_swap(f, near),
            cube.gather_swap(p1, 1, mixed),
        )
    )
    f = join(f, got)
    p = cube.gather_steps(join(p, jnp.concatenate([got_p0, got_p1], 1)), 2, far, mixed)

    h0, f, p = lock((hidden_in, f, p))
    full, acts = open_attention(cube, seg_ends, h0, (a, last_a, core_a0, core_a1), sizes)
    full, acts, last_f, core_f0, p = lock(
        (
            full,
            acts,
            cube.gather_swap(f, last),
            cube.swap_core(f),
            cube.gather_steps(p, far, last, mixed),
        )
    )
    wqkv, vec, fb, tot = full
    a0, qkv0, lse0, mixed0 = acts

    core_f1 = cube.swap_core(last_f)
    core_f1, p = lock((core_f1, p))
    opened = open_fc(cube, h0, mixed0, (f, last_f, core_f0, core_f1), vec, fb, sizes)
    opened, last_p, core_p0 = lock((opened, cube.gather_swap(p, last, mixed), cube.swap_core(p)))
    (wfc, wout), (mid0, c0, g0, gp0) = opened
    core_p1 = cube.swap_core(last_p)
    made, slots = second_pass(
        cube, seg_ends, pass_counts, mid0, g0, (p, last_p, core_p0, core_p1), cotangent, wqkv, wout, wfc, vec, fb
    )
    wpt, hidden, d1, a1, mixed1, c1, dqkv1, dhl1, dfl1, dvec1, dfb1 = made
    keep_p, send_p = slots
    total = tot[0, 0]
    end = cube.bits - 1

    p = cube.scatter_add(keep_p, cube.swap_core(send_p))

    d1, p = lock((d1, p))
    back, send_f, rest = ffn_backward_and_grad(
        cube, d1, mid0, gp0, wfc, wpt, vec, c1, c0, dfl1, mixed1, mixed0, dhl1, sizes
    )
    back, send_f, rest, got = lock((back, send_f, rest, cube.scatter_swap(p, 0)))
    dfb0, dhm0, dhl0, dvec0 = back
    p = cube.scatter_add(p[0], got)

    send_f, rest, p = lock((send_f, rest, p))
    keep_f = ffn_grad_keep(cube, rest, sizes)
    keep_f, got_f, got = lock((keep_f, cube.swap_core(send_f), cube.scatter_swap(p, 1)))
    f = cube.scatter_add(keep_f, got_f)
    p = cube.scatter_add(p[0], got)

    dhl0, f, p = lock((dhl0, f, p))
    input_grad, send_a, rest = attention_backward_and_grad(
        cube, seg_ends, dhm0, dhl0, h0, qkv0, lse0, mixed0, wqkv, wout, vec, a1, a0, dqkv1,
        (dvec1, dvec0), (dfb1, dfb0), sizes,
    )
    send_a, rest, got_f, p = lock((send_a, rest, cube.scatter_swap(f, 0), cube.scatter_steps(p, 2, 3)))
    f = cube.scatter_add(f[0], got_f)

    send_a, rest, f, p = lock((send_a, rest, f, p))
    keep_a = attention_grad_keep(cube, rest, sizes)
    keep_a, got_a, got_f, sum_p = lock(
        (keep_a, cube.swap_core(send_a), cube.scatter_swap(f, 1), cube.scatter_steps(p, 3, end))
    )
    a = cube.scatter_add(keep_a, got_a)
    f = cube.scatter_add(f[0], got_f)

    a, f = lock((a, f))
    a = cube.scatter_steps(a, 0, 1)
    got_a, sum_f = lock((cube.scatter_swap(a, 1), cube.scatter_steps(f, 2, end)))
    a = cube.scatter_add(a[0], got_a)
    sum_a = cube.scatter_steps(a, 2, end)

    sum_a, sum_f = sum_a.astype(F32), sum_f.astype(F32)
    summed = (
        untiled(sum_a[: 3 * tr], 3),
        untiled(sum_f[rows_w:], 1),
        sum_f[:rows_w],
        sum_p.T.astype(F32),
        sum_a[3 * tr : 3 * tr + vrows, :vcols],
        sum_a[3 * tr + vrows, :bias],
    )
    grads = tuple(s / total for s in summed)
    keep_feat = 1.0 - reset_flag.astype(F32)
    keep_rows = lax.dynamic_slice_in_dim(keep_feat, lax.axis_index("row") * rows_w, rows_w)[:, None]
    keep_cols = lax.dynamic_slice_in_dim(keep_feat, lax.axis_index("grp") * vcols, vcols)[None, :]
    bias_index = (my_number(cube) * bias + jnp.arange(bias, dtype=jnp.int32)) % D
    keeps = (keep_rows, keep_rows, keep_rows, keep_cols, keep_cols, keep_feat[bias_index])
    weights = (w_qkv, w_out, w_fc, w_proj, vectors, fc_bias)
    firsts = (first_qkv, first_out, first_fc, first_proj, first_vectors, first_fc_bias)
    seconds = (second_qkv, second_out, second_fc, second_proj, second_vectors, second_fc_bias)
    updated = [
        adam_update(w, m, v, g, kp) for w, m, v, g, kp in zip(weights, firsts, seconds, grads, keeps)
    ]
    return (
        (hidden, input_grad)
        + grads
        + tuple(u[0] for u in updated)
        + tuple(u[1] for u in updated)
        + tuple(u[2] for u in updated)
    )


def solution(mesh):
    tokens = P(("grp", "row"), None)
    flat = P(("grp", "row"))
    tiles = P("row", "grp")
    six = (tiles, tiles, tiles, tiles, tiles, flat)
    return jax.shard_map(
        body,
        mesh=mesh,
        in_specs=(tokens, tokens) + six * 3 + (tokens, P("grp"), P()),
        out_specs=(tokens, tokens) + six * 4,
        check_vma=False,
    )
```

```python
import functools

import jax
import jax.numpy as jnp
from jax import lax
from jax.experimental import pallas as pl
from jax.experimental.pallas import tpu as pltpu
from jax.sharding import PartitionSpec as P

D = 768
HEADS = 12
HEAD = 64
FF = 3072
STEP = 10
LEARN_RATE = 0.03
WEIGHT_DECAY = 0.1
F32 = jnp.float32
BF16 = jnp.bfloat16
NN = (((1,), (0,)), ((), ()))
NT = (((1,), (1,)), ((), ()))
TN = (((0,), (0,)), ((), ()))
NB = 256
LN_ROWS = 32
EXTRA = 16
GELU_A = 0.7978845608028654
GELU_B = 0.044715
BOTH = ("grp", "row")

VM = pl.BlockSpec(memory_space=pltpu.VMEM)
SM = pl.BlockSpec(memory_space=pltpu.SMEM)
HB = pl.BlockSpec(memory_space=pl.ANY)


def params(mib):
    return pltpu.CompilerParams(vmem_limit_bytes=mib * 2**20)


def like(shape, dtype):
    return jax.ShapeDtypeStruct(shape, dtype)


def mm(a, b, dims):
    return lax.dot_general(a, b, dims, preferred_element_type=F32)


def kernel_call(body, outs, specs, scratch=(), us=5, mib=60):
    return pl.pallas_call(
        body,
        out_shape=outs,
        in_specs=specs,
        out_specs=[VM] * len(outs),
        scratch_shapes=list(scratch),
        compiler_params=params(mib),
        cost_estimate=pl.CostEstimate(
            flops=int(us * 1e9), bytes_accessed=int(us * 3e6), transcendentals=0
        ),
    )


class Fetched:
    def __init__(self, src, dst, sems, axis):
        self.ref, n = dst, len(sems)
        size = dst.shape[axis] // n
        self.copies, self.begun, self.waited = [], 0, 0
        for i in range(n):
            at = tuple(pl.ds(i * size, size) if d == axis else slice(None) for d in range(len(dst.shape)))
            self.copies.append(pltpu.make_async_copy(src.at[at], dst.at[at], sems[i]))

    def start(self, n=None):
        for copy in self.copies[self.begun : n]:
            copy.start()
            self.begun += 1

    def get(self, n=None):
        self.start(n)
        for copy in self.copies[self.waited : n]:
            copy.wait()
            self.waited += 1
        return self.ref


class Flushed:
    def __init__(self, dst, src, sems):
        self.dst, self.ref, self.sems, self.copies = dst, src, list(sems), []

    def flush(self, *at):
        at = at or (slice(None),)
        copy = pltpu.make_async_copy(self.ref.at[at], self.dst.at[at], self.sems[len(self.copies)])
        copy.start()
        self.copies.append(copy)

    def finish(self):
        if not self.copies:
            self.flush()
        for copy in self.copies:
            copy.wait()


class Sink:
    def __init__(self, dst, sems):
        self.dst, self.sems, self.copies = dst, list(sems), []

    def put(self, src, *at):
        copy = pltpu.make_async_copy(src, self.dst.at[at], self.sems[len(self.copies)])
        copy.start()
        self.copies.append(copy)

    def finish(self):
        for copy in self.copies:
            copy.wait()


def staged_call(body, ins, outs, scratch=(), us=5, mib=60):
    n_in, n_out = len(ins), len(outs)
    spec_of = {"smem": SM, "vmem": VM, "any": HB, "fetch": HB, "flush": HB, "sink": HB}
    fetches = [i for i, how in enumerate(ins) if how[1] == "fetch"]
    flushes = [i for i, how in enumerate(outs) if how[2] == "flush"]
    sinks = [i for i, how in enumerate(outs) if how[2] == "sink"]
    extra = [pltpu.VMEM(ins[i][0].shape, ins[i][0].dtype) for i in fetches]
    extra += [pltpu.VMEM(outs[i][0], outs[i][1]) for i in flushes]
    counts = [(ins[i] + (0, 1))[3] if len(ins[i]) > 2 else 1 for i in fetches]
    counts += [outs[i][3] if len(outs[i]) > 3 else 1 for i in flushes + sinks]
    axes = [ins[i][2] if len(ins[i]) > 2 else 0 for i in fetches]
    extra += [pltpu.SemaphoreType.DMA((max(sum(counts), 1),))]

    def run(*refs):
        given, made = list(refs[:n_in]), list(refs[n_in : n_in + n_out])
        rest = refs[n_in + n_out :]
        own, mine = rest[: len(scratch)], rest[len(scratch) :]
        buffers, sem = mine[:-1], mine[-1]
        first = 0
        for j, i in enumerate(fetches + flushes + sinks):
            sems = [sem.at[first + k] for k in range(counts[j])]
            first += counts[j]
            if j < len(fetches):
                given[i] = Fetched(given[i], buffers[j], sems, axes[j])
            elif j < len(buffers):
                made[i] = Flushed(made[i], buffers[j], sems)
            else:
                made[i] = Sink(made[i], sems)
        body(*given, *made, *own)
        for i in fetches:
            given[i].get()
        for i in flushes + sinks:
            made[i].finish()

    return pl.pallas_call(
        run,
        out_shape=[like(out[0], out[1]) for out in outs],
        in_specs=[spec_of[how[1]] for how in ins],
        out_specs=[spec_of[how[2]] for how in outs],
        scratch_shapes=list(scratch) + extra,
        compiler_params=params(mib),
        cost_estimate=pl.CostEstimate(
            flops=int(us * 1e9), bytes_accessed=int(us * 3e6), transcendentals=0
        ),
    )(*[how[0] for how in ins])


def norm_stats(x):
    centred = x - jnp.mean(x, -1, keepdims=True)
    inv = lax.rsqrt(jnp.mean(centred * centred, -1, keepdims=True) + 1e-5)
    return centred * inv, inv


def colsum(x):
    return jnp.sum(x, 0, keepdims=True)


def norm_forward(x, gain, bias, out):
    for i in range(0, x.shape[0], LN_ROWS):
        rows = slice(i, i + LN_ROWS)
        xhat, _ = norm_stats(x[rows, :].astype(F32))
        out[rows, :] = (xhat * gain + bias).astype(BF16)


def fold(x):
    return jnp.sum(x.reshape(x.shape[0] // 8, 8, x.shape[1]), 0)


def fill_mask(ends_ref, mask_ref):
    tokens = mask_ref.shape[0]
    n_ends = ends_ref.shape[1]

    def segments(pos):
        seg = jnp.zeros(pos.shape, jnp.int32)
        for e in range(n_ends):
            seg += (pos >= ends_ref[0, e]).astype(jnp.int32)
        return seg

    seg_keys = segments(lax.broadcasted_iota(jnp.int32, (1, tokens), 1))
    for i in range(0, tokens, 128):
        pos = lax.broadcasted_iota(jnp.int32, (128, 1), 0) + i
        key = lax.broadcasted_iota(jnp.int32, (128, tokens), 1)
        seen = (segments(pos) == seg_keys) & (key <= pos)
        mask_ref[i : i + 128, :] = jnp.where(seen, 0.0, -1e30)


def attention_forward(h, wqkv, vec, mask, a, qkv, lse, mixed, tile=256, done=None):
    tokens = h.shape[0]
    done = done or (lambda which: None)
    norm_forward(h, vec[0:1, :], vec[1:2, :], a)
    for part in range(3):
        for j in range(0, D, NB):
            o = part * D + j
            r = mm(a[...], wqkv[:, o : o + NB], NN)
            if part == 0:
                r = r + vec[2:3, j : j + NB]
            if part == 2:
                r = r + vec[3:4, j : j + NB]
            qkv[:, o : o + NB] = r.astype(BF16)
    done("qkv")
    lanes = lax.broadcasted_iota(jnp.int32, (tile, 128), 1)
    low = lanes < HEAD
    together = 2
    for i in range(tokens // tile):
        rows = slice(i * tile, (i + 1) * tile)
        seen = (i + 1) * tile
        logs = jnp.zeros((tile, 128), F32)
        for first in range(0, HEADS // 2, together):
            jobs = [(p, half) for p in range(first, first + together) for half in range(2)]
            scores = []
            for p, half in jobs:
                q = qkv[rows, 128 * p : 128 * p + 128] * BF16(HEAD**-0.5)
                k = qkv[0:seen, D + 128 * p : D + 128 * p + 128]
                own = low if half == 0 else ~low
                scores.append(mm(jnp.where(own, q, BF16(0)), k, NT) + mask[rows, 0:seen])
            tops = [jnp.max(x, -1, keepdims=True) for x in scores]
            expo = [jnp.exp(x - top) for x, top in zip(scores, tops)]
            dens = [jnp.sum(x, -1, keepdims=True) for x in expo]
            outs = []
            for (p, half), x, den, top in zip(jobs, expo, dens, tops):
                v = qkv[0:seen, 2 * D + 128 * p : 2 * D + 128 * p + 128]
                outs.append(mm(x.astype(BF16), v, NN) / den)
                logs = jnp.where(lanes == 2 * p + half, top + jnp.log(den), logs)
            for n, (p, half) in enumerate(jobs):
                if half == 1:
                    mixed[rows, 128 * p : 128 * p + 128] = jnp.where(low, outs[n - 1], outs[n]).astype(BF16)
        lse[rows, :] = logs
    done("mixed")


def out_forward(h, mixed, wout, vec, h_mid):
    for j in range(0, D, NB):
        r = mm(mixed[...], wout[:, j : j + NB], NN)
        h_mid[:, j : j + NB] = h[:, j : j + NB].astype(F32) + r + vec[4:5, j : j + NB]


def fc_forward(h_mid, wfc, vec, fb, c, g, gp, done=None):
    done = done or (lambda j: None)
    norm_forward(h_mid, vec[5:6, :], vec[6:7, :], c)
    for j in range(0, FF, NB):
        f = mm(c[...], wfc[:, j : j + NB], NN) + fb[0:1, j : j + NB]
        sq = f * f
        t = jnp.tanh(GELU_A * (f + GELU_B * sq * f))
        half = 0.5 * (1.0 + t)
        g[:, j : j + NB] = (f * half).astype(BF16)
        slope = half + (0.5 * GELU_A) * f * (1.0 - t * t) * (1.0 + (3 * GELU_B) * sq)
        gp[:, j : j + NB] = slope.astype(BF16)
        done(j + NB)


def proj_forward(h_mid, g, wpt, vec, h_out):
    for j in range(0, D, NB):
        r = mm(g[...], wpt[j : j + NB, :], NT)
        h_out[:, j : j + NB] = h_mid[:, j : j + NB] + r + vec[7:8, j : j + NB]


def norm_backward(dout, x, gain, base, store):
    sums = [jnp.zeros((8, x.shape[1]), F32) for _ in range(3)]
    for i in range(0, x.shape[0], LN_ROWS):
        rows = slice(i, i + LN_ROWS)
        xhat, inv = norm_stats(x[rows, :].astype(F32))
        d = dout[rows, :]
        sums[0] += fold(d * xhat)
        sums[1] += fold(d)
        dx = d * gain
        m1 = jnp.mean(dx, -1, keepdims=True)
        m2 = jnp.mean(dx * xhat, -1, keepdims=True)
        total = base[rows, :] + inv * (dx - m1 - xhat * m2)
        sums[2] += fold(total)
        store(rows, total)
    return [colsum(x) for x in sums]


def ffn_backward(
    dy, h_mid, gp, wfc, wpt, vec, dy_low, df_low, dfb, dh_mid, dh_low, dvec, dc, use=None, done=None
):
    use = use or (lambda which, j=0: None)
    done = done or (lambda which: None)
    d_out = dy[...]
    dy_low[...] = d_out.astype(BF16)
    dvec[0:4, :] = jnp.zeros((4, D), F32)
    dvec[7:8, :] = colsum(d_out)
    for j in range(0, FF, NB):
        use("hidden", j)
        d = mm(dy_low[...], wpt[:, j : j + NB], NN)
        df = d * gp[:, j : j + NB].astype(F32)
        dfb[0:1, j : j + NB] = colsum(df)
        df_low[:, j : j + NB] = df.astype(BF16)
    done("df")
    for j in range(0, D, NB):
        use("wfc", j)
        dc[:, j : j + NB] = mm(df_low[...], wfc[j : j + NB, :], NT)
    use("h_mid")

    def store(rows, total):
        dh_mid[rows, :] = total
        dh_low[rows, :] = total.astype(BF16)

    dvec[5:6, :], dvec[6:7, :], dvec[4:5, :] = norm_backward(dc, h_mid, vec[5:6, :], dy, store)


def attention_backward(
    dh_mid, dh_low, h, qkv, lse, mixed, mask, wqkv, wout, vec, dmix, dqkv, da, d_in, dvec,
    use=None, done=None,
):
    use = use or (lambda which: None)
    done = done or (lambda which: None)
    tokens = h.shape[0]
    use("wout")
    use("dh_low")
    for j in range(0, D, NB):
        dmix[:, j : j + NB] = mm(dh_low[...], wout[j : j + NB, :], NT).astype(BF16)
    use("qkv")
    use("mixed")
    use("lse")
    tile = 256
    low = lax.broadcasted_iota(jnp.int32, (tokens, 128), 1) < HEAD
    low_rows = lax.broadcasted_iota(jnp.int32, (128, tokens), 0) < HEAD
    for p in range(HEADS // 2):
        c = 128 * p
        cs = slice(c, c + 128)
        q = qkv[:, cs] * BF16(HEAD**-0.5)
        k = qkv[:, D + c : D + c + 128]
        v = qkv[:, 2 * D + c : 2 * D + c + 128]
        dm = dmix[:, cs]
        prod = dm.astype(F32) * mixed[:, cs].astype(F32)
        dm_t = dm.astype(F32).T.astype(BF16)
        q_t = q.astype(F32).T.astype(BF16)
        masks = ((low, low_rows), (~low, ~low_rows))
        deltas = [jnp.sum(jnp.where(own, prod, 0.0), -1, keepdims=True) for own, _ in masks]
        q_own = [jnp.where(own, q, BF16(0)) for own, _ in masks]
        k_own = [jnp.where(own, k, BF16(0)) for own, _ in masks]
        dm_own = [jnp.where(own, dm, BF16(0)) for own, _ in masks]
        dm_t_own = [jnp.where(own, dm_t, BF16(0)) for _, own in masks]
        q_t_own = [jnp.where(own, q_t, BF16(0)) for _, own in masks]
        dq, dk_t, dv_t = [], [], []
        for i in range(tokens // tile):
            rows, seen = slice(i * tile, (i + 1) * tile), (i + 1) * tile
            scores = [mm(x[rows], k[0:seen], NT) + mask[rows, 0:seen] for x in q_own]
            probs = [jnp.exp(x - lse[rows, 2 * p + n : 2 * p + n + 1]) for n, x in enumerate(scores)]
            dps = [mm(x[rows], v[0:seen], NT) for x in dm_own]
            ds = [(x * (y - z[rows])).astype(BF16) for x, y, z in zip(probs, dps, deltas)]
            dv_t.append(sum(mm(x[:, rows], y.astype(BF16), NN) for x, y in zip(dm_t_own, probs)))
            dk_t.append(sum(mm(x[:, rows], y, NN) for x, y in zip(q_t_own, ds)))
            dq.append(sum(mm(x, y[0:seen], NN) for x, y in zip(ds, k_own)))

        def joined(parts):
            cols = []
            for n in range(len(parts)):
                cols.append(sum(part[:, n * tile : (n + 1) * tile] for part in parts[n:]))
            return jnp.concatenate(cols, 1)

        dq = jnp.concatenate(dq, 0) * HEAD**-0.5
        dv = joined(dv_t).T
        dk = joined(dk_t).T
        dvec[2:3, cs] = colsum(dq)
        dvec[3:4, cs] = colsum(dv)
        dqkv[:, cs] = dq.astype(BF16)
        dqkv[:, D + c : D + c + 128] = dk.astype(BF16)
        dqkv[:, 2 * D + c : 2 * D + c + 128] = dv.astype(BF16)
    done("dqkv")
    use("wqkv")
    for j in range(0, D, NB):
        da[:, j : j + NB] = mm(dqkv[...], wqkv[j : j + NB, :], NT)
    use("h")
    use("dh_mid")

    def store(rows, total):
        d_in[rows, :] = total

    dvec[0:1, :], dvec[1:2, :], _ = norm_backward(da, h, vec[0:1, :], dh_mid, store)
    dvec[4:8, :] = jnp.zeros((4, D), F32)


def attention_forward_call(ends, h, wqkv, vec):
    t = h.shape[0]
    outs = [like((t, D), BF16), like((t, 3 * D), BF16), like((t, 128), F32), like((t, D), BF16)]

    def body(ends, h, wqkv, vec, a, qkv, lse, mixed, mask):
        fill_mask(ends, mask)
        attention_forward(h, wqkv, vec, mask, a, qkv, lse, mixed)

    return kernel_call(body, outs, [SM, VM, VM, VM], [pltpu.VMEM((t, t), F32)], us=13)(ends, h, wqkv, vec)


def fc_forward_call(h, mixed, wout, wfc, vec, fb):
    t = h.shape[0]
    outs = [like((t, D), F32), like((t, D), BF16), like((t, FF), BF16), like((t, FF), BF16)]

    def body(h, mixed, wout, wfc, vec, fb, mid, c, g, gp):
        out_forward(h, mixed, wout, vec, mid)
        fc_forward(mid, wfc, vec, fb, c, g, gp)

    return kernel_call(body, outs, [VM] * 6, us=9)(h, mixed, wout, wfc, vec, fb)


def ffn_backward_call(dy, h_mid, gp, wfc, wpt, vec):
    t = dy.shape[0]
    outs = [
        like((t, FF), BF16),
        like((1, FF), F32),
        like((t, D), F32),
        like((t, D), BF16),
        like((8, D), F32),
    ]

    def body(dy, h_mid, gp, wfc, wpt, vec, df_low, dfb, dh_mid, dh_low, dvec, dy_low, dc):
        ffn_backward(dy, h_mid, gp, wfc, wpt, vec, dy_low, df_low, dfb, dh_mid, dh_low, dvec, dc)

    scratch = [pltpu.VMEM((t, D), BF16), pltpu.VMEM((t, D), F32)]
    return kernel_call(body, outs, [VM] * 6, scratch, us=13)(dy, h_mid, gp, wfc, wpt, vec)


def attention_backward_call(ends, dh_mid, dh_low, h, qkv, lse, mixed, wqkv, wout, vec):
    t = h.shape[0]

    def body(
        ends, dh_mid, dh_low, h, qkv, lse, mixed, wqkv, wout, vec, dqkv, d_in, dvec, mask, dmix, da
    ):
        fill_mask(ends, mask)
        attention_backward(
            dh_mid, dh_low, h, qkv, lse, mixed, mask, wqkv, wout, vec, dmix, dqkv, da, d_in, dvec
        )

    outs = [like((t, 3 * D), BF16), like((t, D), F32), like((8, D), F32)]
    scratch = [pltpu.VMEM((t, t), F32), pltpu.VMEM((t, D), BF16), pltpu.VMEM((t, D), F32)]
    return kernel_call(body, outs, [SM] + [VM] * 9, scratch, us=18)(
        ends, dh_mid, dh_low, h, qkv, lse, mixed, wqkv, wout, vec
    )


class Cube:
    def __init__(self, groups, rows):
        self.groups, self.rows = groups, rows
        self.n = groups * rows
        self.bits = self.n.bit_length() - 1
        far = list(range(self.bits - 1, 2, -1))
        self.gather_plans = (far + [2, 1], far + [1, 2])
        self.mixed_plans = ([2] + far + [1], [1] + far + [2])
        self.scatter_plans = tuple(list(reversed(p)) for p in self.gather_plans)
        self.half = self.n // 2

    def swap(self, x, plans, step):
        pairs = [(i, i ^ (1 << plans[i & 1][step])) for i in range(self.n)]
        return lax.ppermute(x, BOTH, pairs)

    def swap_core(self, x):
        return lax.ppermute(x, BOTH, [(i, i ^ 1) for i in range(self.n)])

    def gather_swap(self, held, step, plans=None):
        return self.swap(held, plans or self.gather_plans, step)

    def gather_steps(self, held, first, end, plans=None):
        for step in range(first, end):
            held = jnp.concatenate([held, self.gather_swap(held, step, plans)], 0)
        return held

    def scatter_swap(self, halves, step):
        return self.swap(halves[1], self.scatter_plans, step)

    def scatter_add(self, keep, got):
        mid = keep.shape[0] // 2
        if mid == 0:
            return (keep + got)[0]
        return keep[:mid] + got[:mid], keep[mid:] + got[mid:]

    def scatter_steps(self, halves, first, end):
        for step in range(first, end):
            halves = self.scatter_add(halves[0], self.scatter_swap(halves, step))
        return halves

    def gather_source(self, me, side, slot, plans):
        core = (me & 1) ^ side
        dest = me ^ side
        for k in range(self.bits - 1):
            if (slot >> k) & 1:
                flip0, flip1 = 1 << plans[0][k], 1 << plans[1][k]
                dest = dest ^ jnp.where(core == 1, flip1, flip0)
        return dest

    def scatter_slot(self, me, dest):
        rel = me ^ dest
        core = dest & 1
        slot = 0
        for k in range(self.bits - 1):
            place = self.bits - 2 - k
            b0 = (rel >> self.scatter_plans[0][k]) & 1
            b1 = (rel >> self.scatter_plans[1][k]) & 1
            slot = slot + (jnp.where(core == 1, b1, b0) << place)
        return slot

    def row_of(self, me, side, pair):
        return 2 * pair + ((me & 1) ^ side)


lock = lax.optimization_barrier


def my_number(cube):
    return lax.axis_index("grp") * cube.rows + lax.axis_index("row")


def canonical(cube, pieces, plans):
    me = my_number(cube)
    ids = [cube.gather_source(me, side, s, plans) for side in (0, 1) for s in range(cube.half)]
    blocks = jnp.concatenate(pieces, 0)
    return jnp.zeros_like(blocks).at[jnp.stack(ids)].set(blocks)


def fits(rows, cols):
    return rows % 16 == 0 and cols % 128 == 0


def place_blocks(cube, pieces, plans, sem, *targets):
    me = my_number(cube)
    part = cube.half // 2
    copies = []
    for i, piece in enumerate(pieces):
        for s in range(part):
            dev = cube.gather_source(me, i // 2, (i % 2) * part + s, plans)
            for target in targets:
                rows, place = target(dev // cube.rows, dev % cube.rows)
                copies.append(pltpu.make_async_copy(piece.at[s, rows], place, sem))
    for cp in copies:
        cp.start()

    def wait():
        for cp in copies:
            cp.wait()

    return wait


def tiled(x, n):
    r, c = x.shape[-2] // 4, x.shape[-1] // n
    x = x.reshape(x.shape[:-2] + (4, r, n, c))
    return jnp.moveaxis(x, (-4, -2), (-2, -4)).reshape(x.shape[:-4] + (n * r, 4 * c))


def untiled(x, n):
    r, c = x.shape[-2] // n, x.shape[-1] // 4
    x = x.reshape(x.shape[:-2] + (n, r, 4, c))
    return jnp.moveaxis(x, (-4, -2), (-2, -4)).reshape(x.shape[:-4] + (4 * r, n * c))


def copy_tiles(src, dst, n, r, c, src_at=(0, 0), dst_at=(0, 0), to_wide=True):
    for i in range(4):
        for j in range(n):
            p, q = ((i, j), (j, i)) if to_wide else ((j, i), (i, j))
            rows = slice(src_at[0] + p[0] * r, src_at[0] + (p[0] + 1) * r)
            cols = slice(src_at[1] + p[1] * c, src_at[1] + (p[1] + 1) * c)
            rows_to = slice(dst_at[0] + q[0] * r, dst_at[0] + (q[0] + 1) * r)
            cols_to = slice(dst_at[1] + q[1] * c, dst_at[1] + (q[1] + 1) * c)
            dst[rows_to, cols_to] = src[rows, cols]


def blocks_of(cube, pieces, plans):
    return canonical(cube, pieces, plans).reshape((cube.groups, cube.rows) + pieces[0].shape[1:])


def unblocked(x):
    g_n, r_n, br, bc = x.shape
    return x.transpose(1, 2, 0, 3).reshape(r_n * br, g_n * bc)


def blocked(x, g_n, r_n):
    return x.reshape(r_n, x.shape[0] // r_n, g_n, x.shape[1] // g_n).transpose(2, 0, 1, 3)


def proj_full(cube, pieces):
    br, bc = pieces[0].shape[1:]
    full = blocks_of(cube, pieces, cube.mixed_plans)
    return full.transpose(0, 2, 1, 3).reshape(cube.groups * br, cube.rows * bc)


def attn_full(cube, pieces, sizes):
    tr, tc, vrows, vcols, bias = sizes
    full = blocks_of(cube, pieces, cube.gather_plans)
    wqkv = unblocked(untiled(full[:, :, : 3 * tr], 3))
    ext = full[:, :, 3 * tr :].astype(F32)
    vec = unblocked(ext[:, :, :vrows, :vcols])
    fb = ext[:, :, vrows, :bias].reshape(1, cube.n * bias)
    total = jnp.sum(ext[:, :, vrows + 1, 0]) * 16.0 + jnp.sum(ext[:, :, vrows + 1, 1])
    return wqkv, vec, fb, jnp.full((8, 128), total, F32)


def open_attention(cube, ends, h, pieces, sizes):
    br, bc = pieces[0].shape[1:]
    if not fits(br, bc):
        full = attn_full(cube, pieces, sizes)
        return full, attention_forward_call(ends, h, *full[:2])
    tr, tc, vrows, vcols, bias = sizes
    g_n, r_n = cube.groups, cube.rows
    t = h.shape[0]

    def body(ends, h, p0, p1, p2, p3, wqkv, vec, fb, tot, a, qkv, lse, mixed, mask, blk, sem):
        def target(g, r):
            return slice(None), blk.at[g, r]

        wait = place_blocks(cube, (p0, p1, p2, p3), cube.gather_plans, sem, target)
        fill_mask(ends, mask)
        wait()
        count = jnp.zeros((1, 128), F32)
        for g in range(g_n):
            for r in range(r_n):
                copy_tiles(
                    blk.at[g, r], wqkv.ref, 3, tr, tc, dst_at=(r * 4 * tr, g * 3 * tc), to_wide=False
                )
                ext = blk[g, r, 3 * tr : br, :].astype(F32)
                vec[r * vrows : (r + 1) * vrows, g * vcols : (g + 1) * vcols] = ext[0:vrows, 0:vcols]
                at = (g * r_n + r) * bias
                fb[0:1, at : at + bias] = ext[vrows : vrows + 1, 0:bias]
                count += ext[vrows + 1 : vrows + 2, 0:128]
        lane = lax.broadcasted_iota(jnp.int32, (1, 128), 1)
        weight = jnp.where(lane == 0, 16.0, jnp.where(lane == 1, 1.0, 0.0))
        tot[...] = jnp.broadcast_to(jnp.sum(count * weight, -1, keepdims=True), (8, 128))
        wqkv.flush()
        whole = {"qkv": (a, qkv), "mixed": ()}
        attention_forward(
            h, wqkv.ref, vec, mask, a.ref, qkv.ref, lse, mixed,
            done=lambda which: [x.flush() for x in whole[which]],
        )

    outs = [
        ((D, 3 * D), BF16, "flush"),
        ((8, D), F32, "vmem"),
        ((1, FF), F32, "vmem"),
        ((8, 128), F32, "vmem"),
        ((t, D), BF16, "flush"),
        ((t, 3 * D), BF16, "flush"),
        ((t, 128), F32, "vmem"),
        ((t, D), BF16, "vmem"),
    ]
    scratch = [
        pltpu.VMEM((t, t), F32),
        pltpu.VMEM((g_n, r_n, br, bc), BF16),
        pltpu.SemaphoreType.DMA,
    ]
    ins = [(ends, "smem"), (h, "vmem")] + [(x, "any") for x in pieces]
    got = staged_call(body, ins, outs, scratch, us=15)
    return got[:4], got[4:]


def open_fc(cube, h, mixed, pieces, vec, fb, sizes):
    br, bc = pieces[0].shape[1:]
    tr, tc = sizes[:2]
    t = h.shape[0]
    if not fits(br, bc):
        full = blocks_of(cube, pieces, cube.gather_plans)
        wfc, wout = unblocked(full[:, :, : 4 * tr]), unblocked(untiled(full[:, :, 4 * tr :], 1))
        return (wfc, wout), fc_forward_call(h, mixed, wout, wfc, vec, fb)

    def body(h, mixed, p0, p1, p2, p3, vec, fb, wfc, wout, mid, c, g, gp, blk, sem):
        def target_fc(g, r):
            rows, cols = pl.multiple_of(r * 4 * tr, 16), pl.multiple_of(g * bc, 128)
            return pl.ds(0, 4 * tr), wfc.ref.at[pl.ds(rows, 4 * tr), pl.ds(cols, bc)]

        def target_out(g, r):
            return pl.ds(4 * tr, tr), blk.at[g, r]

        place_blocks(cube, (p0, p1, p2, p3), cube.gather_plans, sem, target_fc, target_out)()
        wfc.flush()
        for g_i in range(cube.groups):
            for r in range(cube.rows):
                copy_tiles(
                    blk.at[g_i, r], wout.ref, 1, tr, tc, dst_at=(r * 4 * tr, g_i * tc), to_wide=False
                )
        wout.flush()
        out_forward(h, mixed, wout.ref, vec, mid.ref)
        mid.flush()

        def done(end):
            if end % D == 0:
                for x in (g, gp):
                    x.flush(slice(None), pl.ds(end - D, D))

        fc_forward(mid.ref, wfc.ref, vec, fb, c.ref, g.ref, gp.ref, done)
        c.flush()

    ins = [(h, "vmem"), (mixed, "vmem")] + [(x, "any") for x in pieces] + [(vec, "vmem"), (fb, "vmem")]
    outs = [
        ((D, FF), BF16, "flush"),
        ((D, D), BF16, "flush"),
        ((t, D), F32, "flush"),
        ((t, D), BF16, "flush"),
        ((t, FF), BF16, "flush", FF // D),
        ((t, FF), BF16, "flush", FF // D),
    ]
    scratch = [pltpu.VMEM((cube.groups, cube.rows, tr, bc), BF16), pltpu.SemaphoreType.DMA]
    got = staged_call(body, ins, outs, scratch, us=12)
    return got[:2], got[2:]


def second_pass(cube, ends, passes, mid0, g0, pieces, cot, wqkv, wout, wfc, vec, fb):
    br, bc = pieces[0].shape[1:]
    t = cot.shape[0]
    whole = fits(br, bc)
    if not whole:
        pieces = (proj_full(cube, pieces),)
    n_p = len(pieces)

    def body(*refs):
        ends, passes, mid0, g0 = refs[:4]
        src = refs[4 : 4 + n_p]
        cot, wqkv, wout, wfc, vec, fb = refs[4 + n_p : 10 + n_p]
        wpt, hidden, d1, a, mixed, c, dqkv, dhl, df, dvec, dfb = refs[10 + n_p : 21 + n_p]
        grad0, grad1 = refs[21 + n_p : 23 + n_p]
        mask, qkv, lse, mid, g, gp, dy, dyl, tmp, dhm, dmix, dvec2, dyt, h1, sem = refs[23 + n_p :]
        grad = wfc.ref
        me = my_number(cube)

        def target(g, r):
            rows, cols = pl.multiple_of(g * br, 16), pl.multiple_of(r * bc, 128)
            return slice(None), wpt.ref.at[pl.ds(rows, br), pl.ds(cols, bc)]

        if whole:
            wait = place_blocks(cube, src, cube.mixed_plans, sem, target)
        else:
            copy = pltpu.make_async_copy(src[0], wpt.ref, sem)
            copy.start()
            wait = copy.wait
        for x in (vec, fb, g0, mid0):
            x.start()
        vec, fb = vec.get(), fb.get()
        fill_mask(ends, mask)
        wait()
        g0.get()
        mid0.get()
        wqkv.start()
        wout.start()
        proj_forward(mid0.ref, g0.ref, wpt.ref, vec, h1)
        wqkv.get()
        wout.get()
        wfc.start()
        cot.start()
        attention_forward(
            h1, wqkv.ref, vec, mask, a.ref, qkv, lse, mixed.ref,
            done=lambda which: {"qkv": a, "mixed": mixed}[which].flush(),
        )
        out_forward(h1, mixed.ref, wout.ref, vec, mid)
        wfc.get()
        wpt.flush()
        fc_forward(mid, wfc.ref, vec, fb, c.ref, g, gp)
        c.flush()
        proj_forward(mid, g, wpt.ref, vec, dy)
        active = passes[0] > 1
        hidden.ref[...] = jnp.where(active, dy[...], h1[...]).astype(BF16)
        hidden.flush()
        valid = lax.broadcasted_iota(jnp.int32, (t, 1), 0) < ends[0, ends.shape[1] - 1]
        cot.get()
        dy[...] = jnp.where(valid & active, cot.ref[...].astype(F32), 0.0)
        ffn_backward(
            dy, mid, gp, wfc.ref, wpt.ref, vec, dyl, df.ref, dfb.ref, dhm, dhl.ref, dvec2, tmp,
            done=lambda which: df.flush(),
        )
        dhl.flush()
        attention_backward(
            dhm, dhl.ref, h1, qkv, lse, mixed.ref, mask, wqkv.ref, wout.ref, vec,
            dmix, dqkv.ref, tmp, dy, dvec.ref, done=lambda which: dqkv.flush(),
        )
        dvec.ref[...] += dvec2[...]
        dvec.flush()
        dfb.flush()
        d1.ref[...] = jnp.where(active, dy[...], jnp.where(valid, cot.ref[...].astype(F32), 0.0))
        d1.flush()
        dyt[:, 0:t] = dyl[...].astype(F32).T.astype(BF16)
        dyt[:, t : 2 * t] = d1.ref[...].T.astype(BF16)
        if not whole:
            grad0[...] = mm(dyt[:, 0:t], g[...], NN) + mm(dyt[:, t : 2 * t], g0.ref[...], NN)
            return
        n = 0
        for side, out in ((1, grad1), (0, grad0)):
            for pair in range(cube.rows // 2):
                r = cube.row_of(me, side, pair)
                cols = pl.ds(pl.multiple_of(r * bc, 128), bc)
                both = mm(dyt[:, 0:t], g[:, cols], NN) + mm(dyt[:, t : 2 * t], g0.ref[:, cols], NN)
                grad[:, n * bc : (n + 1) * bc] = both.astype(BF16)
                for group in range(cube.groups):
                    block = grad.at[pl.ds(group * br, br), pl.ds(n * bc, bc)]
                    out.put(block, cube.scatter_slot(me, group * cube.rows + r))
                n += 1

    ins = [(ends, "smem"), (passes, "smem"), (mid0, "fetch"), (g0, "fetch")]
    ins += [(x, "any") for x in pieces]
    ins += [(x, "fetch") for x in (cot, wqkv, wout, wfc, vec, fb)]
    outs = [
        ((D, FF), BF16, "flush"),
        ((t, D), BF16, "flush"),
        ((t, D), F32, "flush"),
        ((t, D), BF16, "flush"),
        ((t, D), BF16, "flush"),
        ((t, D), BF16, "flush"),
        ((t, 3 * D), BF16, "flush"),
        ((t, D), BF16, "flush"),
        ((t, FF), BF16, "flush"),
        ((8, D), F32, "flush"),
        ((1, FF), F32, "flush"),
    ]
    if whole:
        outs += [((cube.half, br, bc), BF16, "sink", cube.half)] * 2
    else:
        outs += [((D, FF), F32, "vmem"), ((8, 128), F32, "vmem")]
    scratch = [
        pltpu.VMEM((t, t), F32),
        pltpu.VMEM((t, 3 * D), BF16),
        pltpu.VMEM((t, 128), F32),
        pltpu.VMEM((t, D), F32),
        pltpu.VMEM((t, FF), BF16),
        pltpu.VMEM((t, FF), BF16),
        pltpu.VMEM((t, D), F32),
        pltpu.VMEM((t, D), BF16),
        pltpu.VMEM((t, D), F32),
        pltpu.VMEM((t, D), F32),
        pltpu.VMEM((t, D), BF16),
        pltpu.VMEM((8, D), F32),
        pltpu.VMEM((D, 2 * t), BF16),
        pltpu.VMEM((t, D), F32),
        pltpu.SemaphoreType.DMA,
    ]
    got = staged_call(body, ins, outs, scratch, us=50)
    slots = got[11:]
    if not whole:
        full = slots[0].astype(BF16).reshape(cube.groups, br, cube.rows, bc).transpose(0, 2, 1, 3)
        slots = ordered_slots(cube, full.reshape(cube.n, br, bc))
    return got[:11], slots


def pack(w_qkv, w_out, w_fc, vectors, fc_bias, seg_ends, sizes):
    tr, tc, vrows, vcols, bias = sizes
    wide = 4 * tc

    def extra(vec, fb, n_valid):
        lane = lax.broadcasted_iota(jnp.int32, (1, wide), 1)
        n_high = n_valid // 16
        count = jnp.where(lane == 0, n_high, jnp.where(lane == 1, n_valid - 16 * n_high, 0))
        rows = [
            jnp.concatenate([vec.astype(F32), jnp.zeros((vrows, wide - vcols), F32)], 1),
            jnp.concatenate([fb.astype(F32), jnp.zeros((1, wide - bias), F32)], 1),
            count.astype(F32),
            jnp.zeros((EXTRA - vrows - 2, wide), F32),
        ]
        return jnp.concatenate(rows, 0).astype(BF16)

    if not fits(tr, wide):
        ext = extra(vectors, fc_bias[None], seg_ends[0, -1])
        return (
            jnp.concatenate([tiled(w_qkv, 3), ext], 0),
            jnp.concatenate([w_fc, tiled(w_out, 1)], 0),
        )

    def body(wq, wo, wf, vec, fb, ends, out_a, out_f):
        copy_tiles(wq, out_a, 3, tr, tc)
        out_a[3 * tr : 3 * tr + EXTRA, :] = extra(vec[...], fb[...], ends[0, ends.shape[1] - 1])
        out_f[0 : 4 * tr, :] = wf[...]
        copy_tiles(wo, out_f, 1, tr, tc, dst_at=(4 * tr, 0))

    outs = [like((3 * tr + EXTRA, wide), BF16), like((5 * tr, wide), BF16)]
    return kernel_call(body, outs, [VM] * 5 + [SM], us=2)(
        w_qkv, w_out, w_fc, vectors, fc_bias[None], seg_ends
    )


def ordered_slots(cube, blocks):
    me = my_number(cube)
    order = [cube.scatter_slot(me, dest) + cube.half * ((me ^ dest) & 1) for dest in range(cube.n)]
    slots = jnp.zeros_like(blocks).at[jnp.stack(order)].set(blocks)
    return slots[: cube.half], slots[cube.half :]


def stacked_t(parts, out):
    t = parts[0].shape[0]
    for i, part in enumerate(parts):
        out[:, i * t : (i + 1) * t] = part[...].astype(F32).T.astype(BF16)


def side_rows(cube, me, side, src, out, height):
    for pair in range(cube.rows // 2):
        r = cube.row_of(me, side, pair)
        out[pair * height : (pair + 1) * height, :] = src[pl.ds(pl.multiple_of(r * height, 16), height), :]


def ffn_grad_side(cube, me, side, sizes, operands, lt, lhs, grad, wide, blocks, out):
    m1, m0, dh1, dh0, c1, c0, df1, df0 = operands
    tr, tc = sizes[:2]
    bc = 4 * tc
    t = lt.shape[1] // 2
    pairs = cube.rows // 2
    stacked_t((m1(), m0()), lt)
    side_rows(cube, me, side, lt, lhs, 4 * tr)
    dh1, dh0 = dh1(), dh0()
    for j in range(0, D, NB):
        cols = slice(j, j + NB)
        both = mm(lhs[:, 0:t], dh1[:, cols], NN) + mm(lhs[:, t : 2 * t], dh0[:, cols], NN)
        wide[:, cols] = both.astype(BF16)
    for g in range(cube.groups):
        for pair in range(pairs):
            copy_tiles(wide, blocks.at[g * pairs + pair], 1, tr, tc, src_at=(pair * 4 * tr, g * tc))
    stacked_t((c1(), c0()), lt)
    side_rows(cube, me, side, lt, lhs, 4 * tr)
    df1, df0 = df1(), df0()
    for first in range(0, cube.groups, 2):
        cols = slice(first * bc, (first + 2) * bc)
        both = mm(lhs[:, 0:t], df1[:, cols], NN) + mm(lhs[:, t : 2 * t], df0[:, cols], NN)
        grad[:, cols] = both.astype(BF16)
        for g in (first, first + 1):
            for pair in range(pairs):
                slot = cube.scatter_slot(me, g * cube.rows + cube.row_of(me, side, pair))
                rows = pl.ds(pair * 4 * tr, 4 * tr)
                out.put(grad.at[rows, pl.ds(g * bc, bc)], slot, pl.ds(0, 4 * tr))
                out.put(blocks.at[g * pairs + pair], slot, pl.ds(4 * tr, tr))


def ffn_grad_scratch(cube, sizes, t):
    tr, tc = sizes[:2]
    return [
        pltpu.VMEM((D, 2 * t), BF16),
        pltpu.VMEM((D // 2, 2 * t), BF16),
        pltpu.VMEM((D // 2, FF), BF16),
        pltpu.VMEM((D // 2, D), BF16),
        pltpu.VMEM((cube.half, tr, 4 * tc), BF16),
    ]


def ffn_backward_and_grad(cube, dy, h_mid, gp, wfc, wpt, vec, c1, c0, df1, m1, m0, dh1, sizes):
    t = dy.shape[0]
    tr, tc = sizes[:2]
    br, bc = 5 * tr, 4 * tc
    if not fits(br, bc):
        df0, *rest = ffn_backward_call(dy, h_mid, gp, wfc, wpt, vec)
        dfc = blocked(mm(c1, df1, TN) + mm(c0, df0, TN), cube.groups, cube.rows)
        dout = blocked(mm(m1, dh1, TN) + mm(m0, rest[2], TN), cube.groups, cube.rows)
        full = jnp.concatenate([dfc, tiled(dout, 1)], 2).astype(BF16)
        keep, send = ordered_slots(cube, full.reshape(cube.n, br, bc))
        return rest, send, keep

    def body(
        dy, h_mid, gp, wfc, wpt, vec, c1, c0, df1, m1, m0, dh1, dfb, dh_mid, dh_low, dvec, df0, send,
        dy_low, dc, *scratch,
    ):
        me = my_number(cube)
        order = {"dy": dy, "wpt": wpt, "gp": gp, "wfc": wfc, "h_mid": h_mid}
        for x in (vec, dy, wpt, gp):
            x.start()

        def use(which, j=0):
            if which == "hidden":
                if j == 0:
                    wpt.get()
                    wfc.start()
                    h_mid.start()
                if j == FF // 2:
                    for x in (m1, m0, dh1, c1, c0, df1):
                        x.start()
                gp.get(j // (FF // 4) + 1)
            else:
                order[which].get()
                vec.get()

        ffn_backward(
            dy.get(), h_mid.ref, gp.ref, wfc.ref, wpt.ref, vec.ref, dy_low, df0.ref, dfb.ref, dh_mid.ref,
            dh_low.ref, dvec.ref, dc, use=use, done=lambda which: df0.flush(),
        )
        for x in (dh_mid, dh_low, dvec, dfb):
            x.flush()
        operands = (m1.get, m0.get, dh1.get, lambda: dh_low.ref, c1.get, c0.get, df1.get, lambda: df0.ref)
        ffn_grad_side(cube, me, 1, sizes, operands, *scratch, send)

    ins = [
        (dy, "fetch"), (h_mid, "fetch"), (gp, "fetch", 1, 4), (wfc, "fetch"), (wpt, "fetch"), (vec, "fetch"),
        (c1, "fetch"), (c0, "fetch"), (df1, "fetch"), (m1, "fetch"), (m0, "fetch"), (dh1, "fetch"),
    ]
    outs = [
        ((1, FF), F32, "flush"),
        ((t, D), F32, "flush"),
        ((t, D), BF16, "flush"),
        ((8, D), F32, "flush"),
        ((t, FF), BF16, "flush"),
        ((cube.half, br, bc), BF16, "sink", 2 * cube.half),
    ]
    scratch = [pltpu.VMEM((t, D), BF16), pltpu.VMEM((t, D), F32)] + ffn_grad_scratch(cube, sizes, t)
    got = staged_call(body, ins, outs, scratch, us=18)
    return got[:4], got[5], (m1, m0, dh1, got[2], c1, c0, df1, got[4])


def ffn_grad_keep(cube, operands, sizes):
    tr, tc = sizes[:2]
    br, bc = 5 * tr, 4 * tc
    if not fits(br, bc):
        return operands
    t = operands[0].shape[0]

    def body(*refs):
        given, keep, scratch = refs[:8], refs[8], refs[9:]
        for x in given:
            x.start()
        ffn_grad_side(cube, my_number(cube), 0, sizes, [x.get for x in given], *scratch, keep)

    ins = [(x, "fetch") for x in operands]
    outs = [((cube.half, br, bc), BF16, "sink", 2 * cube.half)]
    return staged_call(body, ins, outs, ffn_grad_scratch(cube, sizes, t), us=8)[0]


def attention_grad_side(cube, me, side, sizes, operands, lt, lhs, wide, blocks, out):
    a1, a0, dq1, dq0, dvec, dfb = operands
    tr, tc, vrows, vcols, bias = sizes
    br, bc = 3 * tr + EXTRA, 4 * tc
    g_n, pairs = cube.groups, cube.rows // 2
    t = lt.shape[1] // 2
    stacked_t((a1(), a0()), lt)
    side_rows(cube, me, side, lt, lhs, 4 * tr)
    dq1, dq0 = dq1(), dq0()
    for j in range(0, 3 * D, NB):
        cols = slice(j, j + NB)
        full = mm(lhs[:, 0:t], dq1[:, cols], NN) + mm(lhs[:, t : 2 * t], dq0[:, cols], NN)
        wide[:, cols] = full.astype(BF16)
    dvec, dfb = dvec(), dfb()

    def extra(g, r):
        vecs = dvec[r * vrows : (r + 1) * vrows, g * vcols : (g + 1) * vcols]
        at = (g * cube.rows + r) * bias
        rows = [
            jnp.concatenate([vecs, jnp.zeros((vrows, bc - vcols), F32)], 1),
            jnp.concatenate([dfb[0:1, at : at + bias], jnp.zeros((1, bc - bias), F32)], 1),
            jnp.zeros((EXTRA - vrows - 1, bc), F32),
        ]
        return jnp.concatenate(rows, 0)

    first = ((me & 1) ^ side) == 0
    for g in range(g_n):
        for pair in range(pairs):
            n = g * pairs + pair
            block = blocks.at[n]
            copy_tiles(wide, block, 3, tr, tc, src_at=(pair * 4 * tr, g * 3 * tc))
            ext = jnp.where(first, extra(g, 2 * pair), extra(g, 2 * pair + 1))
            block[3 * tr : br, :] = ext.astype(BF16)
            out.put(blocks.at[n], cube.scatter_slot(me, g * cube.rows + cube.row_of(me, side, pair)))


def attention_grad_scratch(cube, sizes, t):
    tr, tc = sizes[:2]
    return [
        pltpu.VMEM((D, 2 * t), BF16),
        pltpu.VMEM((D // 2, 2 * t), BF16),
        pltpu.VMEM((D // 2, 3 * D), BF16),
        pltpu.VMEM((cube.half, 3 * tr + EXTRA, 4 * tc), BF16),
    ]


def attention_backward_and_grad(
    cube, ends, dh_mid, dh0, h, qkv, lse, m0, wqkv, wout, vec, a1, a0, dq1, dvecs, dfbs, sizes
):
    tr, tc, vrows, vcols, bias = sizes
    br, bc = 3 * tr + EXTRA, 4 * tc
    g_n, r_n = cube.groups, cube.rows
    t = h.shape[0]
    if not fits(br, bc):
        dq0, d_in, dvec = attention_backward_call(ends, dh_mid, dh0, h, qkv, lse, m0, wqkv, wout, vec)
        dvec, dfb = dvec + dvecs[0] + dvecs[1], dfbs[0] + dfbs[1]
        dqkv = tiled(blocked(mm(a1, dq1, TN) + mm(a0, dq0, TN), g_n, r_n), 3)
        vecs = blocked(dvec, g_n, r_n)
        biases = dfb.reshape(g_n, r_n, 1, bias)
        ext = jnp.zeros((g_n, r_n, EXTRA, bc), F32)
        ext = ext.at[:, :, :vrows, :vcols].set(vecs).at[:, :, vrows : vrows + 1, :bias].set(biases)
        full = jnp.concatenate([dqkv, ext], 2).astype(BF16)
        keep, send = ordered_slots(cube, full.reshape(cube.n, br, bc))
        return d_in, send, keep

    def body(
        ends, dh_mid, dh0, h, qkv, lse, m0, wqkv, wout, vec, a1, a0, dq1, dvec1, dvec0, dfb1, dfb0,
        d_in, dq0, dvec, dfb, send, mask, dmix, da, *scratch,
    ):
        waits = {
            "dh_low": dh0, "wout": wout, "qkv": qkv, "mixed": m0, "lse": lse, "wqkv": wqkv, "h": h,
            "dh_mid": dh_mid,
        }
        for x in (*waits.values(), vec, a1, a0, dq1, dvec1, dvec0, dfb1, dfb0):
            x.start()
        fill_mask(ends, mask)
        attention_backward(
            dh_mid.ref, dh0.ref, h.ref, qkv.ref, lse.ref, m0.ref, mask, wqkv.ref, wout.ref, vec.get(),
            dmix, dq0.ref, da, d_in.ref, dvec.ref, use=lambda which: waits[which].get(),
            done=lambda which: dq0.flush(),
        )
        d_in.flush()
        dvec.ref[...] += dvec1.get()[...] + dvec0.get()[...]
        dfb.ref[...] = dfb1.get()[...] + dfb0.get()[...]
        dvec.flush()
        dfb.flush()
        operands = (a1.get, a0.get, dq1.get, lambda: dq0.ref, lambda: dvec.ref, lambda: dfb.ref)
        attention_grad_side(cube, my_number(cube), 1, sizes, operands, *scratch, send)

    ins = [(ends, "smem")] + [(x, "fetch") for x in (dh_mid, dh0, h, qkv, lse, m0, wqkv, wout)]
    ins += [(x, "fetch") for x in (vec, a1, a0, dq1, *dvecs, *dfbs)]
    outs = [
        ((t, D), F32, "flush"),
        ((t, 3 * D), BF16, "flush"),
        ((8, D), F32, "flush"),
        ((1, FF), F32, "flush"),
        ((cube.half, br, bc), BF16, "sink", cube.half),
    ]
    scratch = [pltpu.VMEM((t, t), F32), pltpu.VMEM((t, D), BF16), pltpu.VMEM((t, D), F32)]
    scratch += attention_grad_scratch(cube, sizes, t)
    got = staged_call(body, ins, outs, scratch, us=17, mib=48)
    return got[0], got[4], (a1, a0, dq1, got[1], got[2], got[3])


def attention_grad_keep(cube, operands, sizes):
    tr, tc = sizes[:2]
    br, bc = 3 * tr + EXTRA, 4 * tc
    if not fits(br, bc):
        return operands
    t = operands[0].shape[0]

    def body(*refs):
        given, keep, scratch = refs[:6], refs[6], refs[7:]
        for x in given:
            x.start()
        attention_grad_side(cube, my_number(cube), 0, sizes, [x.get for x in given], *scratch, keep)

    ins = [(x, "fetch") for x in operands]
    outs = [((cube.half, br, bc), BF16, "sink", cube.half)]
    return staged_call(body, ins, outs, attention_grad_scratch(cube, sizes, t), us=8, mib=32)[0]


def adam_update(weight, first, second, grad, keep_frac):
    t_step = float(STEP)
    first_new = 0.9 * first * keep_frac + 0.1 * grad
    second_new = 0.95 * second * keep_frac + 0.05 * grad * grad
    first_hat = first_new / (1.0 - 0.9**t_step)
    second_hat = second_new / (1.0 - 0.95**t_step)
    weight_new = weight.astype(F32) * (1.0 - LEARN_RATE * WEIGHT_DECAY) - LEARN_RATE * first_hat / (
        jnp.sqrt(second_hat) + 1e-08
    )
    return (weight_new.astype(BF16), first_new, second_new)


def body(
    hidden_in,
    cotangent,
    w_qkv,
    w_out,
    w_fc,
    w_proj,
    vectors,
    fc_bias,
    first_qkv,
    first_out,
    first_fc,
    first_proj,
    first_vectors,
    first_fc_bias,
    second_qkv,
    second_out,
    second_fc,
    second_proj,
    second_vectors,
    second_fc_bias,
    seg_ends,
    pass_counts,
    reset_flag,
):
    cube = Cube(lax.axis_size("grp"), lax.axis_size("row"))
    rows_w = w_qkv.shape[0]
    vrows, vcols = vectors.shape
    bias = fc_bias.shape[0]
    tr, tc = rows_w // 4, w_out.shape[1]
    sizes = (tr, tc, vrows, vcols, bias)

    far = cube.bits - 3
    near, last = far, far + 1
    join = lambda x, y: jnp.concatenate([x, y], 0)
    a, f = pack(w_qkv, w_out, w_fc, vectors, fc_bias, seg_ends, sizes)
    mixed = cube.mixed_plans
    a, p = lock((cube.gather_steps(a[None], 0, 1), cube.gather_steps(w_proj.T[None], 0, 1, mixed)))
    a = cube.gather_steps(a, 1, far)

    a, f = lock((a, f[None]))
    got, f = lock((cube.gather_swap(a, near), cube.gather_steps(f, 0, 1)))
    a = join(a, got)

    a, f, p = lock((a, f, p))
    part = p.shape[1] // 3
    last_a, f, got_p0 = lock(
        (
            cube.gather_swap(a, last),
            cube.gather_steps(f, 1, far),
            cube.gather_swap(p[:, :part], 1, mixed),
        )
    )

    f, p1 = lock((f, p[:, part:]))
    core_a0, core_a1, got, got_p1 = lock(
        (
            cube.swap_core(a),
            cube.swap_core(last_a),
            cube.gather_swap(f, near),
            cube.gather_swap(p1, 1, mixed),
        )
    )
    f = join(f, got)
    p = cube.gather_steps(join(p, jnp.concatenate([got_p0, got_p1], 1)), 2, far, mixed)

    h0, f, p = lock((hidden_in, f, p))
    full, acts = open_attention(cube, seg_ends, h0, (a, last_a, core_a0, core_a1), sizes)
    full, acts, last_f, core_f0, p = lock(
        (
            full,
            acts,
            cube.gather_swap(f, last),
            cube.swap_core(f),
            cube.gather_steps(p, far, last, mixed),
        )
    )
    wqkv, vec, fb, tot = full
    a0, qkv0, lse0, mixed0 = acts

    core_f1 = cube.swap_core(last_f)
    core_f1, p = lock((core_f1, p))
    opened = open_fc(cube, h0, mixed0, (f, last_f, core_f0, core_f1), vec, fb, sizes)
    opened, last_p, core_p0 = lock((opened, cube.gather_swap(p, last, mixed), cube.swap_core(p)))
    (wfc, wout), (mid0, c0, g0, gp0) = opened
    core_p1 = cube.swap_core(last_p)
    made, slots = second_pass(
        cube, seg_ends, pass_counts, mid0, g0, (p, last_p, core_p0, core_p1), cotangent, wqkv, wout, wfc, vec, fb
    )
    wpt, hidden, d1, a1, mixed1, c1, dqkv1, dhl1, dfl1, dvec1, dfb1 = made
    keep_p, send_p = slots
    total = tot[0, 0]
    end = cube.bits - 1

    p = cube.scatter_add(keep_p, cube.swap_core(send_p))

    d1, p = lock((d1, p))
    back, send_f, rest = ffn_backward_and_grad(
        cube, d1, mid0, gp0, wfc, wpt, vec, c1, c0, dfl1, mixed1, mixed0, dhl1, sizes
    )
    back, send_f, rest, got = lock((back, send_f, rest, cube.scatter_swap(p, 0)))
    dfb0, dhm0, dhl0, dvec0 = back
    p = cube.scatter_add(p[0], got)

    send_f, rest, p = lock((send_f, rest, p))
    keep_f = ffn_grad_keep(cube, rest, sizes)
    keep_f, got_f, got = lock((keep_f, cube.swap_core(send_f), cube.scatter_swap(p, 1)))
    f = cube.scatter_add(keep_f, got_f)
    p = cube.scatter_add(p[0], got)

    dhl0, f, p = lock((dhl0, f, p))
    input_grad, send_a, rest = attention_backward_and_grad(
        cube, seg_ends, dhm0, dhl0, h0, qkv0, lse0, mixed0, wqkv, wout, vec, a1, a0, dqkv1,
        (dvec1, dvec0), (dfb1, dfb0), sizes,
    )
    send_a, rest, got_f, p = lock((send_a, rest, cube.scatter_swap(f, 0), cube.scatter_steps(p, 2, 3)))
    f = cube.scatter_add(f[0], got_f)

    send_a, rest, f, p = lock((send_a, rest, f, p))
    keep_a = attention_grad_keep(cube, rest, sizes)
    got_f = cube.scatter_swap(f, 1)
    keep_a, got_a, sum_p = lock((keep_a, cube.swap_core(send_a), cube.scatter_steps(p, 3, end)))
    a = cube.scatter_add(keep_a, got_a)
    f = cube.scatter_add(f[0], got_f)

    a = cube.scatter_steps(a, 0, 1)
    got_a, sum_f = lock((cube.scatter_swap(a, 1), cube.scatter_steps(f, 2, end)))
    a = cube.scatter_add(a[0], got_a)
    sum_a = cube.scatter_steps(a, 2, end)

    sum_a, sum_f = sum_a.astype(F32), sum_f.astype(F32)
    summed = (
        untiled(sum_a[: 3 * tr], 3),
        untiled(sum_f[rows_w:], 1),
        sum_f[:rows_w],
        sum_p.T.astype(F32),
        sum_a[3 * tr : 3 * tr + vrows, :vcols],
        sum_a[3 * tr + vrows, :bias],
    )
    grads = tuple(s / total for s in summed)
    keep_feat = 1.0 - reset_flag.astype(F32)
    keep_rows = lax.dynamic_slice_in_dim(keep_feat, lax.axis_index("row") * rows_w, rows_w)[:, None]
    keep_cols = lax.dynamic_slice_in_dim(keep_feat, lax.axis_index("grp") * vcols, vcols)[None, :]
    bias_index = (my_number(cube) * bias + jnp.arange(bias, dtype=jnp.int32)) % D
    keeps = (keep_rows, keep_rows, keep_rows, keep_cols, keep_cols, keep_feat[bias_index])
    weights = (w_qkv, w_out, w_fc, w_proj, vectors, fc_bias)
    firsts = (first_qkv, first_out, first_fc, first_proj, first_vectors, first_fc_bias)
    seconds = (second_qkv, second_out, second_fc, second_proj, second_vectors, second_fc_bias)
    updated = [
        adam_update(w, m, v, g, kp) for w, m, v, g, kp in zip(weights, firsts, seconds, grads, keeps)
    ]
    return (
        (hidden, input_grad)
        + grads
        + tuple(u[0] for u in updated)
        + tuple(u[1] for u in updated)
        + tuple(u[2] for u in updated)
    )


def solution(mesh):
    tokens = P(("grp", "row"), None)
    flat = P(("grp", "row"))
    tiles = P("row", "grp")
    six = (tiles, tiles, tiles, tiles, tiles, flat)
    return jax.shard_map(
        body,
        mesh=mesh,
        in_specs=(tokens, tokens) + six * 3 + (tokens, P("grp"), P()),
        out_specs=(tokens, tokens) + six * 4,
        check_vma=False,
    )
```
